32 devices in a mesh: grid: 4 (over y, x), band: 8 (over z, core).
Axes of the slice: x: 2, y: 2, z: 4, core: 2. Of those that a mesh axis runs over, the one named last changes fastest.
Arguments:
- psi: float32 [2, 8, 2048, 96], P(None, 'band', 'grid'), may hold values from -6 to 6
- col_map: int32 [2048], P('grid'), may hold values from 0 to 9215, as said below
- potential: float32 [96, 9216], P('grid'), may hold values from -3 to 3
- lower: float32 [1], replicated, may hold values from 0.2 to 0.6
- upper: float32 [1], replicated, may hold values from 2.6 to 3.2
Outputs:
- filtered: float32 [2, 8, 2048, 96], P(None, 'band', 'grid')
- gram: float32 [2, 8, 8], P(None, 'band', 'grid')
The draws below stay inside these ranges and needn't reach their ends.
Inputs may be any that keep to these rules, and one draw needn't show every extreme that they name: `col_map`: the entries are distinct; every column with gx^2 + gy^2 <= 24^2 appears once, the remaining entries are other columns of the grid.
All inputs are finite; a program needn't handle non-finite values.
Results may differ from the reference program's by a relative error of at most 0.0003.
Values may be sent and summed in bfloat16 or wider, within the bound.
No kernel may reach another device: no remote copies, remote signals or barrier semaphores. Data moves between devices by JAX's collectives and lax.ppermute only.
A program may use at most 64 MiB of HBM per device.

```python
import jax
import jax.numpy as jnp
from jax import lax

NG = 96
GMAX = 24
COLS = 2048
BANDS = 8


def draw_col_map(key, part):
    key = jax.random.fold_in(key, 11)
    first_key, second_key = jax.random.split(key)
    total = NG * NG
    places = jnp.arange(total, dtype=jnp.int32)
    row_freq = jnp.where(places // NG < NG // 2, places // NG, places // NG - NG)
    col_freq = jnp.where(places % NG < NG // 2, places % NG, places % NG - NG)
    outside = (row_freq * row_freq + col_freq * col_freq > GMAX * GMAX).astype(jnp.int32)
    scores = jax.random.permutation(first_key, total).astype(jnp.int32) + total * outside
    chosen = places[jnp.argsort(scores, stable=True)][:COLS]
    return chosen[jax.random.permutation(second_key, COLS)].astype(jnp.int32)


def steps_of(rng, shape, cuts, least, largest):
    gain, own = 1.0, jax.random.fold_in(rng, 6)
    for position, blocks in cuts:
        heights = jnp.exp(jax.random.uniform(jax.random.fold_in(own, position), (blocks,), jnp.float32, least / len(cuts), largest / len(cuts)))
        gain = gain * jnp.repeat(heights, shape[position] // blocks).reshape([-1 if axis == position else 1 for axis in range(len(shape))])
    return gain


def normal_values(rng, shape, spread, limit, cuts=(), kind=jnp.bfloat16):
    result = spread * jax.random.normal(rng, shape, jnp.float32)
    if cuts:
        result = result * steps_of(rng, shape, cuts, -0.22, 0.18)
    return jnp.clip(result, -limit, limit).astype(kind)


def setup_inputs(seed: int = 0) -> dict:
    arg_keys = jax.random.split(jax.random.key(seed), 6)
    return {
        "psi": normal_values(arg_keys[0], (2, BANDS, COLS, NG), 1.0, 6.0, ((1, 8), (2, 4)), jnp.float32),
        "col_map": draw_col_map(jax.random.fold_in(arg_keys[5], 71), 0),
        "potential": normal_values(arg_keys[2], (NG, NG * NG), 0.5, 3.0, ((0, 4),), jnp.float32),
        "lower": jnp.clip(jax.random.uniform(arg_keys[3], (1,), jnp.float32, 0.2, 0.6), 0.2, 0.6),
        "upper": jnp.clip(jax.random.uniform(arg_keys[4], (1,), jnp.float32, 2.6, 3.2), 2.6, 3.2),
    }


def folded(index):
    return jnp.where(index < NG // 2, index, index - NG)


def reference(psi, col_map, potential, lower, upper):
    fx = folded(col_map // NG)
    fy = folded(col_map % NG)
    fz = folded(jnp.arange(NG, dtype=jnp.int32))
    radius2 = (fx * fx + fy * fy)[:, None] + (fz * fz)[None, :]
    inside = (radius2 <= GMAX * GMAX).astype(jnp.float32)
    kinetic = 2.0 * radius2.astype(jnp.float32) / (GMAX * GMAX)
    center = (upper[0] + lower[0]) / 2.0
    half = (upper[0] - lower[0]) / 2.0
    volume = potential.reshape(NG, NG, NG)

    def apply_h(coeff):
        values = lax.complex(coeff[0], coeff[1])
        dense = jnp.zeros((NG * NG, NG), values.dtype).at[col_map].set(values)
        dense = jnp.transpose(dense.reshape(NG, NG, NG), (2, 0, 1))
        field = jnp.fft.ifftn(dense) * volume
        back = jnp.transpose(jnp.fft.fftn(field), (1, 2, 0)).reshape(NG * NG, NG)[col_map]
        return jnp.stack([kinetic * coeff[0] + inside * jnp.real(back), kinetic * coeff[1] + inside * jnp.imag(back)])

    def filter_band(coeff):
        start = inside * coeff
        first = (apply_h(start) - center * start) / half
        return 2.0 * (apply_h(first) - center * first) / half - start

    filtered = jnp.transpose(lax.map(filter_band, jnp.transpose(psi, (1, 0, 2, 3))), (1, 0, 2, 3))
    rounded = filtered.astype(jnp.bfloat16).reshape(2, BANDS, COLS * NG)
    real_part = jnp.dot(rounded[0], rounded[0].T, preferred_element_type=jnp.float32) + jnp.dot(rounded[1], rounded[1].T, preferred_element_type=jnp.float32)
    imag_part = jnp.dot(rounded[0], rounded[1].T, preferred_element_type=jnp.float32) - jnp.dot(rounded[1], rounded[0].T, preferred_element_type=jnp.float32)
    gram = jnp.stack([real_part, imag_part]) / (4.0 * GMAX ** 3)
    return filtered, gram
```

```python
import functools

import jax
import jax.numpy as jnp
import ml_dtypes
import numpy as np
from jax import lax
from jax.experimental import pallas as pl
from jax.experimental.pallas import tpu as pltpu
from jax.sharding import PartitionSpec as P

GY = 64
GX = 56
F32 = jnp.float32
BF16 = jnp.bfloat16
VMEM_LIMIT = 60 * 1024 * 1024


def round_up(value, unit):
    return -(-value // unit) * unit


def halves(table):
    table = np.asarray(table, np.float32)
    high = table.astype(ml_dtypes.bfloat16)
    low = (table - high.astype(np.float32)).astype(ml_dtypes.bfloat16)
    return np.stack([high, low])


def folded(index, size):
    return np.where(index < size // 2, index, index - size)


def z_tables(size, devices, pad):
    depth = size // devices
    radius = size // 4
    freq = np.arange(size)
    keep = np.abs(folded(freq, size)) <= radius
    ahead = np.zeros((devices, 2, 2 * pad, size))
    back = np.zeros((devices, 2 * pad, 256))
    for d in range(devices):
        plane = d * depth + np.arange(depth)
        angle = 2 * np.pi * ((plane[:, None] * freq[None, :]) % size) / size
        c, s = np.cos(angle) * keep, np.sin(angle) * keep
        ahead[d, 0, :depth], ahead[d, 0, pad : pad + depth] = c, s
        ahead[d, 1, :depth], ahead[d, 1, pad : pad + depth] = -s, c
        back[d, :depth, :size], back[d, :depth, 128 : 128 + size] = c, -s
        back[d, pad : pad + depth, :size], back[d, pad : pad + depth, 128 : 128 + size] = s, c
    return halves(ahead), halves(back)


def plane_tables(size):
    radius = size // 4
    count = 2 * radius + 1
    freq = np.arange(count) - radius
    angle = 2 * np.pi * ((freq[:, None] * np.arange(size)[None, :]) % size) / size
    c, s = np.cos(angle), np.sin(angle)
    ty = np.zeros((2 * GY, 256))
    ty[:count, :size], ty[:count, 128 : 128 + size] = c, s
    ty[GY : GY + count, :size], ty[GY : GY + count, 128 : 128 + size] = -s, c
    tyb = np.zeros((256, 2 * GY))
    tyb[:size, :count], tyb[:size, GY : GY + count] = c.T, -s.T
    tyb[128 : 128 + size, :count], tyb[128 : 128 + size, GY : GY + count] = s.T, c.T
    tx = np.zeros((2 * size, 2 * GX))
    tx[:size, :count], tx[:size, GX : GX + count] = c.T, -s.T
    tx[size:, :count], tx[size:, GX : GX + count] = s.T, c.T
    txb = np.zeros((2 * GX, 2 * size))
    txb[:count, :size], txb[:count, size:] = c, s
    txb[GX : GX + count, :size], txb[GX : GX + count, size:] = -s, c
    return halves(ty), halves(tx), halves(txb), halves(tyb)


def split(value):
    high = value.astype(BF16)
    low = (value - high.astype(F32)).astype(BF16)
    return high, low


def dot(a, b, dims=((1,), (0,))):
    return lax.dot_general(a, b, (dims, ((), ())), preferred_element_type=F32)


def dot3(a, b, dims=((1,), (0,))):
    return dot(a[0], b[0], dims) + dot(a[0], b[1], dims) + dot(a[1], b[0], dims)


def call(kernel, out_shape, in_specs, scratch=()):
    return pl.pallas_call(
        kernel,
        out_shape=out_shape,
        in_specs=in_specs,
        scratch_shapes=list(scratch),
        compiler_params=pltpu.CompilerParams(vmem_limit_bytes=VMEM_LIMIT),
    )


SMEM = pl.BlockSpec(memory_space=pltpu.SMEM)
VMEM = pl.BlockSpec(memory_space=pltpu.VMEM)


def column_values(row, lanes):
    return jnp.transpose(jnp.broadcast_to(row, (lanes, row.shape[1])))


def sphere(radius_row, size):
    cols = radius_row.shape[1]
    radius = size // 4
    flat = column_values(radius_row, 128)[:, :size]
    lane = lax.broadcasted_iota(jnp.int32, (cols, size), 1)
    freq = jnp.where(lane < size // 2, lane, lane - size).astype(F32)
    radius2 = flat + freq * freq
    return radius2 <= float(radius * radius), radius2 * (2.0 / (radius * radius))


def to_planes(me, parts, table_ref, outs, step):
    count = len(outs)
    total = None
    for p in range(2):
        high, low = split(parts[p])
        ta = jnp.concatenate([table_ref[0, step(me, k), p] for k in range(count)], axis=0)
        tb = jnp.concatenate([table_ref[1, step(me, k), p] for k in range(count)], axis=0)
        piece = dot3((ta, tb), (high, low), ((1,), (1,)))
        total = piece if total is None else total + piece
    rows = outs[0].shape[0]
    for k in range(count):
        outs[k][...] = total[k * rows : (k + 1) * rows]


def from_planes(me, planes, table_ref, step, size):
    count = len(planes)
    stacked = jnp.concatenate([ref[...] for ref in planes], axis=0)
    high, low = split(jnp.transpose(stacked))
    ta = jnp.concatenate([table_ref[0, step(me, k)] for k in range(count)], axis=0)
    tb = jnp.concatenate([table_ref[1, step(me, k)] for k in range(count)], axis=0)
    total = dot3((high, low), (ta, tb))
    return total[:, :size], total[:, 128 : 128 + size]


def first_kernel(devices, step, size, me_ref, psi_ref, radius_ref, ahead_ref, *outs):
    inside, _ = sphere(radius_ref[...], size)
    parts = [jnp.where(inside, psi_ref[p], 0.0) for p in range(2)]
    to_planes(me_ref[0], parts, ahead_ref, outs, step)


def middle_kernel(devices, step, size, me_ref, low_ref, up_ref, *refs):
    planes, refs = refs[:devices], refs[devices:]
    psi_ref, radius_ref, ahead_ref, back_ref, first_ref = refs[:5]
    outs = refs[5:]
    center = (up_ref[0] + low_ref[0]) / 2.0
    half = (up_ref[0] - low_ref[0]) / 2.0
    inside, kinetic = sphere(radius_ref[...], size)
    back = from_planes(me_ref[0], planes, back_ref, step, size)
    parts = []
    for p in range(2):
        value = jnp.where(inside, ((kinetic - center) * psi_ref[p] + back[p]) / half, 0.0)
        first_ref[p] = value
        parts.append(value)
    to_planes(me_ref[0], parts, ahead_ref, outs, step)


def last_kernel(devices, step, size, me_ref, low_ref, up_ref, *refs):
    planes, refs = refs[:devices], refs[devices:]
    psi_ref, first_ref, radius_ref, back_ref, pick_ref, filtered_ref, packed_ref = refs
    center = (up_ref[0] + low_ref[0]) / 2.0
    half = (up_ref[0] - low_ref[0]) / 2.0
    inside, kinetic = sphere(radius_ref[...], size)
    back = from_planes(me_ref[0], planes, back_ref, step, size)
    packed = None
    for p in range(2):
        value = 2.0 * ((kinetic - center) * first_ref[p] + back[p]) / half - psi_ref[p]
        value = jnp.where(inside, value, 0.0)
        filtered_ref[p] = value
        piece = dot(value.astype(BF16), pick_ref[p])
        packed = piece if packed is None else packed + piece
    packed_ref[...] = packed.astype(BF16)


def slab_kernel(devices, size, depth, *refs):
    planes, refs = refs[:devices], refs[devices:]
    place_ref, pot_ref, ty_ref, tx_ref, txb_ref, tyb_ref = refs[:6]
    outs = refs[6 : 6 + devices]
    y0_ref, y1_ref, q_ref, box_ref, gxc_ref, oy_ref = refs[6 + devices :]
    pad = planes[0].shape[0] // 2
    cols = planes[0].shape[1]
    total = cols * devices
    radius = size // 4
    tiles = -(-(2 * radius + 1) // 4)
    gx_row, gy_row = place_ref[0:1, :], place_ref[1:2, :]
    lane = lax.broadcasted_iota(jnp.int32, (total, 128), 1)
    gxc_ref[...] = column_values(gx_row, 128).astype(BF16)
    oy_ref[...] = jnp.where(column_values(gy_row, 128) == (lane % GY).astype(F32), 1.0, 0.0).astype(BF16)
    side = (lax.broadcasted_iota(jnp.int32, (total, 128), 1) // GY).astype(BF16)
    near = lax.broadcasted_iota(jnp.int32, (pad, 128), 1) < GY

    stacked = jnp.concatenate([ref[...] for ref in planes], axis=1)
    lhs = jnp.concatenate(split(stacked), axis=0)
    ty = (ty_ref[0], ty_ref[1])
    zero = jnp.zeros((), BF16)
    for t in range(tiles):
        hot = []
        for u in range(2):
            hot.append(jnp.where(gxc_ref[...] - side == float(4 * t + 2 * u), oy_ref[...], zero))
        got = dot(lhs, jnp.concatenate(hot, axis=1))
        got = got[: 2 * pad] + got[2 * pad :]
        rows = []
        for u in range(2):
            re, im = got[:pad, 128 * u : 128 * u + 128], got[pad:, 128 * u : 128 * u + 128]
            rows.append(jnp.where(near, re, pltpu.roll(im, GY, 1)))
            rows.append(jnp.where(near, pltpu.roll(re, GY, 1), im))
        moved = dot3(split(jnp.concatenate(rows, axis=0)), ty)
        y0_ref[4 * t * pad : 4 * (t + 1) * pad] = moved[:, :128]
        y1_ref[4 * t * pad : 4 * (t + 1) * pad] = moved[:, 128:]
    if tiles * 4 < GX:
        rest = jnp.zeros(((GX - 4 * tiles) * pad, 128), F32)
        y0_ref[4 * tiles * pad :] = rest
        y1_ref[4 * tiles * pad :] = rest
    if depth < pad:
        q_ref[depth * GX :] = jnp.zeros(((pad - depth) * GX, 128), F32)

    tx = (tx_ref[0], tx_ref[1])
    txb = (txb_ref[0], txb_ref[1])
    tyb = (tyb_ref[0], tyb_ref[1])
    for z in range(0, depth, 2):
        sides = []
        for w in range(2):
            rows = pl.ds(z + w, GX, stride=pad)
            sides.append(jnp.concatenate([y0_ref[rows, :], y1_ref[rows, :]], axis=0))
        field = dot3(tx, split(jnp.concatenate(sides, axis=1)))
        pot = jnp.concatenate([pot_ref[z], pot_ref[z + 1]], axis=1)
        field = field * jnp.concatenate([pot, pot], axis=0)
        back = dot3(txb, split(field))
        rows = [
            jnp.concatenate([back[:GX, 128 * w : 128 * w + 128], back[GX:, 128 * w : 128 * w + 128]], axis=1)
            for w in range(2)
        ]
        q_ref[z * GX : (z + 2) * GX] = dot3(split(jnp.concatenate(rows, axis=0)), tyb)

    for t in range(tiles):
        for u in range(2):
            a = q_ref[pl.ds(4 * t + 2 * u, pad, stride=GX), :]
            b = q_ref[pl.ds(4 * t + 2 * u + 1, pad, stride=GX), :]
            re = jnp.where(near, a, pltpu.roll(b, GY, 1))
            im = jnp.where(near, pltpu.roll(a, GY, 1), b)
            at = 256 * t + 128 * u
            box_ref[:, at : at + 128] = jnp.concatenate(split(jnp.concatenate([re, im], axis=0)), axis=0)

    box = box_ref[...]
    wide = min(256, cols)
    down = lax.broadcasted_iota(jnp.int32, (GY, wide), 0).astype(F32)
    for k in range(devices):
        for at in range(0, cols, wide):
            here = k * cols + at
            gx = jnp.broadcast_to(gx_row[:, here : here + wide], (GY, wide)).astype(BF16)
            hot = jnp.where(jnp.broadcast_to(gy_row[:, here : here + wide], (GY, wide)) == down, 1.0, 0.0).astype(BF16)
            tall = jnp.concatenate([jnp.where(gx == float(v), hot, zero) for v in range(4 * tiles)], axis=0)
            got = dot(box, tall)
            outs[k][:, at : at + wide] = got[: 2 * pad] + got[2 * pad :]


def body(devices, bands, psi, col_map, potential, lower, upper):
    cols, size = psi.shape[2], psi.shape[3]
    radius = size // 4
    depth = size // devices
    pad = round_up(depth, 8)
    rows = 2 * pad
    me = lax.axis_index("grid")
    me_arg = me.astype(jnp.int32).reshape(1)
    if devices & (devices - 1) == 0:
        step = lambda at, k: at ^ k
        back_step = step
    else:
        raise ValueError("grid size")

    def exchange(values):
        return [values[0]] + [
            lax.ppermute(values[k], "grid", [(d, step(d, k)) for d in range(devices)]) for k in range(1, devices)
        ]

    ahead, back = z_tables(size, devices, pad)
    ty, tx, txb, tyb = plane_tables(size)
    count = 2 * radius + 1
    pick = np.zeros((2, size, 128), ml_dtypes.bfloat16)
    for j in range(count):
        pick[0, (j - radius) % size, j] = 1
        pick[1, (j - radius) % size, GY + j] = 1

    kx, ky = col_map // size, col_map % size
    gx = jnp.where(kx < size // 2, kx, kx - size)
    gy = jnp.where(ky < size // 2, ky, ky - size)
    radius2 = gx * gx + gy * gy
    used = radius2 <= radius * radius
    place = jnp.stack([jnp.where(used, gx + radius, -9), jnp.where(used, gy + radius, -9)]).astype(F32)
    radius_row = radius2.astype(F32).reshape(1, cols)
    places = jnp.concatenate(exchange([place] * devices), axis=1)
    pot = (potential * (1.0 / float(size**3))).reshape(depth, size, size)
    pot = jnp.pad(pot, ((0, 0), (0, 0), (0, 128 - size)))

    psi2 = psi.reshape(2, cols, size)
    plane_shape = [jax.ShapeDtypeStruct((rows, cols), F32)] * devices
    sent = call(
        functools.partial(first_kernel, devices, step, size),
        plane_shape,
        [SMEM, VMEM, VMEM, VMEM],
    )(me_arg, psi2, radius_row, ahead)

    def slab(values):
        return call(
            functools.partial(slab_kernel, devices, size, depth),
            plane_shape,
            [VMEM] * (devices + 6),
            [
                pltpu.VMEM((GX * pad, 128), F32),
                pltpu.VMEM((GX * pad, 128), F32),
                pltpu.VMEM((pad * GX, 128), F32),
                pltpu.VMEM((2 * rows, 256 * (-(-count // 4))), BF16),
                pltpu.VMEM((cols * devices, 128), BF16),
                pltpu.VMEM((cols * devices, 128), BF16),
            ],
        )(*values, places, pot, ty, tx, txb, tyb)

    planes = exchange(slab(exchange(sent)))
    first, *sent = call(
        functools.partial(middle_kernel, devices, step, size),
        [jax.ShapeDtypeStruct((2, cols, size), F32)] + plane_shape,
        [SMEM] * 3 + [VMEM] * (devices + 4),
    )(me_arg, lower, upper, *planes, psi2, radius_row, ahead, back)
    planes = exchange(slab(exchange(sent)))
    filtered, packed = call(
        functools.partial(last_kernel, devices, step, size),
        [jax.ShapeDtypeStruct((2, cols, size), F32), jax.ShapeDtypeStruct((cols, 128), BF16)],
        [SMEM] * 3 + [VMEM] * (devices + 5),
    )(me_arg, lower, upper, *planes, psi2, first, radius_row, back, pick)

    part = cols // bands
    spread = lax.all_to_all(packed.reshape(bands, part, 128), "band", split_axis=0, concat_axis=0, tiled=True)
    real, imag = spread[:, :, :GY], spread[:, :, GY:]
    dims = (((1, 2), (1, 2)), ((), ()))
    real_part = lax.dot_general(spread, spread, dims, preferred_element_type=F32)
    cross = lax.dot_general(real, imag, dims, preferred_element_type=F32)
    sums = lax.psum(jnp.stack([real_part, cross - cross.T]), ("grid", "band"))
    own = bands // devices
    gram = lax.dynamic_slice(sums, (0, lax.axis_index("band"), me * own), (2, 1, own)) / (4.0 * radius**3)
    return filtered.reshape(psi.shape), gram


def solution(mesh):
    return jax.shard_map(
        functools.partial(body, mesh.shape["grid"], mesh.shape["band"]),
        mesh=mesh,
        in_specs=(P(None, "band", "grid", None), P("grid"), P("grid", None), P(), P()),
        out_specs=(P(None, "band", "grid", None), P(None, "band", "grid")),
        check_vma=False,
    )
```

```python
import functools

import jax
import jax.numpy as jnp
import ml_dtypes
import numpy as np
from jax import lax
from jax.experimental import pallas as pl
from jax.experimental.pallas import tpu as pltpu
from jax.sharding import PartitionSpec as P

GY = 64
GX = 56
F32 = jnp.float32
BF16 = jnp.bfloat16
MIB = 1024 * 1024


def round_up(value, unit):
    return -(-value // unit) * unit


def halves(table):
    table = np.asarray(table, np.float32)
    high = table.astype(ml_dtypes.bfloat16)
    low = (table - high.astype(np.float32)).astype(ml_dtypes.bfloat16)
    return high, low


def stacked_table(table, axis):
    high, low = halves(table)
    return np.concatenate([high, high, low], axis=axis)


def folded(index, size):
    return np.where(index < size // 2, index, index - size)


def z_tables(size, devices, pad):
    depth = size // devices
    rows = 2 * pad
    freq = np.arange(size)
    ahead = np.zeros((devices, rows, 2 * size))
    back = np.zeros((2 * size, devices * rows))
    for d in range(devices):
        plane = d * depth + np.arange(depth)
        angle = 2 * np.pi * ((plane[:, None] * freq[None, :]) % size) / size
        c, s = np.cos(angle), np.sin(angle)
        ahead[d, :depth, :size], ahead[d, :depth, size:] = c, -s
        ahead[d, pad : pad + depth, :size], ahead[d, pad : pad + depth, size:] = s, c
        at = d * rows
        back[:size, at : at + depth], back[:size, at + pad : at + pad + depth] = c.T, s.T
        back[size:, at : at + depth], back[size:, at + pad : at + pad + depth] = -s.T, c.T
    return stacked_table(ahead, 2), stacked_table(back, 1)


def plane_tables(size):
    radius = size // 4
    count = 2 * radius + 1
    freq = np.arange(count) - radius
    angle = 2 * np.pi * ((freq[:, None] * np.arange(size)[None, :]) % size) / size
    c, s = np.cos(angle), np.sin(angle)
    ty = np.zeros((2 * GY, 256))
    ty[:count, :size], ty[:count, 128 : 128 + size] = c, s
    ty[GY : GY + count, :size], ty[GY : GY + count, 128 : 128 + size] = -s, c
    tyb = np.zeros((256, 2 * GY))
    tyb[:size, :count], tyb[:size, GY : GY + count] = c.T, -s.T
    tyb[128 : 128 + size, :count], tyb[128 : 128 + size, GY : GY + count] = s.T, c.T
    tx = np.zeros((2 * size, 2 * GX))
    tx[:size, :count], tx[:size, GX : GX + count] = c.T, -s.T
    tx[size:, :count], tx[size:, GX : GX + count] = s.T, c.T
    txb = np.zeros((2 * GX, 2 * size))
    txb[:count, :size], txb[:count, size:] = c, s
    txb[GX : GX + count, :size], txb[GX : GX + count, size:] = -s, c
    return stacked_table(ty, 0), stacked_table(tx, 1), stacked_table(txb, 1), stacked_table(tyb, 0)


def split(value):
    high = value.astype(BF16)
    low = (value - high.astype(F32)).astype(BF16)
    return high, low


def tripled(value, axis):
    high, low = split(value)
    return jnp.concatenate([high, low, high], axis=axis)


def dot(a, b, dims=((1,), (0,))):
    return lax.dot_general(a, b, (dims, ((), ())), preferred_element_type=F32)


SMEM = pl.BlockSpec(memory_space=pltpu.SMEM)
VMEM = pl.BlockSpec(memory_space=pltpu.VMEM)


def call(kernel, out_shape, scalars, arrays, scratch=(), limit=24):
    arrays = [pltpu.with_memory_space_constraint(value, pltpu.VMEM) if keep else value for value, keep in arrays]
    return pl.pallas_call(
        kernel,
        out_shape=out_shape,
        in_specs=[SMEM] * len(scalars) + [VMEM] * len(arrays),
        out_specs=[VMEM] * len(out_shape),
        scratch_shapes=list(scratch),
        compiler_params=pltpu.CompilerParams(vmem_limit_bytes=limit * MIB),
    )(*scalars, *arrays)


def position(col_row, size):
    place = col_row.astype(F32)
    kx = jnp.floor((place + 0.5) * (1.0 / size))
    ky = place - kx * size
    half = float(size // 2)
    return jnp.where(kx < half, kx, kx - size), jnp.where(ky < half, ky, ky - size)


def sphere(col_row, size):
    cols = col_row.shape[1]
    radius = size // 4
    gx, gy = position(col_row, size)
    index = lax.broadcasted_iota(jnp.int32, (size, cols), 0)
    freq = jnp.where(index < size // 2, index, index - size).astype(F32)
    radius2 = (gx * gx + gy * gy) + freq * freq
    return radius2 <= float(radius * radius), radius2 * (2.0 / (radius * radius))


def to_planes(me, parts, table_ref, outs, step):
    value = tripled(jnp.concatenate(parts, axis=0), 0)
    table = jnp.concatenate([table_ref[step(me, k)] for k in range(len(outs))], axis=0)
    total = dot(table, value)
    rows = table_ref.shape[1]
    for k in range(len(outs)):
        outs[k][:rows] = total[k * rows : (k + 1) * rows]


def from_planes(me, planes, table_ref, held, step, size):
    rows = planes[0].shape[0]
    third = rows * len(planes)
    for k in range(len(planes)):
        high, low = split(planes[k][...])
        at = step(me, k) * rows
        for j, value in enumerate((high, low, high)):
            held[pl.ds(pl.multiple_of(j * third + at, 16), rows), :] = value
    total = dot(table_ref[...], held[...])
    return total[:size], total[size:]


def first_kernel(devices, step, size, me_ref, psi_ref, col_ref, ahead_ref, *outs):
    inside, _ = sphere(col_ref[...], size)
    parts = [jnp.where(inside, psi_ref[p], 0.0) for p in range(2)]
    to_planes(me_ref[0], parts, ahead_ref, outs, step)
    radius = size // 4
    gx, gy = position(col_ref[...], size)
    used = gx * gx + gy * gy <= float(radius * radius)
    rows = ahead_ref.shape[1]
    row = lax.broadcasted_iota(jnp.int32, (8, gx.shape[1]), 0)
    place = jnp.where(used, jnp.where(row == 0, gx, gy) + float(radius), -9.0)
    for k in range(devices):
        outs[k][rows:] = place


def middle_kernel(devices, step, size, me_ref, low_ref, up_ref, *refs):
    planes, refs = refs[:devices], refs[devices:]
    psi_ref, col_ref, ahead_ref, back_ref, first_ref = refs[:5]
    outs, held = refs[5 : 5 + devices], refs[5 + devices]
    center = (up_ref[0] + low_ref[0]) / 2.0
    half = (up_ref[0] - low_ref[0]) / 2.0
    inside, kinetic = sphere(col_ref[...], size)
    back = from_planes(me_ref[0], planes, back_ref, held, step, size)
    parts = []
    for p in range(2):
        value = jnp.where(inside, ((kinetic - center) * psi_ref[p] + back[p]) / half, 0.0)
        first_ref[p] = value
        parts.append(value)
    to_planes(me_ref[0], parts, ahead_ref, outs, step)


def last_kernel(devices, bands, step, band_step, size, me_ref, band_ref, low_ref, up_ref, *refs):
    planes, refs = refs[:devices], refs[devices:]
    psi_ref, first_ref, col_ref, back_ref, pick_ref, filtered_ref = refs[:6]
    outs, (held, packed) = refs[6 : 6 + bands], refs[6 + bands :]
    center = (up_ref[0] + low_ref[0]) / 2.0
    half = (up_ref[0] - low_ref[0]) / 2.0
    inside, kinetic = sphere(col_ref[...], size)
    back = from_planes(me_ref[0], planes, back_ref, held, step, size)
    total = None
    for p in range(2):
        value = 2.0 * ((kinetic - center) * first_ref[p] + back[p]) / half - psi_ref[p]
        value = jnp.where(inside, value, 0.0)
        filtered_ref[p] = value
        piece = dot(pick_ref[p], value.astype(BF16))
        total = piece if total is None else total + piece
    packed[...] = total.astype(BF16)
    rows = packed.shape[0] // bands
    for k in range(bands):
        outs[k][...] = packed[pl.ds(pl.multiple_of(band_step(band_ref[0], k) * rows, 16), rows), :]


def gram_kernel(bands, band_step, band_ref, *refs):
    parts, sum_ref, held = refs[:bands], refs[bands], refs[bands + 1]
    rows, cols = parts[0].shape
    blocks = cols // 128
    for k in range(bands):
        at = pl.multiple_of(band_step(band_ref[0], k) * rows, 16)
        value = parts[k][...].astype(F32)
        for j in range(blocks):
            held[j, pl.ds(at, rows), :] = value[:, 128 * j : 128 * j + 128]
    lines = [[held[j, pl.ds(r, bands, stride=rows), :] for j in range(blocks)] for r in range(rows)]
    real = jnp.concatenate([v for r in range(rows // 2) for v in lines[r]], axis=1)
    imag = jnp.concatenate([v for r in range(rows // 2, rows) for v in lines[r]], axis=1)
    left = jnp.concatenate([real, imag], axis=1).astype(BF16)
    right = jnp.concatenate([imag, -real], axis=1).astype(BF16)
    sum_ref[0] = dot(left, left, ((1,), (1,)))
    sum_ref[1] = dot(left, right, ((1,), (1,)))


def slab_kernel(devices, size, depth, again, *refs):
    planes, refs = refs[:devices], refs[devices:]
    marks = planes
    if again:
        marks, refs = refs[:devices], refs[devices:]
    pot_ref, ty_ref, tx_ref, txb_ref, tyb_ref = refs[:5]
    outs = refs[5 : 5 + devices]
    y0_ref, y1_ref, q_ref, box_ref = refs[5 + devices :]
    pad = round_up(depth, 8)
    rows = 2 * pad
    cols = planes[0].shape[1]
    radius = size // 4
    tiles = -(-(2 * radius + 1) // 4)
    zero = jnp.zeros((), BF16)
    near = lax.broadcasted_iota(jnp.int32, (pad, 128), 1) < GY

    def one_hot(k, at, wide):
        gx = jnp.broadcast_to(marks[k][rows : rows + 1, at : at + wide], (16, wide)).astype(BF16)
        gy = jnp.broadcast_to(marks[k][rows + 1 : rows + 2, at : at + wide], (GY, wide))
        down = lax.broadcasted_iota(jnp.int32, (GY, wide), 0).astype(F32)
        hot = jnp.where(gy == down, 1.0, 0.0).astype(BF16)
        return gx, [hot[16 * i : 16 * i + 16] for i in range(GY // 16)]

    def expand(pieces, first, count):
        gx, hot = pieces
        tall = []
        for v in range(first, first + count):
            here = gx == float(v)
            tall += [jnp.where(here, piece, zero) for piece in hot]
        return jnp.concatenate(tall, axis=0)

    lhs = jnp.concatenate(split(jnp.concatenate([ref[:rows] for ref in planes], axis=1)), axis=0)
    sources = [one_hot(k, 0, cols) for k in range(devices)]
    whole = (
        jnp.concatenate([s[0] for s in sources], axis=1),
        [jnp.concatenate([s[1][i] for s in sources], axis=1) for i in range(GY // 16)],
    )
    for t in range(tiles):
        got = dot(lhs, expand(whole, 4 * t, 4), ((1,), (1,)))
        got = got[:rows] + got[rows:]
        mixed = []
        for u in range(2):
            re, im = got[:pad, 128 * u : 128 * u + 128], got[pad:, 128 * u : 128 * u + 128]
            mixed.append(jnp.where(near, re, pltpu.roll(im, GY, 1)))
            mixed.append(jnp.where(near, pltpu.roll(re, GY, 1), im))
        moved = dot(tripled(jnp.concatenate(mixed, axis=0), 1), ty_ref[...])
        y0_ref[4 * t * pad : 4 * (t + 1) * pad] = moved[:, :128]
        y1_ref[4 * t * pad : 4 * (t + 1) * pad] = moved[:, 128:]
    if tiles * 4 < GX:
        rest = jnp.zeros(((GX - 4 * tiles) * pad, 128), F32)
        y0_ref[4 * tiles * pad :] = rest
        y1_ref[4 * tiles * pad :] = rest
    if depth < pad:
        q_ref[depth * GX :] = jnp.zeros(((pad - depth) * GX, 128), F32)

    for z in range(0, depth, 2):
        sides = []
        for w in range(2):
            line = pl.ds(z + w, GX, stride=pad)
            sides.append(jnp.concatenate([y0_ref[line, :], y1_ref[line, :]], axis=0))
        field = dot(tx_ref[...], tripled(jnp.concatenate(sides, axis=1), 0))
        pot = jnp.concatenate([pot_ref[z], pot_ref[z + 1]], axis=1)
        field = field * jnp.concatenate([pot, pot], axis=0)
        back = dot(txb_ref[...], tripled(field, 0))
        turned = [
            jnp.concatenate([back[:GX, 128 * w : 128 * w + 128], back[GX:, 128 * w : 128 * w + 128]], axis=1)
            for w in range(2)
        ]
        q_ref[z * GX : (z + 2) * GX] = dot(tripled(jnp.concatenate(turned, axis=0), 1), tyb_ref[...])

    for t in range(2 * tiles):
        a = q_ref[pl.ds(2 * t, pad, stride=GX), :]
        b = q_ref[pl.ds(2 * t + 1, pad, stride=GX), :]
        re = jnp.where(near, a, pltpu.roll(b, GY, 1))
        im = jnp.where(near, pltpu.roll(a, GY, 1), b)
        box_ref[:, 128 * t : 128 * t + 128] = jnp.concatenate(split(jnp.concatenate([re, im], axis=0)), axis=0)

    box = box_ref[...]
    wide = min(256, cols)
    for k in range(devices):
        for at in range(0, cols, wide):
            got = dot(box, expand(one_hot(k, at, wide), 0, 4 * tiles))
            outs[k][:, at : at + wide] = got[:rows] + got[rows:]


def body(devices, bands, psi, col_map, potential, lower, upper):
    cols, size = psi.shape[2], psi.shape[3]
    radius = size // 4
    depth = size // devices
    pad = round_up(depth, 8)
    rows = 2 * pad
    me, band = lax.axis_index("grid"), lax.axis_index("band")
    me_arg = me.astype(jnp.int32).reshape(1)
    band_arg = band.astype(jnp.int32).reshape(1)
    if devices & (devices - 1) or bands & (bands - 1):
        raise ValueError("mesh size")

    def step(at, k):
        return at ^ k

    def exchange(values, axis="grid"):
        size = len(values)
        return [values[0]] + [
            lax.ppermute(values[k], axis, [(d, step(d, k)) for d in range(size)]) for k in range(1, size)
        ]

    def total(value, axis, size):
        bit = 1
        while bit < size:
            value = value + lax.ppermute(value, axis, [(d, d ^ bit) for d in range(size)])
            bit *= 2
        return value

    ahead, back = z_tables(size, devices, pad)
    tables = plane_tables(size)
    count = 2 * radius + 1
    slots = round_up(-(-count // bands), 8)
    pick = np.zeros((2, bands * 2 * slots, size), ml_dtypes.bfloat16)
    for j in range(count):
        at = (j % bands) * 2 * slots + j // bands
        pick[0, at, (j - radius) % size] = 1
        pick[1, at + slots, (j - radius) % size] = 1

    pot = (potential * (1.0 / float(size**3))).reshape(depth, size, size)
    pot = jnp.pad(pot, ((0, 0), (0, 0), (0, 128 - size)))
    psi_t = jnp.transpose(psi.reshape(2, cols, size), (0, 2, 1))
    col_row = col_map.reshape(1, cols)

    def vmem(shape, dtype=F32):
        return pltpu.VMEM(shape, dtype)

    marks = exchange(
        call(
            functools.partial(first_kernel, devices, step, size),
            [vmem((rows + 8, cols))] * devices,
            [me_arg],
            [(psi_t, False), (col_row, False), (ahead, False)],
        )
    )

    def slab(values, again):
        given = values + (marks if again else [])
        return call(
            functools.partial(slab_kernel, devices, size, depth, again),
            [vmem((rows, cols))] * devices,
            [],
            [(value, True) for value in given] + [(pot, False)] + [(table, False) for table in tables],
            [
                pltpu.VMEM((GX * pad, 128), F32),
                pltpu.VMEM((GX * pad, 128), F32),
                pltpu.VMEM((pad * GX, 128), F32),
                pltpu.VMEM((2 * rows, 256 * (-(-count // 4))), BF16),
            ],
        )

    held = pltpu.VMEM((3 * devices * rows, cols), BF16)
    planes = exchange(slab(marks, False))
    first, *sent = call(
        functools.partial(middle_kernel, devices, step, size),
        [vmem((2, size, cols))] + [vmem((rows, cols))] * devices,
        [me_arg, lower, upper],
        [(value, True) for value in planes] + [(psi_t, False), (col_row, False), (ahead, False), (back, False)],
        [held],
    )
    planes = exchange(slab(exchange(sent), True))
    filtered, *packed = call(
        functools.partial(last_kernel, devices, bands, step, step, size),
        [jax.ShapeDtypeStruct((2, size, cols), F32)] + [vmem((2 * slots, cols), BF16)] * bands,
        [me_arg, band_arg, lower, upper],
        [(value, True) for value in planes]
        + [(psi_t, False), (first, True), (col_row, False), (back, False), (pick, False)],
        [held, pltpu.VMEM((bands * 2 * slots, cols), BF16)],
    )
    (partial_sum,) = call(
        functools.partial(gram_kernel, bands, step),
        [vmem((2, bands, bands))],
        [band_arg],
        [(value, True) for value in exchange(packed, "band")],
        [pltpu.VMEM((cols // 128, bands * 2 * slots, 128), F32)],
    )
    sums = total(total(partial_sum, "grid", devices), "band", bands)
    own = bands // devices
    gram = lax.dynamic_slice(sums, (0, band, me * own), (2, 1, own)) / (4.0 * radius**3)
    return jnp.transpose(filtered, (0, 2, 1)).reshape(psi.shape), gram


def solution(mesh):
    return jax.shard_map(
        functools.partial(body, mesh.shape["grid"], mesh.shape["band"]),
        mesh=mesh,
        in_specs=(P(None, "band", "grid", None), P("grid"), P("grid", None), P(), P()),
        out_specs=(P(None, "band", "grid", None), P(None, "band", "grid")),
        check_vma=False,
    )
```

```python
import functools

import jax
import jax.numpy as jnp
import ml_dtypes
import numpy as np
from jax import lax
from jax.experimental import pallas as pl
from jax.experimental.pallas import tpu as pltpu
from jax.sharding import PartitionSpec as P

GY = 64
GX = 56
F32 = jnp.float32
BF16 = jnp.bfloat16
MIB = 1024 * 1024


def round_up(value, unit):
    return -(-value // unit) * unit


def halves(table):
    table = np.asarray(table, np.float32)
    high = table.astype(ml_dtypes.bfloat16)
    low = (table - high.astype(np.float32)).astype(ml_dtypes.bfloat16)
    return high, low


def stacked_table(table, axis):
    high, low = halves(table)
    return np.concatenate([high, high, low], axis=axis)


def folded(index, size):
    return np.where(index < size // 2, index, index - size)


def z_tables(size, devices, pad):
    depth = size // devices
    rows = 2 * pad
    freq = np.arange(size)
    ahead = np.zeros((devices, rows, 2 * size))
    back = np.zeros((2 * size, devices * rows))
    for d in range(devices):
        plane = d * depth + np.arange(depth)
        angle = 2 * np.pi * ((plane[:, None] * freq[None, :]) % size) / size
        c, s = np.cos(angle), np.sin(angle)
        ahead[d, :depth, :size], ahead[d, :depth, size:] = c, -s
        ahead[d, pad : pad + depth, :size], ahead[d, pad : pad + depth, size:] = s, c
        at = d * rows
        back[:size, at : at + depth], back[:size, at + pad : at + pad + depth] = c.T, s.T
        back[size:, at : at + depth], back[size:, at + pad : at + pad + depth] = -s.T, c.T
    return stacked_table(ahead, 2), stacked_table(back, 1)


def plane_tables(size):
    radius = size // 4
    count = 2 * radius + 1
    freq = np.arange(count) - radius
    angle = 2 * np.pi * ((freq[:, None] * np.arange(size)[None, :]) % size) / size
    c, s = np.cos(angle), np.sin(angle)
    ty = np.zeros((2 * GY, 256))
    ty[:count, :size], ty[:count, 128 : 128 + size] = c, s
    ty[GY : GY + count, :size], ty[GY : GY + count, 128 : 128 + size] = -s, c
    tyb = np.zeros((256, 2 * GY))
    tyb[:size, :count], tyb[:size, GY : GY + count] = c.T, -s.T
    tyb[128 : 128 + size, :count], tyb[128 : 128 + size, GY : GY + count] = s.T, c.T
    tx = np.zeros((2 * size, 2 * GX))
    tx[:size, :count], tx[:size, GX : GX + count] = c.T, -s.T
    tx[size:, :count], tx[size:, GX : GX + count] = s.T, c.T
    txb = np.zeros((2 * GX, 2 * size))
    txb[:count, :size], txb[:count, size:] = c, s
    txb[GX : GX + count, :size], txb[GX : GX + count, size:] = -s, c
    return stacked_table(ty, 0), stacked_table(tx, 1), stacked_table(txb, 1), stacked_table(tyb, 0)


def packing(size):
    radius = size // 4
    widths = [int(np.sqrt(radius * radius - g * g)) for g in range(-radius, radius + 1)]
    slots, free = [None] * len(widths), []
    for i in sorted(range(len(widths)), key=lambda j: (-widths[j], j)):
        span = 2 * widths[i] + 1
        for s in range(len(free) + 1):
            if s == len(free):
                free.append(128)
            if free[s] >= span:
                slots[i] = (widths[i], s, 128 - free[s] + widths[i])
                free[s] -= span
                break
    return slots, round_up(len(free), 2)


def split(value):
    high = value.astype(BF16)
    low = (value - high.astype(F32)).astype(BF16)
    return high, low


def tripled(value, axis):
    high, low = split(value)
    return jnp.concatenate([high, low, high], axis=axis)


def dot(a, b, dims=((1,), (0,))):
    return lax.dot_general(a, b, (dims, ((), ())), preferred_element_type=F32)


SMEM = pl.BlockSpec(memory_space=pltpu.SMEM)
VMEM = pl.BlockSpec(memory_space=pltpu.VMEM)


def call(kernel, out_shape, scalars, arrays, scratch=(), limit=24):
    arrays = [pltpu.with_memory_space_constraint(value, pltpu.VMEM) if keep else value for value, keep in arrays]
    return pl.pallas_call(
        kernel,
        out_shape=out_shape,
        in_specs=[SMEM] * len(scalars) + [VMEM] * len(arrays),
        out_specs=[VMEM] * len(out_shape),
        scratch_shapes=list(scratch),
        compiler_params=pltpu.CompilerParams(vmem_limit_bytes=limit * MIB),
    )(*scalars, *arrays)


def position(col_row, size):
    place = col_row.astype(F32)
    kx = jnp.floor((place + 0.5) * (1.0 / size))
    ky = place - kx * size
    half = float(size // 2)
    return jnp.where(kx < half, kx, kx - size), jnp.where(ky < half, ky, ky - size)


def sphere(col_row, size):
    cols = col_row.shape[1]
    radius = size // 4
    gx, gy = position(col_row, size)
    index = lax.broadcasted_iota(jnp.int32, (size, cols), 0)
    freq = jnp.where(index < size // 2, index, index - size).astype(F32)
    radius2 = (gx * gx + gy * gy) + freq * freq
    return radius2 <= float(radius * radius), radius2 * (2.0 / (radius * radius))


def to_planes(me, parts, table_ref, outs, step):
    value = tripled(jnp.concatenate(parts, axis=0), 0)
    table = jnp.concatenate([table_ref[step(me, k)] for k in range(len(outs))], axis=0)
    total = dot(table, value)
    rows = table_ref.shape[1]
    for k in range(len(outs)):
        outs[k][:rows] = total[k * rows : (k + 1) * rows]


def from_planes(me, planes, table_ref, held, step, size):
    rows = planes[0].shape[0]
    third = rows * len(planes)
    for k in range(len(planes)):
        high, low = split(planes[k][...])
        at = step(me, k) * rows
        for j, value in enumerate((high, low, high)):
            held[pl.ds(pl.multiple_of(j * third + at, 16), rows), :] = value
    total = dot(table_ref[...], held[...])
    return total[:size], total[size:]


def first_kernel(devices, step, size, me_ref, psi_ref, col_ref, ahead_ref, *outs):
    inside, _ = sphere(col_ref[...], size)
    parts = [jnp.where(inside, psi_ref[p], 0.0) for p in range(2)]
    to_planes(me_ref[0], parts, ahead_ref, outs, step)
    radius = size // 4
    gx, gy = position(col_ref[...], size)
    used = gx * gx + gy * gy <= float(radius * radius)
    rows = ahead_ref.shape[1]
    row = lax.broadcasted_iota(jnp.int32, (8, gx.shape[1]), 0)
    slot, lane = jnp.zeros(row.shape, F32), jnp.zeros(row.shape, F32)
    for i, (_, s, middle) in enumerate(packing(size)[0]):
        here = gx == float(i - radius)
        slot, lane = jnp.where(here, float(s), slot), jnp.where(here, float(middle), lane)
    place = jnp.where(used, jnp.where(row == 0, slot, lane + gy), -9.0)
    for k in range(devices):
        outs[k][rows:] = place


def middle_kernel(devices, step, size, me_ref, low_ref, up_ref, *refs):
    planes, refs = refs[:devices], refs[devices:]
    psi_ref, col_ref, ahead_ref, back_ref, first_ref = refs[:5]
    outs, held = refs[5 : 5 + devices], refs[5 + devices]
    center = (up_ref[0] + low_ref[0]) / 2.0
    half = (up_ref[0] - low_ref[0]) / 2.0
    inside, kinetic = sphere(col_ref[...], size)
    back = from_planes(me_ref[0], planes, back_ref, held, step, size)
    parts = []
    for p in range(2):
        value = jnp.where(inside, ((kinetic - center) * psi_ref[p] + back[p]) / half, 0.0)
        first_ref[p] = value
        parts.append(value)
    to_planes(me_ref[0], parts, ahead_ref, outs, step)


def last_kernel(devices, bands, step, band_step, size, me_ref, band_ref, low_ref, up_ref, *refs):
    planes, refs = refs[:devices], refs[devices:]
    psi_ref, first_ref, col_ref, back_ref, pick_ref, filtered_ref = refs[:6]
    outs, (held, packed) = refs[6 : 6 + bands], refs[6 + bands :]
    center = (up_ref[0] + low_ref[0]) / 2.0
    half = (up_ref[0] - low_ref[0]) / 2.0
    inside, kinetic = sphere(col_ref[...], size)
    back = from_planes(me_ref[0], planes, back_ref, held, step, size)
    total = None
    for p in range(2):
        value = 2.0 * ((kinetic - center) * first_ref[p] + back[p]) / half - psi_ref[p]
        value = jnp.where(inside, value, 0.0)
        filtered_ref[p] = value
        piece = dot(pick_ref[p], value.astype(BF16))
        total = piece if total is None else total + piece
    packed[...] = total.astype(BF16)
    rows = packed.shape[0] // bands
    for k in range(bands):
        outs[k][...] = packed[pl.ds(pl.multiple_of(band_step(band_ref[0], k) * rows, 16), rows), :]


def gram_kernel(bands, band_step, band_ref, *refs):
    parts, sum_ref, held = refs[:bands], refs[bands], refs[bands + 1]
    rows, cols = parts[0].shape
    blocks = cols // 128
    for k in range(bands):
        at = pl.multiple_of(band_step(band_ref[0], k) * rows, 16)
        value = parts[k][...].astype(F32)
        for j in range(blocks):
            held[j, pl.ds(at, rows), :] = value[:, 128 * j : 128 * j + 128]
    lines = [[held[j, pl.ds(r, bands, stride=rows), :] for j in range(blocks)] for r in range(rows)]
    real = jnp.concatenate([v for r in range(rows // 2) for v in lines[r]], axis=1)
    imag = jnp.concatenate([v for r in range(rows // 2, rows) for v in lines[r]], axis=1)
    left = jnp.concatenate([real, imag], axis=1).astype(BF16)
    right = jnp.concatenate([imag, -real], axis=1).astype(BF16)
    sum_ref[0] = dot(left, left, ((1,), (1,)))
    sum_ref[1] = dot(left, right, ((1,), (1,)))


def slab_kernel(devices, size, depth, again, *refs):
    planes, refs = refs[:devices], refs[devices:]
    marks = planes
    if again:
        marks, refs = refs[:devices], refs[devices:]
    pot_ref, ty_ref, tx_ref, txb_ref, tyb_ref = refs[:5]
    outs = refs[5 : 5 + devices]
    in_ref, y0_ref, y1_ref, back_ref, q_ref, box_ref = refs[5 + devices :]
    pad = round_up(depth, 8)
    rows = 2 * pad
    cols = planes[0].shape[1]
    radius = size // 4
    places, slots = packing(size)
    zero = jnp.zeros((), BF16)
    lane = lax.broadcasted_iota(jnp.int32, (pad, 128), 1)

    def between(first, last):
        return (lane >= first) & (lane <= last)

    def one_hot(k, at, wide):
        slot = jnp.broadcast_to(marks[k][rows : rows + 1, at : at + wide], (16, wide)).astype(BF16)
        spot = jnp.broadcast_to(marks[k][rows + 1 : rows + 2, at : at + wide], (128, wide))
        down = lax.broadcasted_iota(jnp.int32, (128, wide), 0).astype(F32)
        hot = jnp.where(spot == down, 1.0, 0.0).astype(BF16)
        return slot, [hot[16 * i : 16 * i + 16] for i in range(8)]

    def expand(pieces, first, count):
        slot, hot = pieces
        tall = []
        for v in range(first, first + count):
            here = slot == float(v)
            tall += [jnp.where(here, piece, zero) for piece in hot]
        return jnp.concatenate(tall, axis=0)

    lhs = jnp.concatenate(split(jnp.concatenate([ref[:rows] for ref in planes], axis=1)), axis=0)
    sources = [one_hot(k, 0, cols) for k in range(devices)]
    whole = (
        jnp.concatenate([s[0] for s in sources], axis=1),
        [jnp.concatenate([s[1][i] for s in sources], axis=1) for i in range(8)],
    )
    for t in range(0, slots, 2):
        got = dot(lhs, expand(whole, t, 2), ((1,), (1,)))
        got = got[:rows] + got[rows:]
        for i, (width, slot, middle) in enumerate(places):
            if slot // 2 * 2 != t:
                continue
            at = 128 * (slot - t)
            re = pltpu.roll(got[:pad, at : at + 128], (radius - middle) % 128, 1)
            im = pltpu.roll(got[pad:, at : at + 128], (radius + GY - middle) % 128, 1)
            im = jnp.where(between(GY + radius - width, GY + radius + width), im, 0.0)
            in_ref[i * pad : (i + 1) * pad] = jnp.where(between(radius - width, radius + width), re, im)
    in_ref[len(places) * pad :] = jnp.zeros(((GX - len(places)) * pad, 128), F32)
    moved = dot(tripled(in_ref[...], 1), ty_ref[...])
    y0_ref[...] = moved[:, :128]
    y1_ref[...] = moved[:, 128:]
    if depth < pad:
        q_ref[depth * GX :] = jnp.zeros(((pad - depth) * GX, 128), F32)

    chunk = 8
    for first in range(0, depth, chunk):
        last = min(depth, first + chunk)
        for z in range(first, last, 2):
            sides = []
            for w in range(2):
                line = pl.ds(z + w, GX, stride=pad)
                sides.append(jnp.concatenate([y0_ref[line, :], y1_ref[line, :]], axis=0))
            field = dot(tx_ref[...], tripled(jnp.concatenate(sides, axis=1), 0))
            pot = jnp.concatenate([pot_ref[z], pot_ref[z + 1]], axis=1)
            field = field * jnp.concatenate([pot, pot], axis=0)
            back = dot(txb_ref[...], tripled(field, 0))
            for w in range(2):
                for p in range(2):
                    back_ref[(z + w) * GX : (z + w + 1) * GX, 128 * p : 128 * p + 128] = back[
                        p * GX : (p + 1) * GX, 128 * w : 128 * w + 128
                    ]
        part = slice(first * GX, last * GX)
        q_ref[part] = dot(tripled(back_ref[part], 1), tyb_ref[...])

    for s in range(slots):
        re, im = jnp.zeros((pad, 128), F32), jnp.zeros((pad, 128), F32)
        for i, (width, slot, middle) in enumerate(places):
            if slot != s:
                continue
            value = q_ref[pl.ds(i, pad, stride=GX), :]
            here = between(middle - width, middle + width)
            re = jnp.where(here, pltpu.roll(value, (middle - radius) % 128, 1), re)
            im = jnp.where(here, pltpu.roll(value, (middle - radius - GY) % 128, 1), im)
        box_ref[:, 128 * s : 128 * s + 128] = jnp.concatenate(split(jnp.concatenate([re, im], axis=0)), axis=0)

    box = box_ref[...]
    wide = min(256, cols)
    for k in range(devices):
        for at in range(0, cols, wide):
            got = dot(box, expand(one_hot(k, at, wide), 0, slots))
            outs[k][:, at : at + wide] = got[:rows] + got[rows:]


def body(devices, bands, psi, col_map, potential, lower, upper):
    cols, size = psi.shape[2], psi.shape[3]
    radius = size // 4
    depth = size // devices
    pad = round_up(depth, 8)
    rows = 2 * pad
    me, band = lax.axis_index("grid"), lax.axis_index("band")
    me_arg = me.astype(jnp.int32).reshape(1)
    band_arg = band.astype(jnp.int32).reshape(1)
    if devices & (devices - 1) or bands & (bands - 1):
        raise ValueError("mesh size")

    def step(at, k):
        return at ^ k

    def exchange(values, axis="grid"):
        size = len(values)
        return [values[0]] + [
            lax.ppermute(values[k], axis, [(d, step(d, k)) for d in range(size)]) for k in range(1, size)
        ]

    def total(value, axis, size):
        return functools.reduce(jnp.add, exchange([value] * size, axis))

    ahead, back = z_tables(size, devices, pad)
    tables = plane_tables(size)
    count = 2 * radius + 1
    slots = round_up(-(-count // bands), 8)
    pick = np.zeros((2, bands * 2 * slots, size), ml_dtypes.bfloat16)
    for j in range(count):
        at = (j % bands) * 2 * slots + j // bands
        pick[0, at, (j - radius) % size] = 1
        pick[1, at + slots, (j - radius) % size] = 1

    pot = (potential * (1.0 / float(size**3))).reshape(depth, size, size)
    pot = jnp.pad(pot, ((0, 0), (0, 0), (0, 128 - size)))
    psi_t = jnp.transpose(psi.reshape(2, cols, size), (0, 2, 1))
    col_row = col_map.reshape(1, cols)

    def vmem(shape, dtype=F32):
        return pltpu.VMEM(shape, dtype)

    marks = exchange(
        call(
            functools.partial(first_kernel, devices, step, size),
            [vmem((rows + 8, cols))] * devices,
            [me_arg],
            [(psi_t, False), (col_row, False), (ahead, False)],
        )
    )

    def slab(values, again):
        given = values + (marks if again else [])
        return call(
            functools.partial(slab_kernel, devices, size, depth, again),
            [vmem((rows, cols))] * devices,
            [],
            [(value, True) for value in given] + [(pot, False)] + [(table, False) for table in tables],
            [
                pltpu.VMEM((GX * pad, 128), F32),
                pltpu.VMEM((GX * pad, 128), F32),
                pltpu.VMEM((GX * pad, 128), F32),
                pltpu.VMEM((pad * GX, 256), F32),
                pltpu.VMEM((pad * GX, 128), F32),
                pltpu.VMEM((2 * rows, 128 * packing(size)[1]), BF16),
            ],
        )

    held = pltpu.VMEM((3 * devices * rows, cols), BF16)
    planes = exchange(slab(marks, False))
    first, *sent = call(
        functools.partial(middle_kernel, devices, step, size),
        [vmem((2, size, cols))] + [vmem((rows, cols))] * devices,
        [me_arg, lower, upper],
        [(value, True) for value in planes] + [(psi_t, False), (col_row, False), (ahead, False), (back, False)],
        [held],
    )
    planes = exchange(slab(exchange(sent), True))
    filtered, *packed = call(
        functools.partial(last_kernel, devices, bands, step, step, size),
        [jax.ShapeDtypeStruct((2, size, cols), F32)] + [vmem((2 * slots, cols), BF16)] * bands,
        [me_arg, band_arg, lower, upper],
        [(value, True) for value in planes]
        + [(psi_t, False), (first, True), (col_row, False), (back, False), (pick, False)],
        [held, pltpu.VMEM((bands * 2 * slots, cols), BF16)],
    )
    (partial_sum,) = call(
        functools.partial(gram_kernel, bands, step),
        [vmem((2, bands, bands))],
        [band_arg],
        [(value, True) for value in exchange(packed, "band")],
        [pltpu.VMEM((cols // 128, bands * 2 * slots, 128), F32)],
    )
    sums = total(total(partial_sum, "grid", devices), "band", bands)
    own = bands // devices
    gram = lax.dynamic_slice(sums, (0, band, me * own), (2, 1, own)) / (4.0 * radius**3)
    return jnp.transpose(filtered, (0, 2, 1)).reshape(psi.shape), gram


def solution(mesh):
    return jax.shard_map(
        functools.partial(body, mesh.shape["grid"], mesh.shape["band"]),
        mesh=mesh,
        in_specs=(P(None, "band", "grid", None), P("grid"), P("grid", None), P(), P()),
        out_specs=(P(None, "band", "grid", None), P(None, "band", "grid")),
        check_vma=False,
    )
```

```python
import functools

import jax
import jax.numpy as jnp
import ml_dtypes
import numpy as np
from jax import lax
from jax.experimental import pallas as pl
from jax.experimental.pallas import tpu as pltpu
from jax.sharding import PartitionSpec as P

GY = 64
GX = 56
F32 = jnp.float32
BF16 = jnp.bfloat16
MIB = 1024 * 1024


def round_up(value, unit):
    return -(-value // unit) * unit


def halves(table):
    table = np.asarray(table, np.float32)
    high = table.astype(ml_dtypes.bfloat16)
    low = (table - high.astype(np.float32)).astype(ml_dtypes.bfloat16)
    return high, low


def stacked_table(table, axis):
    high, low = halves(table)
    return np.concatenate([high, high, low], axis=axis)


def folded(index, size):
    return np.where(index < size // 2, index, index - size)


def z_tables(size, devices, pad):
    depth = size // devices
    rows = 2 * pad
    freq = np.arange(size)
    ahead = np.zeros((devices, rows, 2 * size))
    back = np.zeros((2 * size, devices * rows))
    for d in range(devices):
        plane = d * depth + np.arange(depth)
        angle = 2 * np.pi * ((plane[:, None] * freq[None, :]) % size) / size
        c, s = np.cos(angle), np.sin(angle)
        ahead[d, :depth, :size], ahead[d, :depth, size:] = c, -s
        ahead[d, pad : pad + depth, :size], ahead[d, pad : pad + depth, size:] = s, c
        at = d * rows
        back[:size, at : at + depth], back[:size, at + pad : at + pad + depth] = c.T, s.T
        back[size:, at : at + depth], back[size:, at + pad : at + pad + depth] = -s.T, c.T
    return stacked_table(ahead, 2), stacked_table(back, 1)


def plane_tables(size):
    radius = size // 4
    count = 2 * radius + 1
    freq = np.arange(count) - radius
    angle = 2 * np.pi * ((freq[:, None] * np.arange(size)[None, :]) % size) / size
    c, s = np.cos(angle), np.sin(angle)
    ty = np.zeros((2 * GY, 256))
    ty[:count, :size], ty[:count, 128 : 128 + size] = c, s
    ty[GY : GY + count, :size], ty[GY : GY + count, 128 : 128 + size] = -s, c
    tyb = np.zeros((256, 2 * GY))
    tyb[:size, :count], tyb[:size, GY : GY + count] = c.T, -s.T
    tyb[128 : 128 + size, :count], tyb[128 : 128 + size, GY : GY + count] = s.T, c.T
    tx = np.zeros((2 * size, 2 * GX))
    tx[:size, :count], tx[:size, GX : GX + count] = c.T, -s.T
    tx[size:, :count], tx[size:, GX : GX + count] = s.T, c.T
    txb = np.zeros((2 * GX, 2 * size))
    txb[:count, :size], txb[:count, size:] = c, s
    txb[GX : GX + count, :size], txb[GX : GX + count, size:] = -s, c
    return stacked_table(ty, 0), stacked_table(tx, 1), stacked_table(txb, 1), stacked_table(tyb, 0)


def packing(size):
    radius = size // 4
    widths = [int(np.sqrt(radius * radius - g * g)) for g in range(-radius, radius + 1)]
    slots, free = [None] * len(widths), []
    for i in sorted(range(len(widths)), key=lambda j: (-widths[j], j)):
        span = 2 * widths[i] + 1
        for s in range(len(free) + 1):
            if s == len(free):
                free.append(128)
            if free[s] >= span:
                slots[i] = (widths[i], s, 128 - free[s] + widths[i])
                free[s] -= span
                break
    return slots, round_up(len(free), 2)


def split(value):
    high = value.astype(BF16)
    low = (value - high.astype(F32)).astype(BF16)
    return high, low


def tripled(value, axis):
    high, low = split(value)
    return jnp.concatenate([high, low, high], axis=axis)


def dot(a, b, dims=((1,), (0,))):
    return lax.dot_general(a, b, (dims, ((), ())), preferred_element_type=F32)


SMEM = pl.BlockSpec(memory_space=pltpu.SMEM)
VMEM = pl.BlockSpec(memory_space=pltpu.VMEM)
HBM = pl.BlockSpec(memory_space=pltpu.HBM)


def call(kernel, out_shape, scalars, arrays, scratch=(), limit=24, far=False):
    arrays = [pltpu.with_memory_space_constraint(value, pltpu.VMEM) if keep else value for value, keep in arrays]
    return pl.pallas_call(
        kernel,
        out_shape=out_shape,
        in_specs=[SMEM] * len(scalars) + [HBM if far else VMEM] * len(arrays),
        out_specs=[VMEM] * len(out_shape),
        scratch_shapes=list(scratch),
        compiler_params=pltpu.CompilerParams(vmem_limit_bytes=limit * MIB),
    )(*scalars, *arrays)


def position(col_row, size):
    place = col_row.astype(F32)
    kx = jnp.floor((place + 0.5) * (1.0 / size))
    ky = place - kx * size
    half = float(size // 2)
    return jnp.where(kx < half, kx, kx - size), jnp.where(ky < half, ky, ky - size)


def sphere(col_row, size):
    cols = col_row.shape[1]
    radius = size // 4
    gx, gy = position(col_row, size)
    index = lax.broadcasted_iota(jnp.int32, (size, cols), 0)
    freq = jnp.where(index < size // 2, index, index - size).astype(F32)
    radius2 = (gx * gx + gy * gy) + freq * freq
    return radius2 <= float(radius * radius), radius2 * (2.0 / (radius * radius))


def to_planes(me, parts, table_ref, outs, step):
    value = tripled(jnp.concatenate(parts, axis=0), 0)
    table = jnp.concatenate([table_ref[step(me, k)] for k in range(len(outs))], axis=0)
    total = dot(table, value)
    rows = table_ref.shape[1]
    for k in range(len(outs)):
        outs[k][:rows] = total[k * rows : (k + 1) * rows]


def from_planes(me, planes, table_ref, held, step, size):
    rows = planes[0].shape[0]
    third = rows * len(planes)
    for k in range(len(planes)):
        high, low = split(planes[k][...])
        at = step(me, k) * rows
        for j, value in enumerate((high, low, high)):
            held[pl.ds(pl.multiple_of(j * third + at, 16), rows), :] = value
    total = dot(table_ref[...], held[...])
    return total[:size], total[size:]


def first_kernel(devices, step, size, me_ref, *refs):
    far, refs = refs[:3], refs[3:]
    outs, (psi_ref, col_ref, ahead_ref, sems) = refs[:devices], refs[devices:]
    copies = [pltpu.make_async_copy(far[i], refs[devices + i], sems.at[i]) for i in range(3)]
    for copy in copies:
        copy.start()
    for copy in copies:
        copy.wait()
    inside, _ = sphere(col_ref[...], size)
    parts = [jnp.where(inside, psi_ref[p], 0.0) for p in range(2)]
    to_planes(me_ref[0], parts, ahead_ref, outs, step)
    radius = size // 4
    gx, gy = position(col_ref[...], size)
    used = gx * gx + gy * gy <= float(radius * radius)
    rows = ahead_ref.shape[1]
    row = lax.broadcasted_iota(jnp.int32, (8, gx.shape[1]), 0)
    slot, lane = jnp.zeros(row.shape, F32), jnp.zeros(row.shape, F32)
    for i, (_, s, middle) in enumerate(packing(size)[0]):
        here = gx == float(i - radius)
        slot, lane = jnp.where(here, float(s), slot), jnp.where(here, float(middle), lane)
    place = jnp.where(used, jnp.where(row == 0, slot, lane + gy), -9.0)
    for k in range(devices):
        outs[k][rows:] = place


def middle_kernel(devices, step, size, me_ref, low_ref, up_ref, *refs):
    planes, refs = refs[:devices], refs[devices:]
    psi_ref, col_ref, ahead_ref, back_ref, first_ref = refs[:5]
    outs, held = refs[5 : 5 + devices], refs[5 + devices]
    center = (up_ref[0] + low_ref[0]) / 2.0
    half = (up_ref[0] - low_ref[0]) / 2.0
    inside, kinetic = sphere(col_ref[...], size)
    back = from_planes(me_ref[0], planes, back_ref, held, step, size)
    parts = []
    for p in range(2):
        value = jnp.where(inside, ((kinetic - center) * psi_ref[p] + back[p]) / half, 0.0)
        first_ref[p] = value
        parts.append(value)
    to_planes(me_ref[0], parts, ahead_ref, outs, step)


def last_kernel(devices, bands, step, band_step, size, me_ref, band_ref, low_ref, up_ref, *refs):
    planes, refs = refs[:devices], refs[devices:]
    psi_ref, first_ref, col_ref, back_ref, pick_ref, filtered_ref = refs[:6]
    outs, (held, packed) = refs[6 : 6 + bands], refs[6 + bands :]
    center = (up_ref[0] + low_ref[0]) / 2.0
    half = (up_ref[0] - low_ref[0]) / 2.0
    inside, kinetic = sphere(col_ref[...], size)
    back = from_planes(me_ref[0], planes, back_ref, held, step, size)
    total = None
    for p in range(2):
        value = 2.0 * ((kinetic - center) * first_ref[p] + back[p]) / half - psi_ref[p]
        value = jnp.where(inside, value, 0.0)
        filtered_ref[p] = value
        piece = dot(pick_ref[p], value.astype(BF16))
        total = piece if total is None else total + piece
    packed[...] = total.astype(BF16)
    rows = packed.shape[0] // bands
    for k in range(bands):
        outs[k][...] = packed[pl.ds(pl.multiple_of(band_step(band_ref[0], k) * rows, 16), rows), :]


def gram_kernel(bands, band_step, band_ref, *refs):
    parts, sum_ref, held = refs[:bands], refs[bands], refs[bands + 1]
    rows, cols = parts[0].shape
    blocks = cols // 128
    for k in range(bands):
        at = pl.multiple_of(band_step(band_ref[0], k) * rows, 16)
        value = parts[k][...].astype(F32)
        for j in range(blocks):
            held[j, pl.ds(at, rows), :] = value[:, 128 * j : 128 * j + 128]
    lines = [[held[j, pl.ds(r, bands, stride=rows), :] for j in range(blocks)] for r in range(rows)]
    real = jnp.concatenate([v for r in range(rows // 2) for v in lines[r]], axis=1)
    imag = jnp.concatenate([v for r in range(rows // 2, rows) for v in lines[r]], axis=1)
    left = jnp.concatenate([real, imag], axis=1).astype(BF16)
    right = jnp.concatenate([imag, -real], axis=1).astype(BF16)
    wide = lax.broadcasted_iota(jnp.int32, (bands, 128), 1) < bands
    for p, other in enumerate((left, right)):
        tall = jnp.concatenate([other, jnp.zeros((128 - bands, other.shape[1]), BF16)], axis=0)
        value = jnp.where(wide, dot(left, tall, ((1,), (1,))), 0.0)
        for g in range(sum_ref.shape[0] // bands):
            sum_ref[g * bands : (g + 1) * bands, p, :] = value


def slab_kernel(devices, size, depth, again, *refs):
    planes, refs = refs[:devices], refs[devices:]
    marks = planes
    if again:
        marks, refs = refs[:devices], refs[devices:]
    pot_ref, ty_ref, tx_ref, txb_ref, tyb_ref = refs[:5]
    outs = refs[5 : 5 + devices]
    in_ref, y0_ref, y1_ref, back_ref, q_ref, box_ref = refs[5 + devices :]
    pad = round_up(depth, 8)
    rows = 2 * pad
    cols = planes[0].shape[1]
    radius = size // 4
    places, slots = packing(size)
    zero = jnp.zeros((), BF16)
    lane = lax.broadcasted_iota(jnp.int32, (pad, 128), 1)

    def between(first, last):
        return (lane >= first) & (lane <= last)

    def one_hot(k, at, wide):
        slot = jnp.broadcast_to(marks[k][rows : rows + 1, at : at + wide], (16, wide)).astype(BF16)
        spot = jnp.broadcast_to(marks[k][rows + 1 : rows + 2, at : at + wide], (128, wide))
        down = lax.broadcasted_iota(jnp.int32, (128, wide), 0).astype(F32)
        hot = jnp.where(spot == down, 1.0, 0.0).astype(BF16)
        return slot, [hot[16 * i : 16 * i + 16] for i in range(8)]

    def expand(pieces, first, count):
        slot, hot = pieces
        tall = []
        for v in range(first, first + count):
            here = slot == float(v)
            tall += [jnp.where(here, piece, zero) for piece in hot]
        return jnp.concatenate(tall, axis=0)

    lhs = jnp.concatenate(split(jnp.concatenate([ref[:rows] for ref in planes], axis=1)), axis=0)
    sources = [one_hot(k, 0, cols) for k in range(devices)]
    whole = (
        jnp.concatenate([s[0] for s in sources], axis=1),
        [jnp.concatenate([s[1][i] for s in sources], axis=1) for i in range(8)],
    )
    for t in range(0, slots, 2):
        got = dot(lhs, expand(whole, t, 2), ((1,), (1,)))
        got = got[:rows] + got[rows:]
        for i, (width, slot, middle) in enumerate(places):
            if slot // 2 * 2 != t:
                continue
            at = 128 * (slot - t)
            re = pltpu.roll(got[:pad, at : at + 128], (radius - middle) % 128, 1)
            im = pltpu.roll(got[pad:, at : at + 128], (radius + GY - middle) % 128, 1)
            im = jnp.where(between(GY + radius - width, GY + radius + width), im, 0.0)
            in_ref[i * pad : (i + 1) * pad] = jnp.where(between(radius - width, radius + width), re, im)
    in_ref[len(places) * pad :] = jnp.zeros(((GX - len(places)) * pad, 128), F32)
    moved = dot(tripled(in_ref[...], 1), ty_ref[...])
    y0_ref[...] = moved[:, :128]
    y1_ref[...] = moved[:, 128:]
    if depth < pad:
        q_ref[depth * GX :] = jnp.zeros(((pad - depth) * GX, 128), F32)

    chunk = 8
    for first in range(0, depth, chunk):
        last = min(depth, first + chunk)
        for z in range(first, last, 2):
            sides = []
            for w in range(2):
                line = pl.ds(z + w, GX, stride=pad)
                sides.append(jnp.concatenate([y0_ref[line, :], y1_ref[line, :]], axis=0))
            field = dot(tx_ref[...], tripled(jnp.concatenate(sides, axis=1), 0))
            pot = jnp.concatenate([pot_ref[z], pot_ref[z + 1]], axis=1)
            field = field * jnp.concatenate([pot, pot], axis=0)
            back = dot(txb_ref[...], tripled(field, 0))
            for w in range(2):
                for p in range(2):
                    back_ref[(z + w) * GX : (z + w + 1) * GX, 128 * p : 128 * p + 128] = back[
                        p * GX : (p + 1) * GX, 128 * w : 128 * w + 128
                    ]
        part = slice(first * GX, last * GX)
        q_ref[part] = dot(tripled(back_ref[part], 1), tyb_ref[...])

    for s in range(slots):
        re, im = jnp.zeros((pad, 128), F32), jnp.zeros((pad, 128), F32)
        for i, (width, slot, middle) in enumerate(places):
            if slot != s:
                continue
            value = q_ref[pl.ds(i, pad, stride=GX), :]
            here = between(middle - width, middle + width)
            re = jnp.where(here, pltpu.roll(value, (middle - radius) % 128, 1), re)
            im = jnp.where(here, pltpu.roll(value, (middle - radius - GY) % 128, 1), im)
        box_ref[:, 128 * s : 128 * s + 128] = jnp.concatenate(split(jnp.concatenate([re, im], axis=0)), axis=0)

    box = box_ref[...]
    wide = min(256, cols)
    for k in range(devices):
        for at in range(0, cols, wide):
            got = dot(box, expand(one_hot(k, at, wide), 0, slots))
            outs[k][:, at : at + wide] = got[:rows] + got[rows:]


def body(devices, bands, psi, col_map, potential, lower, upper):
    cols, size = psi.shape[2], psi.shape[3]
    radius = size // 4
    depth = size // devices
    pad = round_up(depth, 8)
    rows = 2 * pad
    me, band = lax.axis_index("grid"), lax.axis_index("band")
    me_arg = me.astype(jnp.int32).reshape(1)
    band_arg = band.astype(jnp.int32).reshape(1)
    if devices & (devices - 1) or bands & (bands - 1):
        raise ValueError("mesh size")

    def step(at, k):
        return at ^ k

    def exchange(values, axis="grid"):
        size = len(values)
        return [values[0]] + [
            lax.ppermute(values[k], axis, [(d, step(d, k)) for d in range(size)]) for k in range(1, size)
        ]

    ahead, back = z_tables(size, devices, pad)
    tables = plane_tables(size)
    count = 2 * radius + 1
    slots = round_up(-(-count // bands), 8)
    pick = np.zeros((2, bands * 2 * slots, size), ml_dtypes.bfloat16)
    for j in range(count):
        at = (j % bands) * 2 * slots + j // bands
        pick[0, at, (j - radius) % size] = 1
        pick[1, at + slots, (j - radius) % size] = 1

    pot = (potential * (1.0 / float(size**3))).reshape(depth, size, size)
    pot = jnp.pad(pot, ((0, 0), (0, 0), (0, 128 - size)))
    psi_t = jnp.transpose(psi.reshape(2, cols, size), (0, 2, 1))
    col_row = col_map.reshape(1, cols)

    def vmem(shape, dtype=F32):
        return pltpu.VMEM(shape, dtype)

    marks = exchange(
        call(
            functools.partial(first_kernel, devices, step, size),
            [vmem((rows + 8, cols))] * devices,
            [me_arg],
            [(psi_t, False), (col_row, False), (ahead, False)],
            [
                pltpu.VMEM(psi_t.shape, F32),
                pltpu.VMEM(col_row.shape, jnp.int32),
                pltpu.VMEM(ahead.shape, BF16),
                pltpu.SemaphoreType.DMA((3,)),
            ],
            far=True,
        )
    )

    def slab(values, again):
        given = values + (marks if again else [])
        return call(
            functools.partial(slab_kernel, devices, size, depth, again),
            [vmem((rows, cols))] * devices,
            [],
            [(value, True) for value in given] + [(pot, False)] + [(table, False) for table in tables],
            [
                pltpu.VMEM((GX * pad, 128), F32),
                pltpu.VMEM((GX * pad, 128), F32),
                pltpu.VMEM((GX * pad, 128), F32),
                pltpu.VMEM((pad * GX, 256), F32),
                pltpu.VMEM((pad * GX, 128), F32),
                pltpu.VMEM((2 * rows, 128 * packing(size)[1]), BF16),
            ],
        )

    held = pltpu.VMEM((3 * devices * rows, cols), BF16)
    planes = exchange(slab(marks, False))
    first, *sent = call(
        functools.partial(middle_kernel, devices, step, size),
        [vmem((2, size, cols))] + [vmem((rows, cols))] * devices,
        [me_arg, lower, upper],
        [(value, True) for value in planes] + [(psi_t, False), (col_row, False), (ahead, False), (back, False)],
        [held],
    )
    planes = exchange(slab(exchange(sent), True))
    filtered, *packed = call(
        functools.partial(last_kernel, devices, bands, step, step, size),
        [jax.ShapeDtypeStruct((2, size, cols), F32)] + [vmem((2 * slots, cols), BF16)] * bands,
        [me_arg, band_arg, lower, upper],
        [(value, True) for value in planes]
        + [(psi_t, False), (first, True), (col_row, False), (back, False), (pick, False)],
        [held, pltpu.VMEM((bands * 2 * slots, cols), BF16)],
    )
    (partial_sum,) = call(
        functools.partial(gram_kernel, bands, step),
        [vmem((devices * bands, 8, 128))],
        [band_arg],
        [(value, True) for value in exchange(packed, "band")],
        [pltpu.VMEM((cols // 128, bands * 2 * slots, 128), F32)],
    )
    sums = jnp.sum(lax.all_to_all(partial_sum, ("grid", "band"), 0, 0, tiled=True), axis=0)
    own = bands // devices
    gram = lax.dynamic_slice(sums, (0, me * own), (2, own)).reshape(2, 1, own) / (4.0 * radius**3)
    return jnp.transpose(filtered, (0, 2, 1)).reshape(psi.shape), gram


def solution(mesh):
    return jax.shard_map(
        functools.partial(body, mesh.shape["grid"], mesh.shape["band"]),
        mesh=mesh,
        in_specs=(P(None, "band", "grid", None), P("grid"), P("grid", None), P(), P()),
        out_specs=(P(None, "band", "grid", None), P(None, "band", "grid")),
        check_vma=False,
    )
```

```python
import functools

import jax
import jax.numpy as jnp
import ml_dtypes
import numpy as np
from jax import lax
from jax.experimental import pallas as pl
from jax.experimental.pallas import tpu as pltpu
from jax.sharding import PartitionSpec as P

GY = 64
GX = 56
F32 = jnp.float32
BF16 = jnp.bfloat16
MIB = 1024 * 1024


def round_up(value, unit):
    return -(-value // unit) * unit


def halves(table):
    table = np.asarray(table, np.float32)
    high = table.astype(ml_dtypes.bfloat16)
    low = (table - high.astype(np.float32)).astype(ml_dtypes.bfloat16)
    return high, low


def stacked_table(table, axis):
    high, low = halves(table)
    return np.concatenate([high, high, low], axis=axis)


def folded(index, size):
    return np.where(index < size // 2, index, index - size)


def z_tables(size, devices, pad):
    depth = size // devices
    rows = 2 * pad
    freq = np.arange(size)
    ahead = np.zeros((devices, rows, 2 * size))
    back = np.zeros((2 * size, devices * rows))
    for d in range(devices):
        plane = d * depth + np.arange(depth)
        angle = 2 * np.pi * ((plane[:, None] * freq[None, :]) % size) / size
        c, s = np.cos(angle), np.sin(angle)
        ahead[d, :depth, :size], ahead[d, :depth, size:] = c, -s
        ahead[d, pad : pad + depth, :size], ahead[d, pad : pad + depth, size:] = s, c
        at = d * rows
        back[:size, at : at + depth], back[:size, at + pad : at + pad + depth] = c.T, s.T
        back[size:, at : at + depth], back[size:, at + pad : at + pad + depth] = -s.T, c.T
    return stacked_table(ahead, 2), stacked_table(back, 1)


def plane_tables(size):
    radius = size // 4
    count = 2 * radius + 1
    freq = np.arange(count) - radius
    angle = 2 * np.pi * ((freq[:, None] * np.arange(size)[None, :]) % size) / size
    c, s = np.cos(angle), np.sin(angle)
    ty = np.zeros((2 * GY, 256))
    ty[:count, :size], ty[:count, 128 : 128 + size] = c, s
    ty[GY : GY + count, :size], ty[GY : GY + count, 128 : 128 + size] = -s, c
    tyb = np.zeros((256, 2 * GY))
    tyb[:size, :count], tyb[:size, GY : GY + count] = c.T, -s.T
    tyb[128 : 128 + size, :count], tyb[128 : 128 + size, GY : GY + count] = s.T, c.T
    tx = np.zeros((2 * size, 2 * GX))
    tx[:size, :count], tx[:size, GX : GX + count] = c.T, -s.T
    tx[size:, :count], tx[size:, GX : GX + count] = s.T, c.T
    txb = np.zeros((2 * GX, 2 * size))
    txb[:count, :size], txb[:count, size:] = c, s
    txb[GX : GX + count, :size], txb[GX : GX + count, size:] = -s, c
    high, low = halves(tx)
    tx = np.concatenate([np.concatenate([high, high], 1), np.concatenate([low, 0 * low], 1)], 0)
    return stacked_table(ty, 0), tx, np.concatenate(halves(txb), 0), stacked_table(tyb, 0)


def packing(size):
    radius = size // 4
    widths = [int(np.sqrt(radius * radius - g * g)) for g in range(-radius, radius + 1)]
    slots, free = [None] * len(widths), []
    for i in sorted(range(len(widths)), key=lambda j: (-widths[j], j)):
        span = 2 * widths[i] + 1
        for s in range(len(free) + 1):
            if s == len(free):
                free.append(128)
            if free[s] >= span:
                slots[i] = (widths[i], s, 128 - free[s] + widths[i])
                free[s] -= span
                break
    return slots, round_up(len(free), 2)


def split(value):
    high = value.astype(BF16)
    low = (value - high.astype(F32)).astype(BF16)
    return high, low


def tripled(value, axis):
    high, low = split(value)
    return jnp.concatenate([high, low, high], axis=axis)


def dot(a, b, dims=((1,), (0,))):
    return lax.dot_general(a, b, (dims, ((), ())), preferred_element_type=F32)


SMEM = pl.BlockSpec(memory_space=pltpu.SMEM)
VMEM = pl.BlockSpec(memory_space=pltpu.VMEM)
HBM = pl.BlockSpec(memory_space=pltpu.HBM)


def call(kernel, out_shape, scalars, arrays, scratch=(), limit=24, far=False):
    space = pltpu.HBM if far else pltpu.VMEM
    arrays = [pltpu.with_memory_space_constraint(value, space) if keep else value for value, keep in arrays]
    return pl.pallas_call(
        kernel,
        out_shape=out_shape,
        in_specs=[SMEM] * len(scalars) + [HBM if far else VMEM] * len(arrays),
        out_specs=[VMEM] * len(out_shape),
        scratch_shapes=list(scratch),
        compiler_params=pltpu.CompilerParams(vmem_limit_bytes=limit * MIB),
    )(*scalars, *arrays)


def position(col_row, size):
    place = col_row.astype(F32)
    kx = jnp.floor((place + 0.5) * (1.0 / size))
    ky = place - kx * size
    half = float(size // 2)
    return jnp.where(kx < half, kx, kx - size), jnp.where(ky < half, ky, ky - size)


def sphere(col_row, size):
    cols = col_row.shape[1]
    radius = size // 4
    gx, gy = position(col_row, size)
    index = lax.broadcasted_iota(jnp.int32, (size, cols), 0)
    freq = jnp.where(index < size // 2, index, index - size).astype(F32)
    radius2 = (gx * gx + gy * gy) + freq * freq
    return radius2 <= float(radius * radius), radius2 * (2.0 / (radius * radius))


def to_planes(me, parts, table_ref, outs, step):
    value = tripled(jnp.concatenate(parts, axis=0), 0)
    table = jnp.concatenate([table_ref[step(me, k)] for k in range(len(outs))], axis=0)
    total = dot(table, value)
    rows = table_ref.shape[1]
    for k in range(len(outs)):
        outs[k][:rows] = total[k * rows : (k + 1) * rows]


def from_planes(me, planes, table_ref, held, step, size):
    rows = planes[0].shape[0]
    third = rows * len(planes)
    for k in range(len(planes)):
        high, low = split(planes[k][...])
        at = step(me, k) * rows
        for j, value in enumerate((high, low, high)):
            held[pl.ds(pl.multiple_of(j * third + at, 16), rows), :] = value
    total = dot(table_ref[...], held[...])
    return total[:size], total[size:]


def first_kernel(devices, step, size, me_ref, *refs):
    far, refs = refs[:3], refs[3:]
    outs, (psi_ref, col_ref, ahead_ref, sems) = refs[:devices], refs[devices:]
    copies = [pltpu.make_async_copy(far[i], refs[devices + i], sems.at[i]) for i in range(3)]
    for copy in copies:
        copy.start()
    for copy in copies:
        copy.wait()
    inside, _ = sphere(col_ref[...], size)
    parts = [jnp.where(inside, psi_ref[p], 0.0) for p in range(2)]
    to_planes(me_ref[0], parts, ahead_ref, outs, step)
    radius = size // 4
    gx, gy = position(col_ref[...], size)
    used = gx * gx + gy * gy <= float(radius * radius)
    rows = ahead_ref.shape[1]
    row = lax.broadcasted_iota(jnp.int32, (8, gx.shape[1]), 0)
    slot, lane = jnp.zeros(row.shape, F32), jnp.zeros(row.shape, F32)
    for i, (_, s, middle) in enumerate(packing(size)[0]):
        here = gx == float(i - radius)
        slot, lane = jnp.where(here, float(s), slot), jnp.where(here, float(middle), lane)
    place = jnp.where(used, jnp.where(row == 0, slot, lane + gy), -9.0)
    for k in range(devices):
        outs[k][rows:] = place


def middle_kernel(devices, step, size, me_ref, low_ref, up_ref, *refs):
    planes, refs = refs[:devices], refs[devices:]
    psi_ref, col_ref, ahead_ref, back_ref, first_ref = refs[:5]
    outs, held = refs[5 : 5 + devices], refs[5 + devices]
    center = (up_ref[0] + low_ref[0]) / 2.0
    half = (up_ref[0] - low_ref[0]) / 2.0
    inside, kinetic = sphere(col_ref[...], size)
    back = from_planes(me_ref[0], planes, back_ref, held, step, size)
    parts = []
    for p in range(2):
        value = jnp.where(inside, ((kinetic - center) * psi_ref[p] + back[p]) / half, 0.0)
        first_ref[p] = value
        parts.append(value)
    to_planes(me_ref[0], parts, ahead_ref, outs, step)


def last_kernel(devices, bands, step, size, me_ref, low_ref, up_ref, *refs):
    planes, refs = refs[:devices], refs[devices:]
    psi_ref, first_ref, col_ref, back_ref, pick_ref, filtered_ref, packed_ref, held = refs
    center = (up_ref[0] + low_ref[0]) / 2.0
    half = (up_ref[0] - low_ref[0]) / 2.0
    inside, kinetic = sphere(col_ref[...], size)
    back = from_planes(me_ref[0], planes, back_ref, held, step, size)
    total = None
    for p in range(2):
        value = 2.0 * ((kinetic - center) * first_ref[p] + back[p]) / half - psi_ref[p]
        value = jnp.where(inside, value, 0.0)
        filtered_ref[p] = value
        piece = dot(pick_ref[p], value.astype(BF16))
        total = piece if total is None else total + piece
    rows = packed_ref.shape[1]
    for k in range(bands):
        packed_ref[k] = total[k * rows : (k + 1) * rows].astype(BF16)


def gram_kernel(bands, parts_ref, sum_ref, held):
    rows, cols = parts_ref.shape[1:]
    blocks = cols // 128
    for k in range(bands):
        value = parts_ref[k].astype(F32)
        for j in range(blocks):
            held[j, k * rows : (k + 1) * rows, :] = value[:, 128 * j : 128 * j + 128]
    lines = [[held[j, pl.ds(r, bands, stride=rows), :] for j in range(blocks)] for r in range(rows)]
    real = jnp.concatenate([v for r in range(rows // 2) for v in lines[r]], axis=1)
    imag = jnp.concatenate([v for r in range(rows // 2, rows) for v in lines[r]], axis=1)
    left = jnp.concatenate([real, imag], axis=1).astype(BF16)
    right = jnp.concatenate([imag, -real], axis=1).astype(BF16)
    none = jnp.zeros((GY - bands, left.shape[1]), BF16)
    tall = jnp.concatenate([left, none, right, none], axis=0)
    value = dot(left, tall, ((1,), (1,)))
    for g in range(sum_ref.shape[0] // bands):
        sum_ref[g * bands : (g + 1) * bands, 0, :] = value


def slab_kernel(devices, size, depth, again, *refs):
    planes, refs = refs[:devices], refs[devices:]
    marks = planes
    if again:
        marks, refs = refs[:devices], refs[devices:]
    pot_ref, ty_ref, tx_ref, txb_ref, tyb_ref = refs[:5]
    outs = refs[5 : 5 + devices]
    in_ref, y0_ref, y1_ref, back_ref, q_ref, box_ref = refs[5 + devices :]
    pad = round_up(depth, 8)
    rows = 2 * pad
    cols = planes[0].shape[1]
    radius = size // 4
    places, slots = packing(size)
    zero = jnp.zeros((), BF16)
    lane = lax.broadcasted_iota(jnp.int32, (pad, 128), 1)

    def between(first, last):
        return (lane >= first) & (lane <= last)

    def one_hot(k, at, wide):
        slot = jnp.broadcast_to(marks[k][rows : rows + 1, at : at + wide], (16, wide)).astype(BF16)
        spot = jnp.broadcast_to(marks[k][rows + 1 : rows + 2, at : at + wide], (128, wide))
        down = lax.broadcasted_iota(jnp.int32, (128, wide), 0).astype(F32)
        hot = jnp.where(spot == down, 1.0, 0.0).astype(BF16)
        return slot, [hot[16 * i : 16 * i + 16] for i in range(8)]

    def expand(pieces, first, count):
        slot, hot = pieces
        tall = []
        for v in range(first, first + count):
            here = slot == float(v)
            tall += [jnp.where(here, piece, zero) for piece in hot]
        return jnp.concatenate(tall, axis=0)

    lhs = jnp.concatenate(split(jnp.concatenate([ref[:rows] for ref in planes], axis=1)), axis=0)
    sources = [one_hot(k, 0, cols) for k in range(devices)]
    whole = (
        jnp.concatenate([s[0] for s in sources], axis=1),
        [jnp.concatenate([s[1][i] for s in sources], axis=1) for i in range(8)],
    )
    for t in range(0, slots, 2):
        got = dot(lhs, expand(whole, t, 2), ((1,), (1,)))
        got = got[:rows] + got[rows:]
        for i, (width, slot, middle) in enumerate(places):
            if slot // 2 * 2 != t:
                continue
            at = 128 * (slot - t)
            re = pltpu.roll(got[:pad, at : at + 128], (radius - middle) % 128, 1)
            im = pltpu.roll(got[pad:, at : at + 128], (radius + GY - middle) % 128, 1)
            im = jnp.where(between(GY + radius - width, GY + radius + width), im, 0.0)
            in_ref[i * pad : (i + 1) * pad] = jnp.where(between(radius - width, radius + width), re, im)
    in_ref[len(places) * pad :] = jnp.zeros(((GX - len(places)) * pad, 128), F32)
    moved = dot(tripled(in_ref[...], 1), ty_ref[...])
    y0_ref[...] = moved[:, :128]
    y1_ref[...] = moved[:, 128:]
    if depth < pad:
        q_ref[depth * GX :] = jnp.zeros(((pad - depth) * GX, 128), F32)

    chunk, group = 8, 4
    for first in range(0, depth, chunk):
        last = min(depth, first + chunk)
        for z in range(first, last, group):
            near = range(z, min(z + group, last))
            sides = []
            for w in near:
                line = pl.ds(w, GX, stride=pad)
                sides.append(jnp.concatenate([y0_ref[line, :], y1_ref[line, :]], axis=0))
            field = dot(tx_ref[...], jnp.concatenate(split(jnp.concatenate(sides, axis=1)), axis=0))
            pot = jnp.concatenate([pot_ref[w] for w in near], axis=1)
            field = (field[: 2 * size] + field[2 * size :]) * jnp.concatenate([pot, pot], axis=0)
            high, low = split(field)
            back = dot(txb_ref[...], high)
            back = back[: 2 * GX] + back[2 * GX :] + dot(txb_ref[: 2 * GX], low)
            for w in near:
                for p in range(2):
                    at = 128 * (w - z)
                    back_ref[w * GX : (w + 1) * GX, 128 * p : 128 * p + 128] = back[
                        p * GX : (p + 1) * GX, at : at + 128
                    ]
        part = slice(first * GX, last * GX)
        q_ref[part] = dot(tripled(back_ref[part], 1), tyb_ref[...])

    for s in range(slots):
        re, im = jnp.zeros((pad, 128), F32), jnp.zeros((pad, 128), F32)
        for i, (width, slot, middle) in enumerate(places):
            if slot != s:
                continue
            value = q_ref[pl.ds(i, pad, stride=GX), :]
            here = between(middle - width, middle + width)
            re = jnp.where(here, pltpu.roll(value, (middle - radius) % 128, 1), re)
            im = jnp.where(here, pltpu.roll(value, (middle - radius - GY) % 128, 1), im)
        box_ref[:, 128 * s : 128 * s + 128] = jnp.concatenate(split(jnp.concatenate([re, im], axis=0)), axis=0)

    box = box_ref[...]
    wide = min(256, cols)
    for k in range(devices):
        for at in range(0, cols, wide):
            got = dot(box, expand(one_hot(k, at, wide), 0, slots))
            outs[k][:, at : at + wide] = got[:rows] + got[rows:]


def body(devices, bands, psi, col_map, potential, lower, upper):
    cols, size = psi.shape[2], psi.shape[3]
    radius = size // 4
    depth = size // devices
    pad = round_up(depth, 8)
    rows = 2 * pad
    me = lax.axis_index("grid")
    me_arg = me.astype(jnp.int32).reshape(1)
    if devices & (devices - 1):
        raise ValueError("mesh size")

    def step(at, k):
        return at ^ k

    def exchange(values):
        return [values[0]] + [
            lax.ppermute(values[k], "grid", [(d, step(d, k)) for d in range(devices)]) for k in range(1, devices)
        ]

    ahead, back = z_tables(size, devices, pad)
    tables = plane_tables(size)
    count = 2 * radius + 1
    slots = round_up(-(-count // bands), 8)
    pick = np.zeros((2, bands * 2 * slots, size), ml_dtypes.bfloat16)
    for j in range(count):
        at = (j % bands) * 2 * slots + j // bands
        pick[0, at, (j - radius) % size] = 1
        pick[1, at + slots, (j - radius) % size] = 1

    pot = (potential * (1.0 / float(size**3))).reshape(depth, size, size)
    pot = jnp.pad(pot, ((0, 0), (0, 0), (0, 128 - size)))
    psi_t = jnp.transpose(psi.reshape(2, cols, size), (0, 2, 1))
    col_row = col_map.reshape(1, cols)

    def vmem(shape, dtype=F32):
        return pltpu.VMEM(shape, dtype)

    marks = exchange(
        call(
            functools.partial(first_kernel, devices, step, size),
            [vmem((rows + 8, cols))] * devices,
            [me_arg],
            [(psi_t, True), (col_row, True), (ahead, True)],
            [
                pltpu.VMEM(psi_t.shape, F32),
                pltpu.VMEM(col_row.shape, jnp.int32),
                pltpu.VMEM(ahead.shape, BF16),
                pltpu.SemaphoreType.DMA((3,)),
            ],
            far=True,
        )
    )

    def slab(values, again):
        given = values + (marks if again else [])
        return call(
            functools.partial(slab_kernel, devices, size, depth, again),
            [vmem((rows, cols))] * devices,
            [],
            [(value, True) for value in given] + [(pot, False)] + [(table, False) for table in tables],
            [
                pltpu.VMEM((GX * pad, 128), F32),
                pltpu.VMEM((GX * pad, 128), F32),
                pltpu.VMEM((GX * pad, 128), F32),
                pltpu.VMEM((pad * GX, 256), F32),
                pltpu.VMEM((pad * GX, 128), F32),
                pltpu.VMEM((2 * rows, 128 * packing(size)[1]), BF16),
            ],
        )

    held = pltpu.VMEM((3 * devices * rows, cols), BF16)
    planes = exchange(slab(marks, False))
    first, *sent = call(
        functools.partial(middle_kernel, devices, step, size),
        [vmem((2, size, cols))] + [vmem((rows, cols))] * devices,
        [me_arg, lower, upper],
        [(value, True) for value in planes] + [(psi_t, False), (col_row, False), (ahead, False), (back, False)],
        [held],
    )
    planes = exchange(slab(exchange(sent), True))
    filtered, packed = call(
        functools.partial(last_kernel, devices, bands, step, size),
        [vmem((2, size, cols)), vmem((bands, 2 * slots, cols), BF16)],
        [me_arg, lower, upper],
        [(value, True) for value in planes]
        + [(psi_t, False), (first, True), (col_row, False), (back, False), (pick, False)],
        [held],
    )
    (partial_sum,) = call(
        functools.partial(gram_kernel, bands),
        [vmem((devices * bands, 1, 128))],
        [],
        [(lax.all_to_all(packed, "band", 0, 0, tiled=True), True)],
        [pltpu.VMEM((cols // 128, bands * 2 * slots, 128), F32)],
    )
    sums = jnp.sum(lax.all_to_all(partial_sum, ("grid", "band"), 0, 0, tiled=True), axis=0)
    own = bands // devices
    sums = sums.reshape(2, 1, GY)
    gram = lax.dynamic_slice(sums, (0, 0, me * own), (2, 1, own)) / (4.0 * radius**3)
    return jnp.transpose(filtered, (0, 2, 1)).reshape(psi.shape), gram


def solution(mesh):
    return jax.shard_map(
        functools.partial(body, mesh.shape["grid"], mesh.shape["band"]),
        mesh=mesh,
        in_specs=(P(None, "band", "grid", None), P("grid"), P("grid", None), P(), P()),
        out_specs=(P(None, "band", "grid", None), P(None, "band", "grid")),
        check_vma=False,
    )
```

```python
import functools

import jax
import jax.numpy as jnp
import ml_dtypes
import numpy as np
from jax import lax
from jax.experimental import pallas as pl
from jax.experimental.pallas import tpu as pltpu
from jax.sharding import PartitionSpec as P

GY = 64
GX = 56
F32 = jnp.float32
BF16 = jnp.bfloat16
MIB = 1024 * 1024


def round_up(value, unit):
    return -(-value // unit) * unit


def halves(table):
    table = np.asarray(table, np.float32)
    high = table.astype(ml_dtypes.bfloat16)
    low = (table - high.astype(np.float32)).astype(ml_dtypes.bfloat16)
    return high, low


def stacked_table(table, axis):
    high, low = halves(table)
    return np.concatenate([high, high, low], axis=axis)


def folded(index, size):
    return np.where(index < size // 2, index, index - size)


def z_tables(size, devices, pad):
    depth = size // devices
    rows = 2 * pad
    freq = np.arange(size)
    ahead = np.zeros((devices, rows, 2 * size))
    back = np.zeros((2 * size, devices * rows))
    for d in range(devices):
        plane = d * depth + np.arange(depth)
        angle = 2 * np.pi * ((plane[:, None] * freq[None, :]) % size) / size
        c, s = np.cos(angle), np.sin(angle)
        ahead[d, :depth, :size], ahead[d, :depth, size:] = c, -s
        ahead[d, pad : pad + depth, :size], ahead[d, pad : pad + depth, size:] = s, c
        at = d * rows
        back[:size, at : at + depth], back[:size, at + pad : at + pad + depth] = c.T, s.T
        back[size:, at : at + depth], back[size:, at + pad : at + pad + depth] = -s.T, c.T
    return stacked_table(ahead, 2), stacked_table(back, 1)


def plane_tables(size):
    radius = size // 4
    count = 2 * radius + 1
    freq = np.arange(count) - radius
    angle = 2 * np.pi * ((freq[:, None] * np.arange(size)[None, :]) % size) / size
    c, s = np.cos(angle), np.sin(angle)
    ty = np.zeros((2 * GY, 256))
    ty[:count, :size], ty[:count, 128 : 128 + size] = c, s
    ty[GY : GY + count, :size], ty[GY : GY + count, 128 : 128 + size] = -s, c
    tyb = np.zeros((256, 2 * GY))
    tyb[:size, :count], tyb[:size, GY : GY + count] = c.T, -s.T
    tyb[128 : 128 + size, :count], tyb[128 : 128 + size, GY : GY + count] = s.T, c.T
    tx = np.zeros((2 * size, 2 * GX))
    tx[:size, :count], tx[:size, GX : GX + count] = c.T, -s.T
    tx[size:, :count], tx[size:, GX : GX + count] = s.T, c.T
    txb = np.zeros((2 * GX, 2 * size))
    txb[:count, :size], txb[:count, size:] = c, s
    txb[GX : GX + count, :size], txb[GX : GX + count, size:] = -s, c
    high, low = halves(tx)
    tx = np.concatenate([np.concatenate([high, high], 1), np.concatenate([low, 0 * low], 1)], 0)
    return stacked_table(ty, 0), tx, np.concatenate(halves(txb), 0), stacked_table(tyb, 0)


def packing(size):
    radius = size // 4
    widths = [int(np.sqrt(radius * radius - g * g)) for g in range(-radius, radius + 1)]
    slots, free = [None] * len(widths), []
    for i in sorted(range(len(widths)), key=lambda j: (-widths[j], j)):
        span = 2 * widths[i] + 1
        for s in range(len(free) + 1):
            if s == len(free):
                free.append(128)
            if free[s] >= span:
                slots[i] = (widths[i], s, 128 - free[s] + widths[i])
                free[s] -= span
                break
    return slots, round_up(len(free), 2)


def split(value):
    high = value.astype(BF16)
    low = (value - high.astype(F32)).astype(BF16)
    return high, low


def tripled(value, axis):
    high, low = split(value)
    return jnp.concatenate([high, low, high], axis=axis)


def dot(a, b, dims=((1,), (0,))):
    return lax.dot_general(a, b, (dims, ((), ())), preferred_element_type=F32)


SMEM = pl.BlockSpec(memory_space=pltpu.SMEM)
VMEM = pl.BlockSpec(memory_space=pltpu.VMEM)
HBM = pl.BlockSpec(memory_space=pltpu.HBM)


def call(kernel, out_shape, scalars, arrays, scratch=(), limit=24, far=False):
    space = pltpu.HBM if far else pltpu.VMEM
    arrays = [pltpu.with_memory_space_constraint(value, space) if keep else value for value, keep in arrays]
    return pl.pallas_call(
        kernel,
        out_shape=out_shape,
        in_specs=[SMEM] * len(scalars) + [HBM if far else VMEM] * len(arrays),
        out_specs=[VMEM] * len(out_shape),
        scratch_shapes=list(scratch),
        compiler_params=pltpu.CompilerParams(vmem_limit_bytes=limit * MIB),
    )(*scalars, *arrays)


def position(col_row, size):
    place = col_row.astype(F32)
    kx = jnp.floor((place + 0.5) * (1.0 / size))
    ky = place - kx * size
    half = float(size // 2)
    return jnp.where(kx < half, kx, kx - size), jnp.where(ky < half, ky, ky - size)


def sphere(col_row, size):
    cols = col_row.shape[1]
    radius = size // 4
    gx, gy = position(col_row, size)
    index = lax.broadcasted_iota(jnp.int32, (size, cols), 0)
    freq = jnp.where(index < size // 2, index, index - size).astype(F32)
    radius2 = (gx * gx + gy * gy) + freq * freq
    return radius2 <= float(radius * radius), radius2 * (2.0 / (radius * radius))


def to_planes(me, parts, table_ref, outs, step):
    value = tripled(jnp.concatenate(parts, axis=0), 0)
    table = jnp.concatenate([table_ref[step(me, k)] for k in range(len(outs))], axis=0)
    total = dot(table, value)
    rows = table_ref.shape[1]
    for k in range(len(outs)):
        outs[k][:rows] = total[k * rows : (k + 1) * rows]


def from_planes(me, planes, table_ref, held, step, size):
    rows = planes[0].shape[0]
    third = rows * len(planes)
    for k in range(len(planes)):
        high, low = split(planes[k][...])
        at = step(me, k) * rows
        for j, value in enumerate((high, low, high)):
            held[pl.ds(pl.multiple_of(j * third + at, 16), rows), :] = value
    total = dot(table_ref[...], held[...])
    return total[:size], total[size:]


def first_kernel(devices, step, size, me_ref, *refs):
    far, refs = refs[:3], refs[3:]
    outs, (psi_ref, col_ref, ahead_ref, sems) = refs[:devices], refs[devices:]
    copies = [pltpu.make_async_copy(far[i], refs[devices + i], sems.at[i]) for i in range(3)]
    for copy in copies:
        copy.start()
    for copy in copies:
        copy.wait()
    inside, _ = sphere(col_ref[...], size)
    parts = [jnp.where(inside, psi_ref[p], 0.0) for p in range(2)]
    to_planes(me_ref[0], parts, ahead_ref, outs, step)
    radius = size // 4
    gx, gy = position(col_ref[...], size)
    used = gx * gx + gy * gy <= float(radius * radius)
    rows = ahead_ref.shape[1]
    row = lax.broadcasted_iota(jnp.int32, (8, gx.shape[1]), 0)
    slot, lane = jnp.zeros(row.shape, F32), jnp.zeros(row.shape, F32)
    for i, (_, s, middle) in enumerate(packing(size)[0]):
        here = gx == float(i - radius)
        slot, lane = jnp.where(here, float(s), slot), jnp.where(here, float(middle), lane)
    place = jnp.where(used, jnp.where(row == 0, slot, lane + gy), -9.0)
    for k in range(devices):
        outs[k][rows:] = place


def middle_kernel(devices, step, size, me_ref, low_ref, up_ref, *refs):
    planes, refs = refs[:devices], refs[devices:]
    psi_ref, col_ref, ahead_ref, back_ref, first_ref = refs[:5]
    outs, held = refs[5 : 5 + devices], refs[5 + devices]
    center = (up_ref[0] + low_ref[0]) / 2.0
    half = (up_ref[0] - low_ref[0]) / 2.0
    inside, kinetic = sphere(col_ref[...], size)
    back = from_planes(me_ref[0], planes, back_ref, held, step, size)
    parts = []
    for p in range(2):
        value = jnp.where(inside, ((kinetic - center) * psi_ref[p] + back[p]) / half, 0.0)
        first_ref[p] = value
        parts.append(value)
    to_planes(me_ref[0], parts, ahead_ref, outs, step)


def last_kernel(devices, bands, step, size, me_ref, low_ref, up_ref, *refs):
    planes, refs = refs[:devices], refs[devices:]
    psi_ref, first_ref, col_ref, back_ref, pick_ref, filtered_ref, packed_ref, held = refs
    center = (up_ref[0] + low_ref[0]) / 2.0
    half = (up_ref[0] - low_ref[0]) / 2.0
    inside, kinetic = sphere(col_ref[...], size)
    back = from_planes(me_ref[0], planes, back_ref, held, step, size)
    total = None
    for p in range(2):
        value = 2.0 * ((kinetic - center) * first_ref[p] + back[p]) / half - psi_ref[p]
        value = jnp.where(inside, value, 0.0)
        filtered_ref[p] = value
        piece = dot(pick_ref[p], value.astype(BF16))
        total = piece if total is None else total + piece
    rows = packed_ref.shape[1]
    for k in range(bands):
        packed_ref[k] = total[k * rows : (k + 1) * rows].astype(BF16)


def gram_kernel(bands, parts_ref, sum_ref, held):
    rows, cols = parts_ref.shape[1:]
    blocks = cols // 128
    for k in range(bands):
        value = parts_ref[k].astype(F32)
        for j in range(blocks):
            held[j, k * rows : (k + 1) * rows, :] = value[:, 128 * j : 128 * j + 128]
    lines = [[held[j, pl.ds(r, bands, stride=rows), :] for j in range(blocks)] for r in range(rows)]
    real = jnp.concatenate([v for r in range(rows // 2) for v in lines[r]], axis=1)
    imag = jnp.concatenate([v for r in range(rows // 2, rows) for v in lines[r]], axis=1)
    left = jnp.concatenate([real, imag], axis=1).astype(BF16)
    right = jnp.concatenate([imag, -real], axis=1).astype(BF16)
    none = jnp.zeros((GY - bands, left.shape[1]), BF16)
    tall = jnp.concatenate([left, none, right, none], axis=0)
    value = dot(left, tall, ((1,), (1,)))
    for g in range(sum_ref.shape[0] // bands):
        sum_ref[g * bands : (g + 1) * bands, 0, :] = value


def slab_kernel(devices, size, depth, again, *refs):
    planes, refs = refs[:devices], refs[devices:]
    marks = planes
    if again:
        marks, refs = refs[:devices], refs[devices:]
    pot_ref, ty_ref, tx_ref, txb_ref, tyb_ref = refs[:5]
    outs = refs[5 : 5 + devices]
    in_ref, y0_ref, y1_ref, back_ref, q_ref, box_ref, slot_ref, spot_ref = refs[5 + devices :]
    pad = round_up(depth, 8)
    rows = 2 * pad
    cols = planes[0].shape[1]
    radius = size // 4
    places, slots = packing(size)
    zero = jnp.zeros((), BF16)
    lane = lax.broadcasted_iota(jnp.int32, (pad, 128), 1)

    def between(first, last):
        return (lane >= first) & (lane <= last)

    def one_hot(k, at, wide):
        slot = jnp.broadcast_to(marks[k][rows : rows + 1, at : at + wide], (16, wide)).astype(BF16)
        spot = jnp.broadcast_to(marks[k][rows + 1 : rows + 2, at : at + wide], (128, wide))
        down = lax.broadcasted_iota(jnp.int32, (128, wide), 0).astype(F32)
        hot = jnp.where(spot == down, 1.0, 0.0).astype(BF16)
        return slot, [hot[16 * i : 16 * i + 16] for i in range(8)]

    def expand(pieces, first, count):
        slot, hot = pieces
        tall = []
        for v in range(first, first + count):
            here = slot == float(v)
            tall += [jnp.where(here, piece, zero) for piece in hot]
        return jnp.concatenate(tall, axis=0)

    lhs = jnp.concatenate(split(jnp.concatenate([ref[:rows] for ref in planes], axis=1)), axis=0)
    row = lax.broadcasted_iota(jnp.int32, (8, 256), 0)
    side = lax.broadcasted_iota(jnp.int32, (8, 256), 1) // 128
    spread = jnp.where(row == side, 1.0, 0.0).astype(BF16)
    both = dot(jnp.concatenate([ref[rows : rows + 8].astype(BF16) for ref in marks], axis=1), spread, ((0,), (0,)))
    slot_ref[...] = both[:, :128].astype(BF16)
    along = lax.broadcasted_iota(jnp.int32, (cols * devices, 128), 1).astype(F32)
    spot_ref[...] = jnp.where(both[:, 128:] == along, 1.0, 0.0).astype(BF16)
    in_ref[...] = jnp.zeros(in_ref.shape, F32)
    for t in range(0, slots, 2):
        hot = [jnp.where(slot_ref[...] == float(v), spot_ref[...], zero) for v in (t, t + 1)]
        got = dot(lhs, jnp.concatenate(hot, axis=1))
        got = got[:rows] + got[rows:]
        for i, (width, slot, middle) in enumerate(places):
            if slot // 2 * 2 != t:
                continue
            at = 128 * (slot - t)
            re = pltpu.roll(got[:pad, at : at + 128], (radius - middle) % 128, 1)
            im = pltpu.roll(got[pad:, at : at + 128], (radius + GY - middle) % 128, 1)
            im = jnp.where(between(GY + radius - width, GY + radius + width), im, 0.0)
            in_ref[pl.ds(i, pad, stride=GX), :] = jnp.where(between(radius - width, radius + width), re, im)
    moved = dot(tripled(in_ref[...], 1), ty_ref[...])
    y0_ref[...] = moved[:, :128]
    y1_ref[...] = moved[:, 128:]
    if depth < pad:
        q_ref[depth * GX :] = jnp.zeros(((pad - depth) * GX, 128), F32)

    chunk, group = 8, 4
    for first in range(0, depth, chunk):
        last = min(depth, first + chunk)
        for z in range(first, last, group):
            near = range(z, min(z + group, last))
            sides = []
            for w in near:
                line = slice(w * GX, (w + 1) * GX)
                sides.append(jnp.concatenate([y0_ref[line, :], y1_ref[line, :]], axis=0))
            field = dot(tx_ref[...], jnp.concatenate(split(jnp.concatenate(sides, axis=1)), axis=0))
            pot = jnp.concatenate([pot_ref[w] for w in near], axis=1)
            field = (field[: 2 * size] + field[2 * size :]) * jnp.concatenate([pot, pot], axis=0)
            high, low = split(field)
            back = dot(txb_ref[...], high)
            back = back[: 2 * GX] + back[2 * GX :] + dot(txb_ref[: 2 * GX], low)
            for w in near:
                for p in range(2):
                    at = 128 * (w - z)
                    back_ref[w * GX : (w + 1) * GX, 128 * p : 128 * p + 128] = back[
                        p * GX : (p + 1) * GX, at : at + 128
                    ]
        part = slice(first * GX, last * GX)
        q_ref[part] = dot(tripled(back_ref[part], 1), tyb_ref[...])

    for s in range(slots):
        re, im = jnp.zeros((pad, 128), F32), jnp.zeros((pad, 128), F32)
        for i, (width, slot, middle) in enumerate(places):
            if slot != s:
                continue
            value = q_ref[pl.ds(i, pad, stride=GX), :]
            here = between(middle - width, middle + width)
            re = jnp.where(here, pltpu.roll(value, (middle - radius) % 128, 1), re)
            im = jnp.where(here, pltpu.roll(value, (middle - radius - GY) % 128, 1), im)
        box_ref[:, 128 * s : 128 * s + 128] = jnp.concatenate(split(jnp.concatenate([re, im], axis=0)), axis=0)

    box = box_ref[...]
    wide = min(256, cols)
    for k in range(devices):
        for at in range(0, cols, wide):
            got = dot(box, expand(one_hot(k, at, wide), 0, slots))
            outs[k][:, at : at + wide] = got[:rows] + got[rows:]


def body(devices, bands, psi, col_map, potential, lower, upper):
    cols, size = psi.shape[2], psi.shape[3]
    radius = size // 4
    depth = size // devices
    pad = round_up(depth, 8)
    rows = 2 * pad
    me = lax.axis_index("grid")
    me_arg = me.astype(jnp.int32).reshape(1)
    if devices & (devices - 1):
        raise ValueError("mesh size")

    def step(at, k):
        return at ^ k

    def exchange(values):
        return [values[0]] + [
            lax.ppermute(values[k], "grid", [(d, step(d, k)) for d in range(devices)]) for k in range(1, devices)
        ]

    ahead, back = z_tables(size, devices, pad)
    tables = plane_tables(size)
    count = 2 * radius + 1
    slots = round_up(-(-count // bands), 8)
    pick = np.zeros((2, bands * 2 * slots, size), ml_dtypes.bfloat16)
    for j in range(count):
        at = (j % bands) * 2 * slots + j // bands
        pick[0, at, (j - radius) % size] = 1
        pick[1, at + slots, (j - radius) % size] = 1

    pot = (potential * (1.0 / float(size**3))).reshape(depth, size, size)
    pot = jnp.pad(pot, ((0, 0), (0, 0), (0, 128 - size)))
    psi_t = jnp.transpose(psi.reshape(2, cols, size), (0, 2, 1))
    col_row = col_map.reshape(1, cols)

    def vmem(shape, dtype=F32):
        return pltpu.VMEM(shape, dtype)

    marks = exchange(
        call(
            functools.partial(first_kernel, devices, step, size),
            [vmem((rows + 8, cols))] * devices,
            [me_arg],
            [(psi_t, True), (col_row, True), (ahead, True)],
            [
                pltpu.VMEM(psi_t.shape, F32),
                pltpu.VMEM(col_row.shape, jnp.int32),
                pltpu.VMEM(ahead.shape, BF16),
                pltpu.SemaphoreType.DMA((3,)),
            ],
            far=True,
        )
    )

    def slab(values, again):
        given = values + (marks if again else [])
        return call(
            functools.partial(slab_kernel, devices, size, depth, again),
            [vmem((rows, cols))] * devices,
            [],
            [(value, True) for value in given] + [(pot, False)] + [(table, False) for table in tables],
            [
                pltpu.VMEM((GX * pad, 128), F32),
                pltpu.VMEM((GX * pad, 128), F32),
                pltpu.VMEM((GX * pad, 128), F32),
                pltpu.VMEM((pad * GX, 256), F32),
                pltpu.VMEM((pad * GX, 128), F32),
                pltpu.VMEM((2 * rows, 128 * packing(size)[1]), BF16),
                pltpu.VMEM((cols * devices, 128), BF16),
                pltpu.VMEM((cols * devices, 128), BF16),
            ],
        )

    held = pltpu.VMEM((3 * devices * rows, cols), BF16)
    planes = exchange(slab(marks, False))
    first, *sent = call(
        functools.partial(middle_kernel, devices, step, size),
        [vmem((2, size, cols))] + [vmem((rows, cols))] * devices,
        [me_arg, lower, upper],
        [(value, True) for value in planes] + [(psi_t, False), (col_row, False), (ahead, False), (back, False)],
        [held],
    )
    planes = exchange(slab(exchange(sent), True))
    filtered, packed = call(
        functools.partial(last_kernel, devices, bands, step, size),
        [vmem((2, size, cols)), vmem((bands, 2 * slots, cols), BF16)],
        [me_arg, lower, upper],
        [(value, True) for value in planes]
        + [(psi_t, False), (first, True), (col_row, False), (back, False), (pick, False)],
        [held],
    )
    (partial_sum,) = call(
        functools.partial(gram_kernel, bands),
        [vmem((devices * bands, 1, 128))],
        [],
        [(lax.all_to_all(packed, "band", 0, 0, tiled=True), True)],
        [pltpu.VMEM((cols // 128, bands * 2 * slots, 128), F32)],
    )
    sums = jnp.sum(lax.all_to_all(partial_sum, ("grid", "band"), 0, 0, tiled=True), axis=0)
    own = bands // devices
    sums = sums.reshape(2, 1, GY)
    gram = lax.dynamic_slice(sums, (0, 0, me * own), (2, 1, own)) / (4.0 * radius**3)
    return jnp.transpose(filtered, (0, 2, 1)).reshape(psi.shape), gram


def solution(mesh):
    return jax.shard_map(
        functools.partial(body, mesh.shape["grid"], mesh.shape["band"]),
        mesh=mesh,
        in_specs=(P(None, "band", "grid", None), P("grid"), P("grid", None), P(), P()),
        out_specs=(P(None, "band", "grid", None), P(None, "band", "grid")),
        check_vma=False,
    )
```

```python
import functools

import jax
import jax.numpy as jnp
import ml_dtypes
import numpy as np
from jax import lax
from jax.experimental import pallas as pl
from jax.experimental.pallas import tpu as pltpu
from jax.sharding import PartitionSpec as P

GY = 64
GX = 56
F32 = jnp.float32
BF16 = jnp.bfloat16
MIB = 1024 * 1024


def round_up(value, unit):
    return -(-value // unit) * unit


def halves(table):
    table = np.asarray(table, np.float32)
    high = table.astype(ml_dtypes.bfloat16)
    low = (table - high.astype(np.float32)).astype(ml_dtypes.bfloat16)
    return high, low


def stacked_table(table, axis):
    high, low = halves(table)
    return np.concatenate([high, high, low], axis=axis)


def folded(index, size):
    return np.where(index < size // 2, index, index - size)


def z_tables(size, devices, pad):
    depth = size // devices
    rows = 2 * pad
    freq = np.arange(size)
    ahead = np.zeros((devices, rows, 2 * size))
    back = np.zeros((2 * size, devices * rows))
    for d in range(devices):
        plane = d * depth + np.arange(depth)
        angle = 2 * np.pi * ((plane[:, None] * freq[None, :]) % size) / size
        c, s = np.cos(angle), np.sin(angle)
        ahead[d, :depth, :size], ahead[d, :depth, size:] = c, -s
        ahead[d, pad : pad + depth, :size], ahead[d, pad : pad + depth, size:] = s, c
        at = d * rows
        back[:size, at : at + depth], back[:size, at + pad : at + pad + depth] = c.T, s.T
        back[size:, at : at + depth], back[size:, at + pad : at + pad + depth] = -s.T, c.T
    return stacked_table(ahead, 2), stacked_table(back, 1)


def plane_tables(size):
    radius = size // 4
    count = 2 * radius + 1
    freq = np.arange(count) - radius
    angle = 2 * np.pi * ((freq[:, None] * np.arange(size)[None, :]) % size) / size
    c, s = np.cos(angle), np.sin(angle)
    ty = np.zeros((2 * GY, 256))
    ty[:count, :size], ty[:count, 128 : 128 + size] = c, s
    ty[GY : GY + count, :size], ty[GY : GY + count, 128 : 128 + size] = -s, c
    tyb = np.zeros((256, 2 * GY))
    tyb[:size, :count], tyb[:size, GY : GY + count] = c.T, -s.T
    tyb[128 : 128 + size, :count], tyb[128 : 128 + size, GY : GY + count] = s.T, c.T
    tx = np.zeros((2 * size, 2 * GX))
    tx[:size, :count], tx[:size, GX : GX + count] = c.T, -s.T
    tx[size:, :count], tx[size:, GX : GX + count] = s.T, c.T
    txb = np.zeros((2 * GX, 2 * size))
    txb[:count, :size], txb[:count, size:] = c, s
    txb[GX : GX + count, :size], txb[GX : GX + count, size:] = -s, c
    high, low = halves(tx)
    tx = np.concatenate([np.concatenate([high, high], 1), np.concatenate([low, 0 * low], 1)], 0)
    return stacked_table(ty, 0), tx, np.concatenate(halves(txb), 0), np.concatenate(halves(tyb), 1)


def packing(size):
    radius = size // 4
    widths = [int(np.sqrt(radius * radius - g * g)) for g in range(-radius, radius + 1)]
    slots, free = [None] * len(widths), []
    for i in sorted(range(len(widths)), key=lambda j: (-widths[j], j)):
        span = 2 * widths[i] + 1
        for s in range(len(free) + 1):
            if s == len(free):
                free.append(128)
            if free[s] >= span:
                slots[i] = (widths[i], s, 128 - free[s] + widths[i])
                free[s] -= span
                break
    return slots, round_up(len(free), 2)


def split(value):
    high = value.astype(BF16)
    low = (value - high.astype(F32)).astype(BF16)
    return high, low


def tripled(value, axis):
    high, low = split(value)
    return jnp.concatenate([high, low, high], axis=axis)


def dot(a, b, dims=((1,), (0,))):
    return lax.dot_general(a, b, (dims, ((), ())), preferred_element_type=F32)


SMEM = pl.BlockSpec(memory_space=pltpu.SMEM)
VMEM = pl.BlockSpec(memory_space=pltpu.VMEM)
HBM = pl.BlockSpec(memory_space=pltpu.HBM)


def call(kernel, out_shape, scalars, arrays, scratch=(), limit=24, far=False):
    space = pltpu.HBM if far else pltpu.VMEM
    arrays = [pltpu.with_memory_space_constraint(value, space) if keep else value for value, keep in arrays]
    return pl.pallas_call(
        kernel,
        out_shape=out_shape,
        in_specs=[SMEM] * len(scalars) + [HBM if far else VMEM] * len(arrays),
        out_specs=[VMEM] * len(out_shape),
        scratch_shapes=list(scratch),
        compiler_params=pltpu.CompilerParams(vmem_limit_bytes=limit * MIB),
    )(*scalars, *arrays)


def position(col_row, size):
    place = col_row.astype(F32)
    kx = jnp.floor((place + 0.5) * (1.0 / size))
    ky = place - kx * size
    half = float(size // 2)
    return jnp.where(kx < half, kx, kx - size), jnp.where(ky < half, ky, ky - size)


def sphere(col_row, size):
    cols = col_row.shape[1]
    radius = size // 4
    gx, gy = position(col_row, size)
    index = lax.broadcasted_iota(jnp.int32, (size, cols), 0)
    freq = jnp.where(index < size // 2, index, index - size).astype(F32)
    radius2 = (gx * gx + gy * gy) + freq * freq
    return radius2 <= float(radius * radius), radius2 * (2.0 / (radius * radius))


def to_planes(me, parts, table_ref, outs, step):
    value = tripled(jnp.concatenate(parts, axis=0), 0)
    table = jnp.concatenate([table_ref[step(me, k)] for k in range(len(outs))], axis=0)
    total = dot(table, value)
    rows = table_ref.shape[1]
    for k in range(len(outs)):
        outs[k][:rows] = total[k * rows : (k + 1) * rows]


def from_planes(me, planes, table_ref, held, step, size):
    rows = planes[0].shape[0]
    third = rows * len(planes)
    for k in range(len(planes)):
        high, low = split(planes[k][...])
        at = step(me, k) * rows
        for j, value in enumerate((high, low, high)):
            held[pl.ds(pl.multiple_of(j * third + at, 16), rows), :] = value
    total = dot(table_ref[...], held[...])
    return total[:size], total[size:]


def first_kernel(devices, step, size, me_ref, *refs):
    far, refs = refs[:3], refs[3:]
    outs, (psi_ref, col_ref, ahead_ref, sems) = refs[:devices], refs[devices:]
    copies = [pltpu.make_async_copy(far[i], refs[devices + i], sems.at[i]) for i in range(3)]
    for copy in copies:
        copy.start()
    for copy in copies:
        copy.wait()
    inside, _ = sphere(col_ref[...], size)
    parts = [jnp.where(inside, psi_ref[p], 0.0) for p in range(2)]
    to_planes(me_ref[0], parts, ahead_ref, outs, step)
    radius = size // 4
    gx, gy = position(col_ref[...], size)
    used = gx * gx + gy * gy <= float(radius * radius)
    rows = ahead_ref.shape[1]
    row = lax.broadcasted_iota(jnp.int32, (8, gx.shape[1]), 0)
    slot, lane = jnp.zeros(row.shape, F32), jnp.zeros(row.shape, F32)
    for i, (_, s, middle) in enumerate(packing(size)[0]):
        here = gx == float(i - radius)
        slot, lane = jnp.where(here, float(s), slot), jnp.where(here, float(middle), lane)
    place = jnp.where(used, jnp.where(row == 0, slot, lane + gy), -9.0)
    for k in range(devices):
        outs[k][rows:] = place


def middle_kernel(devices, step, size, me_ref, low_ref, up_ref, *refs):
    planes, refs = refs[:devices], refs[devices:]
    psi_ref, col_ref, ahead_ref, back_ref, first_ref = refs[:5]
    outs, held = refs[5 : 5 + devices], refs[5 + devices]
    center = (up_ref[0] + low_ref[0]) / 2.0
    half = (up_ref[0] - low_ref[0]) / 2.0
    inside, kinetic = sphere(col_ref[...], size)
    back = from_planes(me_ref[0], planes, back_ref, held, step, size)
    parts = []
    for p in range(2):
        value = jnp.where(inside, ((kinetic - center) * psi_ref[p] + back[p]) / half, 0.0)
        first_ref[p] = value
        parts.append(value)
    to_planes(me_ref[0], parts, ahead_ref, outs, step)


def last_kernel(devices, bands, step, size, me_ref, low_ref, up_ref, *refs):
    planes, refs = refs[:devices], refs[devices:]
    psi_ref, first_ref, col_ref, back_ref, pick_ref, filtered_ref, packed_ref, held = refs
    center = (up_ref[0] + low_ref[0]) / 2.0
    half = (up_ref[0] - low_ref[0]) / 2.0
    inside, kinetic = sphere(col_ref[...], size)
    back = from_planes(me_ref[0], planes, back_ref, held, step, size)
    total = None
    for p in range(2):
        value = 2.0 * ((kinetic - center) * first_ref[p] + back[p]) / half - psi_ref[p]
        value = jnp.where(inside, value, 0.0)
        filtered_ref[p] = value
        piece = dot(pick_ref[p], value.astype(BF16))
        total = piece if total is None else total + piece
    rows = packed_ref.shape[1]
    for k in range(bands):
        packed_ref[k] = total[k * rows : (k + 1) * rows].astype(BF16)


def gram_kernel(bands, parts_ref, sum_ref, held):
    rows, cols = parts_ref.shape[1:]
    blocks = cols // 128
    for k in range(bands):
        value = parts_ref[k].astype(F32)
        for j in range(blocks):
            held[j, k * rows : (k + 1) * rows, :] = value[:, 128 * j : 128 * j + 128]
    lines = [[held[j, pl.ds(r, bands, stride=rows), :] for j in range(blocks)] for r in range(rows)]
    real = jnp.concatenate([v for r in range(rows // 2) for v in lines[r]], axis=1)
    imag = jnp.concatenate([v for r in range(rows // 2, rows) for v in lines[r]], axis=1)
    left = jnp.concatenate([real, imag], axis=1).astype(BF16)
    right = jnp.concatenate([imag, -real], axis=1).astype(BF16)
    none = jnp.zeros((bands, GY - bands), F32)
    value = jnp.concatenate(
        [dot(left, left, ((1,), (1,))), none, dot(left, right, ((1,), (1,))), none], axis=1
    )
    for g in range(sum_ref.shape[0] // bands):
        sum_ref[g * bands : (g + 1) * bands, 0, :] = value


def scatter(plane_ref, mark_ref, slots):
    rows, cols = mark_ref.shape[0] - 8, mark_ref.shape[1]
    row = lax.broadcasted_iota(jnp.int32, (8, 256), 0)
    side = lax.broadcasted_iota(jnp.int32, (8, 256), 1) // 128
    spread = jnp.where(row == side, 1.0, 0.0).astype(BF16)
    both = dot(mark_ref[rows:].astype(BF16), spread, ((0,), (0,)))
    slot = both[:, :128].astype(BF16)
    along = lax.broadcasted_iota(jnp.int32, (cols, 128), 1).astype(F32)
    spot = jnp.where(both[:, 128:] == along, 1.0, 0.0).astype(BF16)
    lhs = jnp.concatenate(split(plane_ref[:rows]), axis=0)
    zero = jnp.zeros((), BF16)
    for t in range(0, slots, 2):
        hot = [jnp.where(slot == float(v), spot, zero) for v in (t, t + 1)]
        got = dot(lhs, jnp.concatenate(hot, axis=1))
        yield t, got[:rows] + got[rows:]


def gather(box, mark_ref, out_ref, slots):
    rows, cols = mark_ref.shape[0] - 8, mark_ref.shape[1]
    zero = jnp.zeros((), BF16)
    wide = min(256, cols)
    for at in range(0, cols, wide):
        slot = jnp.broadcast_to(mark_ref[rows : rows + 1, at : at + wide], (16, wide)).astype(BF16)
        spot = jnp.broadcast_to(mark_ref[rows + 1 : rows + 2, at : at + wide], (128, wide))
        down = lax.broadcasted_iota(jnp.int32, (128, wide), 0).astype(F32)
        hot = jnp.where(spot == down, 1.0, 0.0).astype(BF16)
        tall = []
        for v in range(slots):
            here = slot == float(v)
            tall += [jnp.where(here, hot[16 * i : 16 * i + 16], zero) for i in range(8)]
        got = dot(box, jnp.concatenate(tall, axis=0))
        out_ref[:, at : at + wide] = got[:rows] + got[rows:]


def scatter_kernel(slots, plane_ref, mark_ref, *refs):
    before, after = refs[:-1], refs[-1]
    for t, tile in scatter(plane_ref, mark_ref, slots):
        here = slice(128 * t, 128 * t + 256)
        after[:, here] = tile + before[0][:, here] if before else tile


def gather_kernel(slots, box_ref, mark_ref, out_ref):
    gather(box_ref[...], mark_ref, out_ref, slots)


def slab_kernel(devices, size, depth, plane_ref, before_ref, *refs):
    marks, refs = refs[: devices - 1], refs[devices - 1 :]
    pot_ref, ty_ref, tx_ref, txb_ref, tyb_ref = refs[:5]
    outs, box_ref = refs[5 : 4 + devices], refs[4 + devices]
    in_ref, y0_ref, y1_ref, back_ref, q_ref = refs[5 + devices :]
    pad = round_up(depth, 8)
    radius = size // 4
    places, slots = packing(size)
    lane = lax.broadcasted_iota(jnp.int32, (pad, 128), 1)

    def between(first, last):
        return (lane >= first) & (lane <= last)

    in_ref[...] = jnp.zeros(in_ref.shape, F32)
    for t, tile in scatter(plane_ref, marks[-1], slots):
        got = tile + before_ref[:, 128 * t : 128 * t + 256]
        for i, (width, slot, middle) in enumerate(places):
            if slot // 2 * 2 != t:
                continue
            at = 128 * (slot - t)
            re = pltpu.roll(got[:pad, at : at + 128], (radius - middle) % 128, 1)
            im = pltpu.roll(got[pad:, at : at + 128], (radius + GY - middle) % 128, 1)
            im = jnp.where(between(GY + radius - width, GY + radius + width), im, 0.0)
            in_ref[pl.ds(i, pad, stride=GX), :] = jnp.where(between(radius - width, radius + width), re, im)
    moved = dot(tripled(in_ref[...], 1), ty_ref[...])
    y0_ref[...] = moved[:, :128]
    y1_ref[...] = moved[:, 128:]
    if depth < pad:
        q_ref[depth * GX :] = jnp.zeros(((pad - depth) * GX, 128), F32)

    chunk, group = 8, 4
    for first in range(0, depth, chunk):
        last = min(depth, first + chunk)
        for z in range(first, last, group):
            near = range(z, min(z + group, last))
            sides = []
            for w in near:
                line = slice(w * GX, (w + 1) * GX)
                sides.append(jnp.concatenate([y0_ref[line, :], y1_ref[line, :]], axis=0))
            field = dot(tx_ref[...], jnp.concatenate(split(jnp.concatenate(sides, axis=1)), axis=0))
            pot = jnp.concatenate([pot_ref[w] for w in near], axis=1)
            field = (field[: 2 * size] + field[2 * size :]) * jnp.concatenate([pot, pot], axis=0)
            high, low = split(field)
            back = dot(txb_ref[...], high)
            back = back[: 2 * GX] + back[2 * GX :] + dot(txb_ref[: 2 * GX], low)
            for w in near:
                for p in range(2):
                    at = 128 * (w - z)
                    back_ref[w * GX : (w + 1) * GX, 128 * p : 128 * p + 128] = back[
                        p * GX : (p + 1) * GX, at : at + 128
                    ]
        part = slice(first * GX, last * GX)
        high, low = split(back_ref[part])
        moved = dot(high, tyb_ref[...])
        q_ref[part] = moved[:, :128] + moved[:, 128:] + dot(low, tyb_ref[:, :128])

    for s in range(slots):
        re, im = jnp.zeros((pad, 128), F32), jnp.zeros((pad, 128), F32)
        for i, (width, slot, middle) in enumerate(places):
            if slot != s:
                continue
            value = q_ref[pl.ds(i, pad, stride=GX), :]
            here = between(middle - width, middle + width)
            re = jnp.where(here, pltpu.roll(value, (middle - radius) % 128, 1), re)
            im = jnp.where(here, pltpu.roll(value, (middle - radius - GY) % 128, 1), im)
        box_ref[:, 128 * s : 128 * s + 128] = jnp.concatenate(split(jnp.concatenate([re, im], axis=0)), axis=0)

    box = box_ref[...]
    for k in range(devices - 1):
        gather(box, marks[k], outs[k], slots)


def body(devices, bands, psi, col_map, potential, lower, upper):
    cols, size = psi.shape[2], psi.shape[3]
    radius = size // 4
    depth = size // devices
    pad = round_up(depth, 8)
    rows = 2 * pad
    me = lax.axis_index("grid")
    me_arg = me.astype(jnp.int32).reshape(1)
    if devices & (devices - 1):
        raise ValueError("mesh size")

    def step(at, k):
        return at ^ k

    def exchange(values):
        return [values[0]] + [
            lax.ppermute(values[k], "grid", [(d, step(d, k)) for d in range(devices)]) for k in range(1, devices)
        ]

    ahead, back = z_tables(size, devices, pad)
    tables = plane_tables(size)
    count = 2 * radius + 1
    slots = round_up(-(-count // bands), 8)
    pick = np.zeros((2, bands * 2 * slots, size), ml_dtypes.bfloat16)
    for j in range(count):
        at = (j % bands) * 2 * slots + j // bands
        pick[0, at, (j - radius) % size] = 1
        pick[1, at + slots, (j - radius) % size] = 1

    pot = (potential * (1.0 / float(size**3))).reshape(depth, size, size)
    pot = jnp.pad(pot, ((0, 0), (0, 0), (0, 128 - size)))
    psi_t = jnp.transpose(psi.reshape(2, cols, size), (0, 2, 1))
    col_row = col_map.reshape(1, cols)

    def vmem(shape, dtype=F32):
        return pltpu.VMEM(shape, dtype)

    marks = exchange(
        call(
            functools.partial(first_kernel, devices, step, size),
            [vmem((rows + 8, cols))] * devices,
            [me_arg],
            [(psi_t, True), (col_row, True), (ahead, True)],
            [
                pltpu.VMEM(psi_t.shape, F32),
                pltpu.VMEM(col_row.shape, jnp.int32),
                pltpu.VMEM(ahead.shape, BF16),
                pltpu.SemaphoreType.DMA((3,)),
            ],
            far=True,
        )
    )

    slots_all = packing(size)[1]
    box_shape = (rows, 128 * slots_all)

    def slab(values):
        sums = []
        for k in range(devices - 1):
            sums = call(
                functools.partial(scatter_kernel, slots_all),
                [vmem(box_shape)],
                [],
                [(value, True) for value in [values[k], marks[k]] + list(sums)],
            )
        given = [values[-1], sums[0]] + marks[1:]
        *sent, box = call(
            functools.partial(slab_kernel, devices, size, depth),
            [vmem((rows, cols))] * (devices - 1) + [vmem((2 * rows, 128 * slots_all), BF16)],
            [],
            [(value, True) for value in given] + [(pot, False)] + [(table, False) for table in tables],
            [
                pltpu.VMEM((GX * pad, 128), F32),
                pltpu.VMEM((GX * pad, 128), F32),
                pltpu.VMEM((GX * pad, 128), F32),
                pltpu.VMEM((pad * GX, 256), F32),
                pltpu.VMEM((pad * GX, 128), F32),
            ],
        )
        own = call(
            functools.partial(gather_kernel, slots_all),
            [vmem((rows, cols))],
            [],
            [(box, True), (marks[0], True)],
        )
        return list(own) + list(sent)

    held = pltpu.VMEM((3 * devices * rows, cols), BF16)
    planes = exchange(slab(marks))
    first, *sent = call(
        functools.partial(middle_kernel, devices, step, size),
        [vmem((2, size, cols))] + [vmem((rows, cols))] * devices,
        [me_arg, lower, upper],
        [(value, True) for value in planes] + [(psi_t, False), (col_row, False), (ahead, False), (back, False)],
        [held],
    )
    planes = exchange(slab(exchange(sent)))
    filtered, packed = call(
        functools.partial(last_kernel, devices, bands, step, size),
        [vmem((2, size, cols)), vmem((bands, 2 * slots, cols), BF16)],
        [me_arg, lower, upper],
        [(value, True) for value in planes]
        + [(psi_t, False), (first, True), (col_row, False), (back, False), (pick, False)],
        [held],
    )
    (partial_sum,) = call(
        functools.partial(gram_kernel, bands),
        [vmem((devices * bands, 1, 128))],
        [],
        [(lax.all_to_all(packed, "band", 0, 0, tiled=True), True)],
        [pltpu.VMEM((cols // 128, bands * 2 * slots, 128), F32)],
    )
    sums = jnp.sum(lax.all_to_all(partial_sum, ("grid", "band"), 0, 0, tiled=True), axis=0)
    own = bands // devices
    sums = sums.reshape(2, 1, GY)
    gram = lax.dynamic_slice(sums, (0, 0, me * own), (2, 1, own)) / (4.0 * radius**3)
    return jnp.transpose(filtered, (0, 2, 1)).reshape(psi.shape), gram


def solution(mesh):
    return jax.shard_map(
        functools.partial(body, mesh.shape["grid"], mesh.shape["band"]),
        mesh=mesh,
        in_specs=(P(None, "band", "grid", None), P("grid"), P("grid", None), P(), P()),
        out_specs=(P(None, "band", "grid", None), P(None, "band", "grid")),
        check_vma=False,
    )
```

```python
import functools

import jax
import jax.numpy as jnp
import ml_dtypes
import numpy as np
from jax import lax
from jax.experimental import pallas as pl
from jax.experimental.pallas import tpu as pltpu
from jax.sharding import PartitionSpec as P

GY = 64
GX = 56
F32 = jnp.float32
BF16 = jnp.bfloat16
MIB = 1024 * 1024


def round_up(value, unit):
    return -(-value // unit) * unit


def halves(table):
    table = np.asarray(table, np.float32)
    high = table.astype(ml_dtypes.bfloat16)
    low = (table - high.astype(np.float32)).astype(ml_dtypes.bfloat16)
    return high, low


def stacked_table(table, axis):
    high, low = halves(table)
    return np.concatenate([high, high, low], axis=axis)


def folded(index, size):
    return np.where(index < size // 2, index, index - size)


def kept(size):
    radius = size // 4
    return round_up(radius + 1, 8), radius


def z_tables(size, devices, pad):
    depth = size // devices
    rows = 2 * pad
    first, last = kept(size)
    count = first + last
    freq = np.concatenate([np.arange(first), np.arange(size - last, size)])
    ahead = np.zeros((devices, rows, 2 * count))
    back = np.zeros((2 * count, devices * rows))
    for d in range(devices):
        plane = d * depth + np.arange(depth)
        angle = 2 * np.pi * ((plane[:, None] * freq[None, :]) % size) / size
        c, s = np.cos(angle), np.sin(angle)
        ahead[d, :depth, :count], ahead[d, :depth, count:] = c, -s
        ahead[d, pad : pad + depth, :count], ahead[d, pad : pad + depth, count:] = s, c
        at = d * rows
        back[:count, at : at + depth], back[:count, at + pad : at + pad + depth] = c.T, s.T
        back[count:, at : at + depth], back[count:, at + pad : at + pad + depth] = -s.T, c.T
    return stacked_table(ahead, 2), stacked_table(back, 1)


def plane_tables(size):
    radius = size // 4
    count = 2 * radius + 1
    freq = np.arange(count) - radius
    angle = 2 * np.pi * ((freq[:, None] * np.arange(size)[None, :]) % size) / size
    c, s = np.cos(angle), np.sin(angle)
    ty = np.zeros((2 * GY, 256))
    ty[:count, :size], ty[:count, 128 : 128 + size] = c, s
    ty[GY : GY + count, :size], ty[GY : GY + count, 128 : 128 + size] = -s, c
    tyb = np.zeros((256, 2 * GY))
    tyb[:size, :count], tyb[:size, GY : GY + count] = c.T, -s.T
    tyb[128 : 128 + size, :count], tyb[128 : 128 + size, GY : GY + count] = s.T, c.T
    tx = np.zeros((2 * size, 2 * GX))
    tx[:size, :count], tx[:size, GX : GX + count] = c.T, -s.T
    tx[size:, :count], tx[size:, GX : GX + count] = s.T, c.T
    txb = np.zeros((2 * GX, 2 * size))
    txb[:count, :size], txb[:count, size:] = c, s
    txb[GX : GX + count, :size], txb[GX : GX + count, size:] = -s, c
    high, low = halves(tx)
    tx = np.concatenate([np.concatenate([high, high], 1), np.concatenate([low, 0 * low], 1)], 0)
    return stacked_table(ty, 0), tx, np.concatenate(halves(txb), 0), np.concatenate(halves(tyb), 1)


def packing(size):
    radius = size // 4
    widths = [int(np.sqrt(radius * radius - g * g)) for g in range(-radius, radius + 1)]
    slots, free = [None] * len(widths), []
    for i in sorted(range(len(widths)), key=lambda j: (-widths[j], j)):
        span = 2 * widths[i] + 1
        for s in range(len(free) + 1):
            if s == len(free):
                free.append(128)
            if free[s] >= span:
                slots[i] = (widths[i], s, 128 - free[s] + widths[i])
                free[s] -= span
                break
    return slots, round_up(len(free), 2)


def split(value):
    high = value.astype(BF16)
    low = (value - high.astype(F32)).astype(BF16)
    return high, low


def tripled(value, axis):
    high, low = split(value)
    return jnp.concatenate([high, low, high], axis=axis)


def dot(a, b, dims=((1,), (0,))):
    return lax.dot_general(a, b, (dims, ((), ())), preferred_element_type=F32)


SMEM = pl.BlockSpec(memory_space=pltpu.SMEM)
VMEM = pl.BlockSpec(memory_space=pltpu.VMEM)
HBM = pl.BlockSpec(memory_space=pltpu.HBM)


def call(kernel, out_shape, scalars, arrays, scratch=(), limit=24, far=False):
    space = pltpu.HBM if far else pltpu.VMEM
    arrays = [pltpu.with_memory_space_constraint(value, space) if keep else value for value, keep in arrays]
    return pl.pallas_call(
        kernel,
        out_shape=out_shape,
        in_specs=[SMEM] * len(scalars) + [HBM if far else VMEM] * len(arrays),
        out_specs=[VMEM] * len(out_shape),
        scratch_shapes=list(scratch),
        compiler_params=pltpu.CompilerParams(vmem_limit_bytes=limit * MIB),
    )(*scalars, *arrays)


def position(col_row, size):
    place = col_row.astype(F32)
    kx = jnp.floor((place + 0.5) * (1.0 / size))
    ky = place - kx * size
    half = float(size // 2)
    return jnp.where(kx < half, kx, kx - size), jnp.where(ky < half, ky, ky - size)


def sphere(col_row, size):
    cols = col_row.shape[1]
    radius = size // 4
    gx, gy = position(col_row, size)
    first, last = kept(size)
    index = lax.broadcasted_iota(jnp.int32, (first + last, cols), 0)
    freq = jnp.where(index < first, index, index - (first + last)).astype(F32)
    radius2 = (gx * gx + gy * gy) + freq * freq
    return radius2 <= float(radius * radius), radius2 * (2.0 / (radius * radius))


def kept_rows(ref, p, size):
    first, last = kept(size)
    return jnp.concatenate([ref[p, :first], ref[p, size - last :]], axis=0)


def to_planes(me, parts, table_ref, outs, step):
    value = tripled(jnp.concatenate(parts, axis=0), 0)
    table = jnp.concatenate([table_ref[step(me, k)] for k in range(len(outs))], axis=0)
    total = dot(table, value)
    rows = table_ref.shape[1]
    for k in range(len(outs)):
        outs[k][:rows] = total[k * rows : (k + 1) * rows]


def from_planes(me, planes, table_ref, held, step, size):
    rows = planes[0].shape[0]
    third = rows * len(planes)
    for k in range(len(planes)):
        high, low = split(planes[k][...])
        at = step(me, k) * rows
        for j, value in enumerate((high, low, high)):
            held[pl.ds(pl.multiple_of(j * third + at, 16), rows), :] = value
    total = dot(table_ref[...], held[...])
    return total[: sum(kept(size))], total[sum(kept(size)) :]


def first_kernel(devices, step, size, me_ref, *refs):
    far, refs = refs[:3], refs[3:]
    outs, (psi_ref, col_ref, ahead_ref, sems) = refs[:devices], refs[devices:]
    first, last = kept(size)
    pairs = [(far[1], col_ref), (far[2], ahead_ref)]
    for p in range(2):
        pairs.append((far[0].at[p, :first], psi_ref.at[p, :first]))
        pairs.append((far[0].at[p, size - last :], psi_ref.at[p, first:]))
    copies = [pltpu.make_async_copy(source, target, sems.at[i]) for i, (source, target) in enumerate(pairs)]
    for copy in copies:
        copy.start()
    for copy in copies:
        copy.wait()
    inside, _ = sphere(col_ref[...], size)
    parts = [jnp.where(inside, psi_ref[p], 0.0) for p in range(2)]
    to_planes(me_ref[0], parts, ahead_ref, outs, step)
    radius = size // 4
    gx, gy = position(col_ref[...], size)
    used = gx * gx + gy * gy <= float(radius * radius)
    rows = ahead_ref.shape[1]
    row = lax.broadcasted_iota(jnp.int32, (8, gx.shape[1]), 0)
    slot, lane = jnp.zeros(row.shape, F32), jnp.zeros(row.shape, F32)
    for i, (_, s, middle) in enumerate(packing(size)[0]):
        here = gx == float(i - radius)
        slot, lane = jnp.where(here, float(s), slot), jnp.where(here, float(middle), lane)
    place = jnp.where(used, jnp.where(row == 0, slot, lane + gy), -9.0)
    for k in range(devices):
        outs[k][rows:] = place


def middle_kernel(devices, step, size, me_ref, low_ref, up_ref, *refs):
    planes, refs = refs[:devices], refs[devices:]
    psi_ref, col_ref, ahead_ref, back_ref, first_ref = refs[:5]
    outs, held = refs[5 : 5 + devices], refs[5 + devices]
    center = (up_ref[0] + low_ref[0]) / 2.0
    half = (up_ref[0] - low_ref[0]) / 2.0
    inside, kinetic = sphere(col_ref[...], size)
    back = from_planes(me_ref[0], planes, back_ref, held, step, size)
    parts = []
    for p in range(2):
        value = jnp.where(inside, ((kinetic - center) * kept_rows(psi_ref, p, size) + back[p]) / half, 0.0)
        first_ref[p] = value
        parts.append(value)
    to_planes(me_ref[0], parts, ahead_ref, outs, step)


def last_kernel(devices, bands, step, size, me_ref, low_ref, up_ref, *refs):
    planes, refs = refs[:devices], refs[devices:]
    psi_ref, first_ref, col_ref, back_ref, pick_ref, filtered_ref, packed_ref, held = refs
    center = (up_ref[0] + low_ref[0]) / 2.0
    half = (up_ref[0] - low_ref[0]) / 2.0
    inside, kinetic = sphere(col_ref[...], size)
    back = from_planes(me_ref[0], planes, back_ref, held, step, size)
    first, last = kept(size)
    total = None
    for p in range(2):
        value = 2.0 * ((kinetic - center) * first_ref[p] + back[p]) / half - kept_rows(psi_ref, p, size)
        value = jnp.where(inside, value, 0.0)
        filtered_ref[p, :first] = value[:first]
        filtered_ref[p, first : size - last] = jnp.zeros((size - last - first, value.shape[1]), F32)
        filtered_ref[p, size - last :] = value[first:]
        piece = dot(pick_ref[p], value.astype(BF16))
        total = piece if total is None else total + piece
    rows = packed_ref.shape[1]
    for k in range(bands):
        packed_ref[k] = total[k * rows : (k + 1) * rows].astype(BF16)


def gram_kernel(bands, parts_ref, sum_ref):
    rows, cols = parts_ref.shape[1:]
    count = bands * rows
    stacked = parts_ref[...].reshape(count, cols)
    product = dot(stacked, stacked, ((1,), (1,)))
    down = lax.broadcasted_iota(jnp.int32, (count, count), 0) % rows
    along = lax.broadcasted_iota(jnp.int32, (count, count), 1) % rows
    real = jnp.where(down == along, product, 0.0)
    imag = jnp.where(along == down + rows // 2, product, jnp.where(down == along + rows // 2, -product, 0.0))
    place = lax.broadcasted_iota(jnp.int32, (count, 128), 0) // rows
    spot = lax.broadcasted_iota(jnp.int32, (count, 128), 1)
    pieces, places = [], []
    for p, value in enumerate((real, imag)):
        value = jnp.sum(value.reshape(bands, rows, count), axis=1)
        hot = jnp.where(place + p * GY == spot, 1.0, 0.0).astype(BF16)
        for _ in range(3):
            pieces.append(value.astype(BF16))
            value = value - pieces[-1].astype(F32)
            places.append(hot)
    value = dot(jnp.concatenate(pieces, axis=1), jnp.concatenate(places, axis=0))
    for g in range(sum_ref.shape[0] // bands):
        sum_ref[g * bands : (g + 1) * bands, 0, :] = value


def total_kernel(own, scale, me_ref, parts_ref, out_ref):
    value = jnp.sum(parts_ref[...], axis=0) * scale
    value = pltpu.roll(value, lax.rem(128 - me_ref[0] * own, 128), 1)
    out_ref[0] = value[:, :own]
    out_ref[1] = value[:, GY : GY + own]


def scatter(plane_ref, mark_ref, slots):
    rows, cols = mark_ref.shape[0] - 8, mark_ref.shape[1]
    row = lax.broadcasted_iota(jnp.int32, (8, 256), 0)
    side = lax.broadcasted_iota(jnp.int32, (8, 256), 1) // 128
    spread = jnp.where(row == side, 1.0, 0.0).astype(BF16)
    both = dot(mark_ref[rows:].astype(BF16), spread, ((0,), (0,)))
    slot = both[:, :128].astype(BF16)
    along = lax.broadcasted_iota(jnp.int32, (cols, 128), 1).astype(F32)
    spot = jnp.where(both[:, 128:] == along, 1.0, 0.0).astype(BF16)
    lhs = jnp.concatenate(split(plane_ref[:rows]), axis=0)
    zero = jnp.zeros((), BF16)
    for t in range(0, slots, 2):
        hot = [jnp.where(slot == float(v), spot, zero) for v in (t, t + 1)]
        got = dot(lhs, jnp.concatenate(hot, axis=1))
        yield t, got[:rows] + got[rows:]


def gather(box, mark_ref, out_ref, slots):
    rows, cols = mark_ref.shape[0] - 8, mark_ref.shape[1]
    zero = jnp.zeros((), BF16)
    wide = min(256, cols)
    for at in range(0, cols, wide):
        slot = jnp.broadcast_to(mark_ref[rows : rows + 1, at : at + wide], (16, wide)).astype(BF16)
        spot = jnp.broadcast_to(mark_ref[rows + 1 : rows + 2, at : at + wide], (128, wide))
        down = lax.broadcasted_iota(jnp.int32, (128, wide), 0).astype(F32)
        hot = jnp.where(spot == down, 1.0, 0.0).astype(BF16)
        tall = []
        for v in range(slots):
            here = slot == float(v)
            tall += [jnp.where(here, hot[16 * i : 16 * i + 16], zero) for i in range(8)]
        got = dot(box, jnp.concatenate(tall, axis=0))
        out_ref[:, at : at + wide] = got[:rows] + got[rows:]


def scatter_kernel(slots, plane_ref, mark_ref, *refs):
    before, after = refs[:-1], refs[-1]
    for t, tile in scatter(plane_ref, mark_ref, slots):
        here = slice(128 * t, 128 * t + 256)
        after[:, here] = tile + before[0][:, here] if before else tile


def gather_kernel(slots, box_ref, mark_ref, out_ref):
    gather(box_ref[...], mark_ref, out_ref, slots)


def slab_kernel(devices, size, depth, plane_ref, before_ref, *refs):
    marks, refs = refs[: devices - 1], refs[devices - 1 :]
    pot_ref, ty_ref, tx_ref, txb_ref, tyb_ref = refs[:5]
    outs, box_ref = refs[5 : 4 + devices], refs[4 + devices]
    in_ref, y0_ref, y1_ref, back_ref, q_ref = refs[5 + devices :]
    pad = round_up(depth, 8)
    radius = size // 4
    places, slots = packing(size)
    lane = lax.broadcasted_iota(jnp.int32, (pad, 128), 1)

    def between(first, last):
        return (lane >= first) & (lane <= last)

    in_ref[...] = jnp.zeros(in_ref.shape, F32)
    for t, tile in scatter(plane_ref, marks[-1], slots):
        got = tile + before_ref[:, 128 * t : 128 * t + 256]
        for i, (width, slot, middle) in enumerate(places):
            if slot // 2 * 2 != t:
                continue
            at = 128 * (slot - t)
            re = pltpu.roll(got[:pad, at : at + 128], (radius - middle) % 128, 1)
            im = pltpu.roll(got[pad:, at : at + 128], (radius + GY - middle) % 128, 1)
            im = jnp.where(between(GY + radius - width, GY + radius + width), im, 0.0)
            in_ref[pl.ds(i, pad, stride=GX), :] = jnp.where(between(radius - width, radius + width), re, im)
    moved = dot(tripled(in_ref[...], 1), ty_ref[...])
    y0_ref[...] = moved[:, :128]
    y1_ref[...] = moved[:, 128:]
    if depth < pad:
        q_ref[depth * GX :] = jnp.zeros(((pad - depth) * GX, 128), F32)

    chunk, group = 8, 4
    for first in range(0, depth, chunk):
        last = min(depth, first + chunk)
        for z in range(first, last, group):
            near = range(z, min(z + group, last))
            sides = []
            for w in near:
                line = slice(w * GX, (w + 1) * GX)
                sides.append(jnp.concatenate([y0_ref[line, :], y1_ref[line, :]], axis=0))
            field = dot(tx_ref[...], jnp.concatenate(split(jnp.concatenate(sides, axis=1)), axis=0))
            pot = jnp.concatenate([pot_ref[w] for w in near], axis=1)
            field = (field[: 2 * size] + field[2 * size :]) * jnp.concatenate([pot, pot], axis=0)
            high, low = split(field)
            back = dot(txb_ref[...], high)
            back = back[: 2 * GX] + back[2 * GX :] + dot(txb_ref[: 2 * GX], low)
            for w in near:
                for p in range(2):
                    at = 128 * (w - z)
                    back_ref[w * GX : (w + 1) * GX, 128 * p : 128 * p + 128] = back[
                        p * GX : (p + 1) * GX, at : at + 128
                    ]
        part = slice(first * GX, last * GX)
        high, low = split(back_ref[part])
        moved = dot(high, tyb_ref[...])
        q_ref[part] = moved[:, :128] + moved[:, 128:] + dot(low, tyb_ref[:, :128])

    for s in range(slots):
        re, im = jnp.zeros((pad, 128), F32), jnp.zeros((pad, 128), F32)
        for i, (width, slot, middle) in enumerate(places):
            if slot != s:
                continue
            value = q_ref[pl.ds(i, pad, stride=GX), :]
            here = between(middle - width, middle + width)
            re = jnp.where(here, pltpu.roll(value, (middle - radius) % 128, 1), re)
            im = jnp.where(here, pltpu.roll(value, (middle - radius - GY) % 128, 1), im)
        box_ref[:, 128 * s : 128 * s + 128] = jnp.concatenate(split(jnp.concatenate([re, im], axis=0)), axis=0)

    box = box_ref[...]
    for k in range(devices - 1):
        gather(box, marks[k], outs[k], slots)


def body(devices, bands, psi, col_map, potential, lower, upper):
    cols, size = psi.shape[2], psi.shape[3]
    radius = size // 4
    depth = size // devices
    pad = round_up(depth, 8)
    rows = 2 * pad
    me = lax.axis_index("grid")
    me_arg = me.astype(jnp.int32).reshape(1)
    if devices & (devices - 1):
        raise ValueError("mesh size")

    def step(at, k):
        return at ^ k

    def exchange(values):
        return [values[0]] + [
            lax.ppermute(values[k], "grid", [(d, step(d, k)) for d in range(devices)]) for k in range(1, devices)
        ]

    ahead, back = z_tables(size, devices, pad)
    tables = plane_tables(size)
    count = 2 * radius + 1
    slots = round_up(-(-count // bands), 8)
    pick = np.zeros((2, bands * 2 * slots, sum(kept(size))), ml_dtypes.bfloat16)
    for j in range(count):
        at = (j % bands) * 2 * slots + j // bands
        pick[0, at, (j - radius) % sum(kept(size))] = 1
        pick[1, at + slots, (j - radius) % sum(kept(size))] = 1

    pot = (potential * (1.0 / float(size**3))).reshape(depth, size, size)
    pot = jnp.pad(pot, ((0, 0), (0, 0), (0, 128 - size)))
    psi_t = jnp.transpose(psi.reshape(2, cols, size), (0, 2, 1))
    col_row = col_map.reshape(1, cols)

    def vmem(shape, dtype=F32):
        return pltpu.VMEM(shape, dtype)

    marks = exchange(
        call(
            functools.partial(first_kernel, devices, step, size),
            [vmem((rows + 8, cols))] * devices,
            [me_arg],
            [(psi_t, True), (col_row, True), (ahead, True)],
            [
                pltpu.VMEM((2, sum(kept(size)), cols), F32),
                pltpu.VMEM(col_row.shape, jnp.int32),
                pltpu.VMEM(ahead.shape, BF16),
                pltpu.SemaphoreType.DMA((6,)),
            ],
            far=True,
        )
    )

    slots_all = packing(size)[1]
    box_shape = (rows, 128 * slots_all)

    def slab(values):
        sums = []
        for k in range(devices - 1):
            sums = call(
                functools.partial(scatter_kernel, slots_all),
                [vmem(box_shape)],
                [],
                [(value, True) for value in [values[k], marks[k]] + list(sums)],
            )
        given = [values[-1], sums[0]] + marks[1:]
        *sent, box = call(
            functools.partial(slab_kernel, devices, size, depth),
            [vmem((rows, cols))] * (devices - 1) + [vmem((2 * rows, 128 * slots_all), BF16)],
            [],
            [(value, True) for value in given] + [(pot, False)] + [(table, False) for table in tables],
            [
                pltpu.VMEM((GX * pad, 128), F32),
                pltpu.VMEM((GX * pad, 128), F32),
                pltpu.VMEM((GX * pad, 128), F32),
                pltpu.VMEM((pad * GX, 256), F32),
                pltpu.VMEM((pad * GX, 128), F32),
            ],
        )
        own = call(
            functools.partial(gather_kernel, slots_all),
            [vmem((rows, cols))],
            [],
            [(box, True), (marks[0], True)],
        )
        return list(own) + list(sent)

    held = pltpu.VMEM((3 * devices * rows, cols), BF16)
    planes = exchange(slab(marks))
    first, *sent = call(
        functools.partial(middle_kernel, devices, step, size),
        [vmem((2, sum(kept(size)), cols))] + [vmem((rows, cols))] * devices,
        [me_arg, lower, upper],
        [(value, True) for value in planes] + [(psi_t, False), (col_row, False), (ahead, False), (back, False)],
        [held],
    )
    planes = exchange(slab(exchange(sent)))
    filtered, packed = call(
        functools.partial(last_kernel, devices, bands, step, size),
        [vmem((2, size, cols)), vmem((bands, 2 * slots, cols), BF16)],
        [me_arg, lower, upper],
        [(value, True) for value in planes]
        + [(psi_t, False), (first, True), (col_row, False), (back, False), (pick, False)],
        [held],
    )
    (partial_sum,) = call(
        functools.partial(gram_kernel, bands),
        [vmem((devices * bands, 1, 128))],
        [],
        [(lax.all_to_all(packed, "band", 0, 0, tiled=True), True)],
    )
    own = bands // devices
    (gram,) = call(
        functools.partial(total_kernel, own, 1.0 / (4.0 * radius**3)),
        [jax.ShapeDtypeStruct((2, 1, own), F32)],
        [me_arg],
        [(lax.all_to_all(partial_sum, ("grid", "band"), 0, 0, tiled=True), True)],
    )
    return jnp.transpose(filtered, (0, 2, 1)).reshape(psi.shape), gram


def solution(mesh):
    return jax.shard_map(
        functools.partial(body, mesh.shape["grid"], mesh.shape["band"]),
        mesh=mesh,
        in_specs=(P(None, "band", "grid", None), P("grid"), P("grid", None), P(), P()),
        out_specs=(P(None, "band", "grid", None), P(None, "band", "grid")),
        check_vma=False,
    )
```

```python
import functools

import jax
import jax.numpy as jnp
import ml_dtypes
import numpy as np
from jax import lax
from jax.experimental import pallas as pl
from jax.experimental.pallas import tpu as pltpu
from jax.sharding import PartitionSpec as P

GY = 64
GX = 56
F32 = jnp.float32
BF16 = jnp.bfloat16
MIB = 1024 * 1024


def round_up(value, unit):
    return -(-value // unit) * unit


def halves(table):
    table = np.asarray(table, np.float32)
    high = table.astype(ml_dtypes.bfloat16)
    low = (table - high.astype(np.float32)).astype(ml_dtypes.bfloat16)
    return high, low


def stacked_table(table, axis):
    high, low = halves(table)
    return np.concatenate([high, high, low], axis=axis)


def folded(index, size):
    return np.where(index < size // 2, index, index - size)


def kept(size):
    radius = size // 4
    return round_up(radius + 1, 8), radius


def z_tables(size, devices, pad):
    depth = size // devices
    rows = 2 * pad
    first, last = kept(size)
    count = first + last
    freq = np.concatenate([np.arange(first), np.arange(size - last, size)])
    ahead = np.zeros((devices, rows, 2 * count))
    back = np.zeros((2 * count, devices * rows))
    for d in range(devices):
        plane = d * depth + np.arange(depth)
        angle = 2 * np.pi * ((plane[:, None] * freq[None, :]) % size) / size
        c, s = np.cos(angle), np.sin(angle)
        ahead[d, :depth, :count], ahead[d, :depth, count:] = c, -s
        ahead[d, pad : pad + depth, :count], ahead[d, pad : pad + depth, count:] = s, c
        at = d * rows
        back[:count, at : at + depth], back[:count, at + pad : at + pad + depth] = c.T, s.T
        back[count:, at : at + depth], back[count:, at + pad : at + pad + depth] = -s.T, c.T
    return stacked_table(ahead, 2), stacked_table(back, 1)


def plane_tables(size):
    radius = size // 4
    count = 2 * radius + 1
    freq = np.arange(count) - radius
    angle = 2 * np.pi * ((freq[:, None] * np.arange(size)[None, :]) % size) / size
    c, s = np.cos(angle), np.sin(angle)
    ty = np.zeros((2 * GY, 256))
    ty[:count, :size], ty[:count, 128 : 128 + size] = c, s
    ty[GY : GY + count, :size], ty[GY : GY + count, 128 : 128 + size] = -s, c
    tyb = np.zeros((256, 2 * GY))
    tyb[:size, :count], tyb[:size, GY : GY + count] = c.T, -s.T
    tyb[128 : 128 + size, :count], tyb[128 : 128 + size, GY : GY + count] = s.T, c.T
    tx = np.zeros((2 * size, 2 * GX))
    tx[:size, :count], tx[:size, GX : GX + count] = c.T, -s.T
    tx[size:, :count], tx[size:, GX : GX + count] = s.T, c.T
    txb = np.zeros((2 * GX, 2 * size))
    txb[:count, :size], txb[:count, size:] = c, s
    txb[GX : GX + count, :size], txb[GX : GX + count, size:] = -s, c
    high, low = halves(tx)
    tx = np.concatenate([np.concatenate([high, high], 1), np.concatenate([low, 0 * low], 1)], 0)
    return stacked_table(ty, 0), tx, np.concatenate(halves(txb), 0), np.concatenate(halves(tyb), 1)


def packing(size):
    radius = size // 4
    widths = [int(np.sqrt(radius * radius - g * g)) for g in range(-radius, radius + 1)]
    slots, free = [None] * len(widths), []
    for i in sorted(range(len(widths)), key=lambda j: (-widths[j], j)):
        span = 2 * widths[i] + 1
        for s in range(len(free) + 1):
            if s == len(free):
                free.append(128)
            if free[s] >= span:
                slots[i] = (widths[i], s, 128 - free[s] + widths[i])
                free[s] -= span
                break
    return slots, round_up(len(free), 2)


def split(value):
    high = value.astype(BF16)
    low = (value - high.astype(F32)).astype(BF16)
    return high, low


def tripled(value, axis):
    high, low = split(value)
    return jnp.concatenate([high, low, high], axis=axis)


def dot(a, b, dims=((1,), (0,))):
    return lax.dot_general(a, b, (dims, ((), ())), preferred_element_type=F32)


SMEM = pl.BlockSpec(memory_space=pltpu.SMEM)
VMEM = pl.BlockSpec(memory_space=pltpu.VMEM)
HBM = pl.BlockSpec(memory_space=pltpu.HBM)


def call(kernel, out_shape, scalars, arrays, scratch=(), limit=24, far=False):
    space = pltpu.HBM if far else pltpu.VMEM
    arrays = [pltpu.with_memory_space_constraint(value, space) if keep else value for value, keep in arrays]
    return pl.pallas_call(
        kernel,
        out_shape=out_shape,
        in_specs=[SMEM] * len(scalars) + [HBM if far else VMEM] * len(arrays),
        out_specs=[VMEM] * len(out_shape),
        scratch_shapes=list(scratch),
        compiler_params=pltpu.CompilerParams(vmem_limit_bytes=limit * MIB),
    )(*scalars, *arrays)


def position(col_row, size):
    place = col_row.astype(F32)
    kx = jnp.floor((place + 0.5) * (1.0 / size))
    ky = place - kx * size
    half = float(size // 2)
    return jnp.where(kx < half, kx, kx - size), jnp.where(ky < half, ky, ky - size)


def sphere(col_row, size):
    cols = col_row.shape[1]
    radius = size // 4
    gx, gy = position(col_row, size)
    first, last = kept(size)
    index = lax.broadcasted_iota(jnp.int32, (first + last, cols), 0)
    freq = jnp.where(index < first, index, index - (first + last)).astype(F32)
    radius2 = (gx * gx + gy * gy) + freq * freq
    return radius2 <= float(radius * radius), radius2 * (2.0 / (radius * radius))


def kept_rows(ref, p, size):
    first, last = kept(size)
    return jnp.concatenate([ref[p, :first], ref[p, size - last :]], axis=0)


def swapped(k, devices):
    bits = devices.bit_length() - 1
    if bits % 2:
        return k
    half = bits // 2
    return (k >> half) | ((k & ((1 << half) - 1)) << half)


def peers_of(devices, me_ref, odd_ref):
    return [me_ref[0] ^ (k + odd_ref[0] * (swapped(k, devices) - k)) for k in range(devices)]


def to_planes(peers, parts, table_ref, outs):
    value = tripled(jnp.concatenate(parts, axis=0), 0)
    table = jnp.concatenate([table_ref[peers[k]] for k in range(len(outs))], axis=0)
    total = dot(table, value)
    rows = table_ref.shape[1]
    for k in range(len(outs)):
        outs[k][:rows] = total[k * rows : (k + 1) * rows]


def from_planes(peers, planes, table_ref, held, size):
    rows = planes[0].shape[0]
    third = rows * len(planes)
    for k in range(len(planes)):
        high, low = split(planes[k][...])
        at = peers[k] * rows
        for j, value in enumerate((high, low, high)):
            held[pl.ds(pl.multiple_of(j * third + at, 16), rows), :] = value
    total = dot(table_ref[...], held[...])
    return total[: sum(kept(size))], total[sum(kept(size)) :]


def first_kernel(devices, size, me_ref, odd_ref, *refs):
    far, refs = refs[:3], refs[3:]
    outs, (psi_ref, col_ref, ahead_ref, sems) = refs[:devices], refs[devices:]
    first, last = kept(size)
    pairs = [(far[1], col_ref), (far[2], ahead_ref)]
    for p in range(2):
        pairs.append((far[0].at[p, :first], psi_ref.at[p, :first]))
        pairs.append((far[0].at[p, size - last :], psi_ref.at[p, first:]))
    copies = [pltpu.make_async_copy(source, target, sems.at[i]) for i, (source, target) in enumerate(pairs)]
    for copy in copies:
        copy.start()
    for copy in copies:
        copy.wait()
    inside, _ = sphere(col_ref[...], size)
    parts = [jnp.where(inside, psi_ref[p], 0.0) for p in range(2)]
    to_planes(peers_of(devices, me_ref, odd_ref), parts, ahead_ref, outs)
    radius = size // 4
    gx, gy = position(col_ref[...], size)
    used = gx * gx + gy * gy <= float(radius * radius)
    rows = ahead_ref.shape[1]
    row = lax.broadcasted_iota(jnp.int32, (8, gx.shape[1]), 0)
    slot, lane = jnp.zeros(row.shape, F32), jnp.zeros(row.shape, F32)
    for i, (_, s, middle) in enumerate(packing(size)[0]):
        here = gx == float(i - radius)
        slot, lane = jnp.where(here, float(s), slot), jnp.where(here, float(middle), lane)
    place = jnp.where(used, jnp.where(row == 0, slot, lane + gy), -9.0)
    for k in range(devices):
        outs[k][rows:] = place


def middle_kernel(devices, size, me_ref, odd_ref, low_ref, up_ref, *refs):
    planes, refs = refs[:devices], refs[devices:]
    psi_ref, col_ref, ahead_ref, back_ref, first_ref = refs[:5]
    outs, held = refs[5 : 5 + devices], refs[5 + devices]
    center = (up_ref[0] + low_ref[0]) / 2.0
    half = (up_ref[0] - low_ref[0]) / 2.0
    inside, kinetic = sphere(col_ref[...], size)
    peers = peers_of(devices, me_ref, odd_ref)
    back = from_planes(peers, planes, back_ref, held, size)
    parts = []
    for p in range(2):
        value = jnp.where(inside, ((kinetic - center) * kept_rows(psi_ref, p, size) + back[p]) / half, 0.0)
        first_ref[p] = value
        parts.append(value)
    to_planes(peers, parts, ahead_ref, outs)


def last_kernel(devices, bands, size, me_ref, odd_ref, low_ref, up_ref, *refs):
    planes, refs = refs[:devices], refs[devices:]
    psi_ref, first_ref, col_ref, back_ref, pick_ref, filtered_ref, packed_ref, held = refs
    center = (up_ref[0] + low_ref[0]) / 2.0
    half = (up_ref[0] - low_ref[0]) / 2.0
    inside, kinetic = sphere(col_ref[...], size)
    back = from_planes(peers_of(devices, me_ref, odd_ref), planes, back_ref, held, size)
    first, last = kept(size)
    total = None
    for p in range(2):
        value = 2.0 * ((kinetic - center) * first_ref[p] + back[p]) / half - kept_rows(psi_ref, p, size)
        value = jnp.where(inside, value, 0.0)
        filtered_ref[p, :first] = value[:first]
        filtered_ref[p, first : size - last] = jnp.zeros((size - last - first, value.shape[1]), F32)
        filtered_ref[p, size - last :] = value[first:]
        piece = dot(pick_ref[p], value.astype(BF16))
        total = piece if total is None else total + piece
    rows = packed_ref.shape[1]
    for k in range(bands):
        packed_ref[k] = total[k * rows : (k + 1) * rows].astype(BF16)


def gram_kernel(bands, parts_ref, sum_ref, spare_ref):
    rows, cols = parts_ref.shape[1:]
    count = bands * rows
    stacked = parts_ref[...].reshape(count, cols)
    product = dot(stacked, stacked, ((1,), (1,)))
    down = lax.broadcasted_iota(jnp.int32, (count, count), 0) % rows
    along = lax.broadcasted_iota(jnp.int32, (count, count), 1) % rows
    real = jnp.where(down == along, product, 0.0)
    imag = jnp.where(along == down + rows // 2, product, jnp.where(down == along + rows // 2, -product, 0.0))
    place = lax.broadcasted_iota(jnp.int32, (count, 128), 0) // rows
    spot = lax.broadcasted_iota(jnp.int32, (count, 128), 1)
    pieces, places = [], []
    for p, value in enumerate((real, imag)):
        value = jnp.sum(value.reshape(bands, rows, count), axis=1)
        hot = jnp.where(place + p * GY == spot, 1.0, 0.0).astype(BF16)
        for _ in range(3):
            pieces.append(value.astype(BF16))
            value = value - pieces[-1].astype(F32)
            places.append(hot)
    value = dot(jnp.concatenate(pieces, axis=1), jnp.concatenate(places, axis=0))
    for g in range(sum_ref.shape[0] // bands):
        sum_ref[g * bands : (g + 1) * bands, 0, :] = value
    spare_ref[...] = value


def total_kernel(own, scale, me_ref, parts_ref, out_ref):
    value = jnp.sum(parts_ref[...], axis=0) * scale
    value = pltpu.roll(value, lax.rem(128 - me_ref[0] * own, 128), 1)
    out_ref[0] = value[:, :own]
    out_ref[1] = value[:, GY : GY + own]


def scatter(plane_ref, mark_ref, slots):
    rows, cols = mark_ref.shape[0] - 8, mark_ref.shape[1]
    row = lax.broadcasted_iota(jnp.int32, (8, 256), 0)
    side = lax.broadcasted_iota(jnp.int32, (8, 256), 1) // 128
    spread = jnp.where(row == side, 1.0, 0.0).astype(BF16)
    both = dot(mark_ref[rows:].astype(BF16), spread, ((0,), (0,)))
    slot = both[:, :128].astype(BF16)
    along = lax.broadcasted_iota(jnp.int32, (cols, 128), 1).astype(F32)
    spot = jnp.where(both[:, 128:] == along, 1.0, 0.0).astype(BF16)
    lhs = jnp.concatenate(split(plane_ref[:rows]), axis=0)
    zero = jnp.zeros((), BF16)
    for t in range(0, slots, 2):
        hot = [jnp.where(slot == float(v), spot, zero) for v in (t, t + 1)]
        got = dot(lhs, jnp.concatenate(hot, axis=1))
        yield t, got[:rows] + got[rows:]


def gather(box, mark_ref, out_ref, slots):
    rows, cols = mark_ref.shape[0] - 8, mark_ref.shape[1]
    zero = jnp.zeros((), BF16)
    wide = min(256, cols)
    for at in range(0, cols, wide):
        slot = jnp.broadcast_to(mark_ref[rows : rows + 1, at : at + wide], (16, wide)).astype(BF16)
        spot = jnp.broadcast_to(mark_ref[rows + 1 : rows + 2, at : at + wide], (128, wide))
        down = lax.broadcasted_iota(jnp.int32, (128, wide), 0).astype(F32)
        hot = jnp.where(spot == down, 1.0, 0.0).astype(BF16)
        tall = []
        for v in range(slots):
            here = slot == float(v)
            tall += [jnp.where(here, hot[16 * i : 16 * i + 16], zero) for i in range(8)]
        got = dot(box, jnp.concatenate(tall, axis=0))
        out_ref[:, at : at + wide] = got[:rows] + got[rows:]


def scatter_kernel(slots, plane_ref, mark_ref, *refs):
    before, after = refs[:-1], refs[-1]
    for t, tile in scatter(plane_ref, mark_ref, slots):
        here = slice(128 * t, 128 * t + 256)
        after[:, here] = tile + before[0][:, here] if before else tile


def gather_kernel(slots, box_ref, mark_ref, out_ref):
    gather(box_ref[...], mark_ref, out_ref, slots)


def slab_kernel(devices, size, depth, plane_ref, before_ref, *refs):
    marks, refs = refs[: devices - 1], refs[devices - 1 :]
    pot_ref, ty_ref, tx_ref, txb_ref, tyb_ref = refs[:5]
    outs, box_ref = refs[5 : 4 + devices], refs[4 + devices]
    in_ref, y0_ref, y1_ref, back_ref, q_ref = refs[5 + devices :]
    pad = round_up(depth, 8)
    radius = size // 4
    places, slots = packing(size)
    lane = lax.broadcasted_iota(jnp.int32, (pad, 128), 1)

    def between(first, last):
        return (lane >= first) & (lane <= last)

    in_ref[...] = jnp.zeros(in_ref.shape, F32)
    for t, tile in scatter(plane_ref, marks[-1], slots):
        got = tile + before_ref[:, 128 * t : 128 * t + 256]
        for i, (width, slot, middle) in enumerate(places):
            if slot // 2 * 2 != t:
                continue
            at = 128 * (slot - t)
            re = pltpu.roll(got[:pad, at : at + 128], (radius - middle) % 128, 1)
            im = pltpu.roll(got[pad:, at : at + 128], (radius + GY - middle) % 128, 1)
            im = jnp.where(between(GY + radius - width, GY + radius + width), im, 0.0)
            in_ref[pl.ds(i, pad, stride=GX), :] = jnp.where(between(radius - width, radius + width), re, im)
    moved = dot(tripled(in_ref[...], 1), ty_ref[...])
    y0_ref[...] = moved[:, :128]
    y1_ref[...] = moved[:, 128:]
    if depth < pad:
        q_ref[depth * GX :] = jnp.zeros(((pad - depth) * GX, 128), F32)

    chunk, group = 8, 4
    for first in range(0, depth, chunk):
        last = min(depth, first + chunk)
        for z in range(first, last, group):
            near = range(z, min(z + group, last))
            sides = []
            for w in near:
                line = slice(w * GX, (w + 1) * GX)
                sides.append(jnp.concatenate([y0_ref[line, :], y1_ref[line, :]], axis=0))
            field = dot(tx_ref[...], jnp.concatenate(split(jnp.concatenate(sides, axis=1)), axis=0))
            pot = jnp.concatenate([pot_ref[w] for w in near], axis=1)
            field = (field[: 2 * size] + field[2 * size :]) * jnp.concatenate([pot, pot], axis=0)
            high, low = split(field)
            back = dot(txb_ref[...], high)
            back = back[: 2 * GX] + back[2 * GX :] + dot(txb_ref[: 2 * GX], low)
            for w in near:
                for p in range(2):
                    at = 128 * (w - z)
                    back_ref[w * GX : (w + 1) * GX, 128 * p : 128 * p + 128] = back[
                        p * GX : (p + 1) * GX, at : at + 128
                    ]
        part = slice(first * GX, last * GX)
        high, low = split(back_ref[part])
        moved = dot(high, tyb_ref[...])
        q_ref[part] = moved[:, :128] + moved[:, 128:] + dot(low, tyb_ref[:, :128])

    for s in range(slots):
        re, im = jnp.zeros((pad, 128), F32), jnp.zeros((pad, 128), F32)
        for i, (width, slot, middle) in enumerate(places):
            if slot != s:
                continue
            value = q_ref[pl.ds(i, pad, stride=GX), :]
            here = between(middle - width, middle + width)
            re = jnp.where(here, pltpu.roll(value, (middle - radius) % 128, 1), re)
            im = jnp.where(here, pltpu.roll(value, (middle - radius - GY) % 128, 1), im)
        box_ref[:, 128 * s : 128 * s + 128] = jnp.concatenate(split(jnp.concatenate([re, im], axis=0)), axis=0)

    box = box_ref[...]
    for k in range(devices - 1):
        gather(box, marks[k], outs[k], slots)


def body(devices, bands, psi, col_map, potential, lower, upper):
    cols, size = psi.shape[2], psi.shape[3]
    radius = size // 4
    depth = size // devices
    pad = round_up(depth, 8)
    rows = 2 * pad
    me = lax.axis_index("grid")
    me_arg = me.astype(jnp.int32).reshape(1)
    odd_arg = (lax.axis_index("band") & 1).astype(jnp.int32).reshape(1)
    if devices & (devices - 1):
        raise ValueError("mesh size")

    def pairs(k):
        steps = [swapped(k, devices) if band % 2 else k for band in range(bands)]
        return [(d * bands + b, (d ^ steps[b]) * bands + b) for d in range(devices) for b in range(bands)]

    def exchange(values):
        return [values[0]] + [
            lax.ppermute(values[k], ("grid", "band"), pairs(k)) for k in range(1, devices)
        ]

    ahead, back = z_tables(size, devices, pad)
    tables = plane_tables(size)
    count = 2 * radius + 1
    slots = round_up(-(-count // bands), 8)
    pick = np.zeros((2, bands * 2 * slots, sum(kept(size))), ml_dtypes.bfloat16)
    for j in range(count):
        at = (j % bands) * 2 * slots + j // bands
        pick[0, at, (j - radius) % sum(kept(size))] = 1
        pick[1, at + slots, (j - radius) % sum(kept(size))] = 1

    pot = (potential * (1.0 / float(size**3))).reshape(depth, size, size)
    pot = jnp.pad(pot, ((0, 0), (0, 0), (0, 128 - size)))
    psi_t = jnp.transpose(psi.reshape(2, cols, size), (0, 2, 1))
    col_row = col_map.reshape(1, cols)

    def vmem(shape, dtype=F32):
        return pltpu.VMEM(shape, dtype)

    marks = exchange(
        call(
            functools.partial(first_kernel, devices, size),
            [vmem((rows + 8, cols))] * devices,
            [me_arg, odd_arg],
            [(psi_t, True), (col_row, True), (ahead, True)],
            [
                pltpu.VMEM((2, sum(kept(size)), cols), F32),
                pltpu.VMEM(col_row.shape, jnp.int32),
                pltpu.VMEM(ahead.shape, BF16),
                pltpu.SemaphoreType.DMA((6,)),
            ],
            far=True,
        )
    )

    slots_all = packing(size)[1]
    box_shape = (rows, 128 * slots_all)

    def slab(values):
        sums = []
        for k in range(devices - 1):
            sums = call(
                functools.partial(scatter_kernel, slots_all),
                [vmem(box_shape)],
                [],
                [(value, True) for value in [values[k], marks[k]] + list(sums)],
            )
        given = [values[-1], sums[0]] + marks[1:]
        *sent, box = call(
            functools.partial(slab_kernel, devices, size, depth),
            [vmem((rows, cols))] * (devices - 1) + [vmem((2 * rows, 128 * slots_all), BF16)],
            [],
            [(value, True) for value in given] + [(pot, False)] + [(table, False) for table in tables],
            [
                pltpu.VMEM((GX * pad, 128), F32),
                pltpu.VMEM((GX * pad, 128), F32),
                pltpu.VMEM((GX * pad, 128), F32),
                pltpu.VMEM((pad * GX, 256), F32),
                pltpu.VMEM((pad * GX, 128), F32),
            ],
        )
        own = call(
            functools.partial(gather_kernel, slots_all),
            [vmem((rows, cols))],
            [],
            [(box, True), (marks[0], True)],
        )
        return list(own) + list(sent)

    held = pltpu.VMEM((3 * devices * rows, cols), BF16)
    planes = exchange(slab(marks))
    first, *sent = call(
        functools.partial(middle_kernel, devices, size),
        [vmem((2, sum(kept(size)), cols))] + [vmem((rows, cols))] * devices,
        [me_arg, odd_arg, lower, upper],
        [(value, True) for value in planes] + [(psi_t, False), (col_row, False), (ahead, False), (back, False)],
        [held],
    )
    planes = exchange(slab(exchange(sent)))
    filtered, packed = call(
        functools.partial(last_kernel, devices, bands, size),
        [vmem((2, size, cols)), vmem((bands, 2 * slots, cols), BF16)],
        [me_arg, odd_arg, lower, upper],
        [(value, True) for value in planes]
        + [(psi_t, False), (first, True), (col_row, False), (back, False), (pick, False)],
        [held],
    )
    partial_sum, _ = call(
        functools.partial(gram_kernel, bands),
        [vmem((devices * bands, 1, 128)), vmem((bands, 128))],
        [],
        [(lax.all_to_all(packed, "band", 0, 0, tiled=True), True)],
    )
    own = bands // devices
    (gram,) = call(
        functools.partial(total_kernel, own, 1.0 / (4.0 * radius**3)),
        [jax.ShapeDtypeStruct((2, 1, own), F32)],
        [me_arg],
        [(lax.all_to_all(partial_sum, ("grid", "band"), 0, 0, tiled=True), True)],
    )
    return jnp.transpose(filtered, (0, 2, 1)).reshape(psi.shape), gram


def solution(mesh):
    return jax.shard_map(
        functools.partial(body, mesh.shape["grid"], mesh.shape["band"]),
        mesh=mesh,
        in_specs=(P(None, "band", "grid", None), P("grid"), P("grid", None), P(), P()),
        out_specs=(P(None, "band", "grid", None), P(None, "band", "grid")),
        check_vma=False,
    )
```

```python
import functools

import jax
import jax.numpy as jnp
import ml_dtypes
import numpy as np
from jax import lax
from jax.experimental import pallas as pl
from jax.experimental.pallas import tpu as pltpu
from jax.sharding import PartitionSpec as P

GY = 64
GX = 56
F32 = jnp.float32
BF16 = jnp.bfloat16
MIB = 1024 * 1024


def round_up(value, unit):
    return -(-value // unit) * unit


def halves(table):
    table = np.asarray(table, np.float32)
    high = table.astype(ml_dtypes.bfloat16)
    low = (table - high.astype(np.float32)).astype(ml_dtypes.bfloat16)
    return high, low


def stacked_table(table, axis):
    high, low = halves(table)
    return np.concatenate([high, high, low], axis=axis)


def folded(index, size):
    return np.where(index < size // 2, index, index - size)


def kept(size):
    radius = size // 4
    return round_up(radius + 1, 8), radius


def z_tables(size, devices, pad):
    depth = size // devices
    rows = 2 * pad
    first, last = kept(size)
    count = first + last
    freq = np.concatenate([np.arange(first), np.arange(size - last, size)])
    ahead = np.zeros((devices, rows, 2 * count))
    back = np.zeros((2 * count, devices * rows))
    for d in range(devices):
        plane = d * depth + np.arange(depth)
        angle = 2 * np.pi * ((plane[:, None] * freq[None, :]) % size) / size
        c, s = np.cos(angle), np.sin(angle)
        ahead[d, :depth, :count], ahead[d, :depth, count:] = c, -s
        ahead[d, pad : pad + depth, :count], ahead[d, pad : pad + depth, count:] = s, c
        at = d * rows
        back[:count, at : at + depth], back[:count, at + pad : at + pad + depth] = c.T, s.T
        back[count:, at : at + depth], back[count:, at + pad : at + pad + depth] = -s.T, c.T
    return stacked_table(ahead, 2), stacked_table(back, 1)


def plane_tables(size):
    radius = size // 4
    count = 2 * radius + 1
    freq = np.arange(count) - radius
    angle = 2 * np.pi * ((freq[:, None] * np.arange(size)[None, :]) % size) / size
    c, s = np.cos(angle), np.sin(angle)
    ty = np.zeros((2 * GY, 256))
    ty[:count, :size], ty[:count, 128 : 128 + size] = c, s
    ty[GY : GY + count, :size], ty[GY : GY + count, 128 : 128 + size] = -s, c
    tyb = np.zeros((256, 2 * GY))
    tyb[:size, :count], tyb[:size, GY : GY + count] = c.T, -s.T
    tyb[128 : 128 + size, :count], tyb[128 : 128 + size, GY : GY + count] = s.T, c.T
    tx = np.zeros((2 * size, 2 * GX))
    tx[:size, :count], tx[:size, GX : GX + count] = c.T, -s.T
    tx[size:, :count], tx[size:, GX : GX + count] = s.T, c.T
    txb = np.zeros((2 * GX, 2 * size))
    txb[:count, :size], txb[:count, size:] = c, s
    txb[GX : GX + count, :size], txb[GX : GX + count, size:] = -s, c
    high, low = halves(tx)
    tx = np.concatenate([np.concatenate([high, high], 1), np.concatenate([low, 0 * low], 1)], 0)
    return stacked_table(ty, 0), tx, np.concatenate(halves(txb), 0), np.concatenate(halves(tyb), 1)


def packing(size):
    radius = size // 4
    widths = [int(np.sqrt(radius * radius - g * g)) for g in range(-radius, radius + 1)]
    slots, free = [None] * len(widths), []
    for i in sorted(range(len(widths)), key=lambda j: (-widths[j], j)):
        span = 2 * widths[i] + 1
        for s in range(len(free) + 1):
            if s == len(free):
                free.append(128)
            if free[s] >= span:
                slots[i] = (widths[i], s, 128 - free[s] + widths[i])
                free[s] -= span
                break
    return slots, round_up(len(free), 2)


def split(value):
    high = value.astype(BF16)
    low = (value - high.astype(F32)).astype(BF16)
    return high, low


def tripled(value, axis):
    high, low = split(value)
    return jnp.concatenate([high, low, high], axis=axis)


def dot(a, b, dims=((1,), (0,))):
    return lax.dot_general(a, b, (dims, ((), ())), preferred_element_type=F32)


SMEM = pl.BlockSpec(memory_space=pltpu.SMEM)
VMEM = pl.BlockSpec(memory_space=pltpu.VMEM)
HBM = pl.BlockSpec(memory_space=pltpu.HBM)


def call(kernel, out_shape, scalars, arrays, scratch=(), limit=24, far=False):
    space = pltpu.HBM if far else pltpu.VMEM
    arrays = [pltpu.with_memory_space_constraint(value, space) if keep else value for value, keep in arrays]
    return pl.pallas_call(
        kernel,
        out_shape=out_shape,
        in_specs=[SMEM] * len(scalars) + [HBM if far else VMEM] * len(arrays),
        out_specs=[VMEM] * len(out_shape),
        scratch_shapes=list(scratch),
        compiler_params=pltpu.CompilerParams(vmem_limit_bytes=limit * MIB),
    )(*scalars, *arrays)


def position(col_row, size):
    place = col_row.astype(F32)
    kx = jnp.floor((place + 0.5) * (1.0 / size))
    ky = place - kx * size
    half = float(size // 2)
    return jnp.where(kx < half, kx, kx - size), jnp.where(ky < half, ky, ky - size)


def sphere(col_row, size):
    cols = col_row.shape[1]
    radius = size // 4
    gx, gy = position(col_row, size)
    first, last = kept(size)
    index = lax.broadcasted_iota(jnp.int32, (first + last, cols), 0)
    freq = jnp.where(index < first, index, index - (first + last)).astype(F32)
    radius2 = (gx * gx + gy * gy) + freq * freq
    return radius2 <= float(radius * radius), radius2 * (2.0 / (radius * radius))


def kept_rows(ref, p, size):
    first, last = kept(size)
    return jnp.concatenate([ref[p, :first], ref[p, size - last :]], axis=0)


def to_planes(me, parts, table_ref, outs, step):
    value = tripled(jnp.concatenate(parts, axis=0), 0)
    table = jnp.concatenate([table_ref[step(me, k)] for k in range(len(outs))], axis=0)
    total = dot(table, value)
    rows = table_ref.shape[1]
    for k in range(len(outs)):
        outs[k][:rows] = total[k * rows : (k + 1) * rows]


def from_planes(me, planes, table_ref, held, step, size):
    rows = planes[0].shape[0]
    third = rows * len(planes)
    for k in range(len(planes)):
        high, low = split(planes[k][...])
        at = step(me, k) * rows
        for j, value in enumerate((high, low, high)):
            held[pl.ds(pl.multiple_of(j * third + at, 16), rows), :] = value
    total = dot(table_ref[...], held[...])
    return total[: sum(kept(size))], total[sum(kept(size)) :]


def first_kernel(devices, step, size, me_ref, *refs):
    far, refs = refs[:3], refs[3:]
    outs, (psi_ref, col_ref, ahead_ref, sems) = refs[:devices], refs[devices:]
    first, last = kept(size)
    pairs = [(far[1], col_ref), (far[2], ahead_ref)]
    for p in range(2):
        pairs.append((far[0].at[p, :first], psi_ref.at[p, :first]))
        pairs.append((far[0].at[p, size - last :], psi_ref.at[p, first:]))
    copies = [pltpu.make_async_copy(source, target, sems.at[i]) for i, (source, target) in enumerate(pairs)]
    for copy in copies:
        copy.start()
    for copy in copies:
        copy.wait()
    inside, _ = sphere(col_ref[...], size)
    parts = [jnp.where(inside, psi_ref[p], 0.0) for p in range(2)]
    to_planes(me_ref[0], parts, ahead_ref, outs, step)
    radius = size // 4
    gx, gy = position(col_ref[...], size)
    used = gx * gx + gy * gy <= float(radius * radius)
    rows = ahead_ref.shape[1]
    row = lax.broadcasted_iota(jnp.int32, (8, gx.shape[1]), 0)
    slot, lane = jnp.zeros(row.shape, F32), jnp.zeros(row.shape, F32)
    for i, (_, s, middle) in enumerate(packing(size)[0]):
        here = gx == float(i - radius)
        slot, lane = jnp.where(here, float(s), slot), jnp.where(here, float(middle), lane)
    place = jnp.where(used, jnp.where(row == 0, slot, lane + gy), -9.0)
    for k in range(devices):
        outs[k][rows:] = place


def middle_kernel(devices, step, size, me_ref, low_ref, up_ref, *refs):
    planes, refs = refs[:devices], refs[devices:]
    psi_ref, col_ref, ahead_ref, back_ref, first_ref = refs[:5]
    outs, held = refs[5 : 5 + devices], refs[5 + devices]
    center = (up_ref[0] + low_ref[0]) / 2.0
    half = (up_ref[0] - low_ref[0]) / 2.0
    inside, kinetic = sphere(col_ref[...], size)
    back = from_planes(me_ref[0], planes, back_ref, held, step, size)
    parts = []
    for p in range(2):
        value = jnp.where(inside, ((kinetic - center) * kept_rows(psi_ref, p, size) + back[p]) / half, 0.0)
        first_ref[p] = value
        parts.append(value)
    to_planes(me_ref[0], parts, ahead_ref, outs, step)


def last_kernel(devices, bands, step, size, me_ref, low_ref, up_ref, *refs):
    planes, refs = refs[:devices], refs[devices:]
    psi_ref, first_ref, col_ref, back_ref, pick_ref, filtered_ref, packed_ref, held = refs
    center = (up_ref[0] + low_ref[0]) / 2.0
    half = (up_ref[0] - low_ref[0]) / 2.0
    inside, kinetic = sphere(col_ref[...], size)
    back = from_planes(me_ref[0], planes, back_ref, held, step, size)
    first, last = kept(size)
    total = None
    for p in range(2):
        value = 2.0 * ((kinetic - center) * first_ref[p] + back[p]) / half - kept_rows(psi_ref, p, size)
        value = jnp.where(inside, value, 0.0)
        filtered_ref[p, :first] = value[:first]
        filtered_ref[p, first : size - last] = jnp.zeros((size - last - first, value.shape[1]), F32)
        filtered_ref[p, size - last :] = value[first:]
        piece = dot(pick_ref[p], value.astype(BF16))
        total = piece if total is None else total + piece
    rows = packed_ref.shape[1]
    for k in range(bands):
        packed_ref[k] = total[k * rows : (k + 1) * rows].astype(BF16)


def gram_kernel(bands, parts_ref, sum_ref):
    rows, cols = parts_ref.shape[1:]
    count = bands * rows
    stacked = parts_ref[...].reshape(count, cols)
    product = dot(stacked, stacked, ((1,), (1,)))
    down = lax.broadcasted_iota(jnp.int32, (count, count), 0) % rows
    along = lax.broadcasted_iota(jnp.int32, (count, count), 1) % rows
    real = jnp.where(down == along, product, 0.0)
    imag = jnp.where(along == down + rows // 2, product, jnp.where(down == along + rows // 2, -product, 0.0))
    place = lax.broadcasted_iota(jnp.int32, (count, 128), 0) // rows
    spot = lax.broadcasted_iota(jnp.int32, (count, 128), 1)
    pieces, places = [], []
    for p, value in enumerate((real, imag)):
        value = jnp.sum(value.reshape(bands, rows, count), axis=1)
        hot = jnp.where(place + p * GY == spot, 1.0, 0.0).astype(BF16)
        for _ in range(3):
            pieces.append(value.astype(BF16))
            value = value - pieces[-1].astype(F32)
            places.append(hot)
    value = dot(jnp.concatenate(pieces, axis=1), jnp.concatenate(places, axis=0))
    for g in range(sum_ref.shape[0] // bands):
        sum_ref[g * bands : (g + 1) * bands, 0, :] = value


def total_kernel(own, scale, me_ref, parts_ref, out_ref):
    value = jnp.sum(parts_ref[...], axis=0) * scale
    value = pltpu.roll(value, lax.rem(128 - me_ref[0] * own, 128), 1)
    out_ref[0] = value[:, :own]
    out_ref[1] = value[:, GY : GY + own]


def scatter(plane_ref, mark_ref, slots):
    rows, cols = mark_ref.shape[0] - 8, mark_ref.shape[1]
    row = lax.broadcasted_iota(jnp.int32, (8, 256), 0)
    side = lax.broadcasted_iota(jnp.int32, (8, 256), 1) // 128
    spread = jnp.where(row == side, 1.0, 0.0).astype(BF16)
    both = dot(mark_ref[rows:].astype(BF16), spread, ((0,), (0,)))
    slot = both[:, :128].astype(BF16)
    along = lax.broadcasted_iota(jnp.int32, (cols, 128), 1).astype(F32)
    spot = jnp.where(both[:, 128:] == along, 1.0, 0.0).astype(BF16)
    lhs = jnp.concatenate(split(plane_ref[:rows]), axis=0)
    zero = jnp.zeros((), BF16)
    for t in range(0, slots, 2):
        hot = [jnp.where(slot == float(v), spot, zero) for v in (t, t + 1)]
        got = dot(lhs, jnp.concatenate(hot, axis=1))
        yield t, got[:rows] + got[rows:]


def gather(box, mark_ref, out_ref, slots):
    rows, cols = mark_ref.shape[0] - 8, mark_ref.shape[1]
    zero = jnp.zeros((), BF16)
    wide = min(256, cols)
    for at in range(0, cols, wide):
        slot = jnp.broadcast_to(mark_ref[rows : rows + 1, at : at + wide], (16, wide)).astype(BF16)
        spot = jnp.broadcast_to(mark_ref[rows + 1 : rows + 2, at : at + wide], (128, wide))
        down = lax.broadcasted_iota(jnp.int32, (128, wide), 0).astype(F32)
        hot = jnp.where(spot == down, 1.0, 0.0).astype(BF16)
        tall = []
        for v in range(slots):
            here = slot == float(v)
            tall += [jnp.where(here, hot[16 * i : 16 * i + 16], zero) for i in range(8)]
        got = dot(box, jnp.concatenate(tall, axis=0))
        out_ref[:, at : at + wide] = got[:rows] + got[rows:]


def scatter_kernel(slots, plane_ref, mark_ref, *refs):
    before, after = refs[:-1], refs[-1]
    for t, tile in scatter(plane_ref, mark_ref, slots):
        here = slice(128 * t, 128 * t + 256)
        after[:, here] = tile + before[0][:, here] if before else tile


def gather_kernel(slots, box_ref, mark_ref, out_ref):
    gather(box_ref[...], mark_ref, out_ref, slots)


def slab_kernel(devices, size, depth, plane_ref, before_ref, *refs):
    marks, refs = refs[: devices - 1], refs[devices - 1 :]
    pot_ref, ty_ref, tx_ref, txb_ref, tyb_ref = refs[:5]
    outs, box_ref = refs[5 : 4 + devices], refs[4 + devices]
    in_ref, y0_ref, y1_ref, back_ref, q_ref = refs[5 + devices :]
    pad = round_up(depth, 8)
    radius = size // 4
    places, slots = packing(size)
    lane = lax.broadcasted_iota(jnp.int32, (pad, 128), 1)

    def between(first, last):
        return (lane >= first) & (lane <= last)

    in_ref[...] = jnp.zeros(in_ref.shape, F32)
    for t, tile in scatter(plane_ref, marks[-1], slots):
        got = tile + before_ref[:, 128 * t : 128 * t + 256]
        for i, (width, slot, middle) in enumerate(places):
            if slot // 2 * 2 != t:
                continue
            at = 128 * (slot - t)
            re = pltpu.roll(got[:pad, at : at + 128], (radius - middle) % 128, 1)
            im = pltpu.roll(got[pad:, at : at + 128], (radius + GY - middle) % 128, 1)
            im = jnp.where(between(GY + radius - width, GY + radius + width), im, 0.0)
            in_ref[pl.ds(i, pad, stride=GX), :] = jnp.where(between(radius - width, radius + width), re, im)
    moved = dot(tripled(in_ref[...], 1), ty_ref[...])
    y0_ref[...] = moved[:, :128]
    y1_ref[...] = moved[:, 128:]
    if depth < pad:
        q_ref[depth * GX :] = jnp.zeros(((pad - depth) * GX, 128), F32)

    chunk, group = 8, 4
    for first in range(0, depth, chunk):
        last = min(depth, first + chunk)
        for z in range(first, last, group):
            near = range(z, min(z + group, last))
            sides = []
            for w in near:
                line = slice(w * GX, (w + 1) * GX)
                sides.append(jnp.concatenate([y0_ref[line, :], y1_ref[line, :]], axis=0))
            field = dot(tx_ref[...], jnp.concatenate(split(jnp.concatenate(sides, axis=1)), axis=0))
            pot = jnp.concatenate([pot_ref[w] for w in near], axis=1)
            field = (field[: 2 * size] + field[2 * size :]) * jnp.concatenate([pot, pot], axis=0)
            high, low = split(field)
            back = dot(txb_ref[...], high)
            back = back[: 2 * GX] + back[2 * GX :] + dot(txb_ref[: 2 * GX], low)
            for w in near:
                for p in range(2):
                    at = 128 * (w - z)
                    back_ref[w * GX : (w + 1) * GX, 128 * p : 128 * p + 128] = back[
                        p * GX : (p + 1) * GX, at : at + 128
                    ]
        part = slice(first * GX, last * GX)
        high, low = split(back_ref[part])
        moved = dot(high, tyb_ref[...])
        q_ref[part] = moved[:, :128] + moved[:, 128:] + dot(low, tyb_ref[:, :128])

    for s in range(slots):
        re, im = jnp.zeros((pad, 128), F32), jnp.zeros((pad, 128), F32)
        for i, (width, slot, middle) in enumerate(places):
            if slot != s:
                continue
            value = q_ref[pl.ds(i, pad, stride=GX), :]
            here = between(middle - width, middle + width)
            re = jnp.where(here, pltpu.roll(value, (middle - radius) % 128, 1), re)
            im = jnp.where(here, pltpu.roll(value, (middle - radius - GY) % 128, 1), im)
        box_ref[:, 128 * s : 128 * s + 128] = jnp.concatenate(split(jnp.concatenate([re, im], axis=0)), axis=0)

    box = box_ref[...]
    for k in range(devices - 1):
        gather(box, marks[k], outs[k], slots)


def body(devices, bands, psi, col_map, potential, lower, upper):
    cols, size = psi.shape[2], psi.shape[3]
    radius = size // 4
    depth = size // devices
    pad = round_up(depth, 8)
    rows = 2 * pad
    me = lax.axis_index("grid")
    me_arg = me.astype(jnp.int32).reshape(1)
    if devices & (devices - 1):
        raise ValueError("mesh size")

    def step(at, k):
        return at ^ k

    def exchange(values):
        return [values[0]] + [
            lax.ppermute(values[k], "grid", [(d, step(d, k)) for d in range(devices)]) for k in range(1, devices)
        ]

    ahead, back = z_tables(size, devices, pad)
    tables = plane_tables(size)
    count = 2 * radius + 1
    slots = round_up(-(-count // bands), 8)
    pick = np.zeros((2, bands * 2 * slots, sum(kept(size))), ml_dtypes.bfloat16)
    for j in range(count):
        at = (j % bands) * 2 * slots + j // bands
        pick[0, at, (j - radius) % sum(kept(size))] = 1
        pick[1, at + slots, (j - radius) % sum(kept(size))] = 1

    pot = (potential * (1.0 / float(size**3))).reshape(depth, size, size)
    pot = jnp.pad(pot, ((0, 0), (0, 0), (0, 128 - size)))
    psi_t = jnp.transpose(psi.reshape(2, cols, size), (0, 2, 1))
    col_row = col_map.reshape(1, cols)

    def vmem(shape, dtype=F32):
        return pltpu.VMEM(shape, dtype)

    marks = exchange(
        call(
            functools.partial(first_kernel, devices, step, size),
            [vmem((rows + 8, cols))] * devices,
            [me_arg],
            [(psi_t, True), (col_row, True), (ahead, True)],
            [
                pltpu.VMEM((2, sum(kept(size)), cols), F32),
                pltpu.VMEM(col_row.shape, jnp.int32),
                pltpu.VMEM(ahead.shape, BF16),
                pltpu.SemaphoreType.DMA((6,)),
            ],
            far=True,
        )
    )

    slots_all = packing(size)[1]
    box_shape = (rows, 128 * slots_all)

    def slab(values):
        order = [0] + list(range(devices - 1, 0, -1))
        sums = []
        for k in order[:-1]:
            sums = call(
                functools.partial(scatter_kernel, slots_all),
                [vmem(box_shape)],
                [],
                [(value, True) for value in [values[k], marks[k]] + list(sums)],
            )
        given = [values[order[-1]], sums[0]] + [marks[k] for k in order[1:]]
        *sent, box = call(
            functools.partial(slab_kernel, devices, size, depth),
            [vmem((rows, cols))] * (devices - 1) + [vmem((2 * rows, 128 * slots_all), BF16)],
            [],
            [(value, True) for value in given] + [(pot, False)] + [(table, False) for table in tables],
            [
                pltpu.VMEM((GX * pad, 128), F32),
                pltpu.VMEM((GX * pad, 128), F32),
                pltpu.VMEM((GX * pad, 128), F32),
                pltpu.VMEM((pad * GX, 256), F32),
                pltpu.VMEM((pad * GX, 128), F32),
            ],
        )
        own = call(
            functools.partial(gather_kernel, slots_all),
            [vmem((rows, cols))],
            [],
            [(box, True), (marks[0], True)],
        )
        return list(own) + [sent[order.index(k) - 1] for k in range(1, devices)]

    held = pltpu.VMEM((3 * devices * rows, cols), BF16)
    planes = exchange(slab(marks))
    first, *sent = call(
        functools.partial(middle_kernel, devices, step, size),
        [vmem((2, sum(kept(size)), cols))] + [vmem((rows, cols))] * devices,
        [me_arg, lower, upper],
        [(value, True) for value in planes] + [(psi_t, False), (col_row, False), (ahead, False), (back, False)],
        [held],
    )
    planes = exchange(slab(exchange(sent)))
    filtered, packed = call(
        functools.partial(last_kernel, devices, bands, step, size),
        [vmem((2, size, cols)), vmem((bands, 2 * slots, cols), BF16)],
        [me_arg, lower, upper],
        [(value, True) for value in planes]
        + [(psi_t, False), (first, True), (col_row, False), (back, False), (pick, False)],
        [held],
    )
    (partial_sum,) = call(
        functools.partial(gram_kernel, bands),
        [vmem((devices * bands, 1, 128))],
        [],
        [(lax.all_to_all(packed, "band", 0, 0, tiled=True), True)],
    )
    own = bands // devices
    (gram,) = call(
        functools.partial(total_kernel, own, 1.0 / (4.0 * radius**3)),
        [jax.ShapeDtypeStruct((2, 1, own), F32)],
        [me_arg],
        [(lax.all_to_all(partial_sum, ("grid", "band"), 0, 0, tiled=True), True)],
    )
    return jnp.transpose(filtered, (0, 2, 1)).reshape(psi.shape), gram


def solution(mesh):
    return jax.shard_map(
        functools.partial(body, mesh.shape["grid"], mesh.shape["band"]),
        mesh=mesh,
        in_specs=(P(None, "band", "grid", None), P("grid"), P("grid", None), P(), P()),
        out_specs=(P(None, "band", "grid", None), P(None, "band", "grid")),
        check_vma=False,
    )
```

```python
import functools

import jax
import jax.numpy as jnp
import ml_dtypes
import numpy as np
from jax import lax
from jax.experimental import pallas as pl
from jax.experimental.pallas import tpu as pltpu
from jax.sharding import PartitionSpec as P

GY = 64
GX = 56
F32 = jnp.float32
BF16 = jnp.bfloat16
MIB = 1024 * 1024


def round_up(value, unit):
    return -(-value // unit) * unit


def halves(table):
    table = np.asarray(table, np.float32)
    high = table.astype(ml_dtypes.bfloat16)
    low = (table - high.astype(np.float32)).astype(ml_dtypes.bfloat16)
    return high, low


def stacked_table(table, axis):
    high, low = halves(table)
    return np.concatenate([high, high, low], axis=axis)


def folded(index, size):
    return np.where(index < size // 2, index, index - size)


def kept(size):
    radius = size // 4
    return round_up(radius + 1, 8), radius


def z_tables(size, devices, pad):
    depth = size // devices
    rows = 2 * pad
    first, last = kept(size)
    count = first + last
    freq = np.concatenate([np.arange(first), np.arange(size - last, size)])
    ahead = np.zeros((devices, rows, 2 * count))
    back = np.zeros((2 * count, devices * rows))
    for d in range(devices):
        plane = d * depth + np.arange(depth)
        angle = 2 * np.pi * ((plane[:, None] * freq[None, :]) % size) / size
        c, s = np.cos(angle), np.sin(angle)
        ahead[d, :depth, :count], ahead[d, :depth, count:] = c, -s
        ahead[d, pad : pad + depth, :count], ahead[d, pad : pad + depth, count:] = s, c
        at = d * rows
        back[:count, at : at + depth], back[:count, at + pad : at + pad + depth] = c.T, s.T
        back[count:, at : at + depth], back[count:, at + pad : at + pad + depth] = -s.T, c.T
    return stacked_table(ahead, 2), stacked_table(back, 1)


def plane_tables(size):
    radius = size // 4
    count = 2 * radius + 1
    freq = np.arange(count) - radius
    angle = 2 * np.pi * ((freq[:, None] * np.arange(size)[None, :]) % size) / size
    c, s = np.cos(angle), np.sin(angle)
    ty = np.zeros((2 * GY, 256))
    ty[:count, :size], ty[:count, 128 : 128 + size] = c, s
    ty[GY : GY + count, :size], ty[GY : GY + count, 128 : 128 + size] = -s, c
    tyb = np.zeros((256, 2 * GY))
    tyb[:size, :count], tyb[:size, GY : GY + count] = c.T, -s.T
    tyb[128 : 128 + size, :count], tyb[128 : 128 + size, GY : GY + count] = s.T, c.T
    tx = np.zeros((2 * size, 2 * GX))
    tx[:size, :count], tx[:size, GX : GX + count] = c.T, -s.T
    tx[size:, :count], tx[size:, GX : GX + count] = s.T, c.T
    txb = np.zeros((2 * GX, 2 * size))
    txb[:count, :size], txb[:count, size:] = c, s
    txb[GX : GX + count, :size], txb[GX : GX + count, size:] = -s, c
    high, low = halves(tx)
    tx = np.concatenate([np.concatenate([high, high], 1), np.concatenate([low, 0 * low], 1)], 0)
    return stacked_table(ty, 0), tx, np.concatenate(halves(txb), 0), np.concatenate(halves(tyb), 1)


def packing(size):
    radius = size // 4
    widths = [int(np.sqrt(radius * radius - g * g)) for g in range(-radius, radius + 1)]
    slots, free = [None] * len(widths), []
    for i in sorted(range(len(widths)), key=lambda j: (-widths[j], j)):
        span = 2 * widths[i] + 1
        for s in range(len(free) + 1):
            if s == len(free):
                free.append(128)
            if free[s] >= span:
                slots[i] = (widths[i], s, 128 - free[s] + widths[i])
                free[s] -= span
                break
    return slots, round_up(len(free), 2)


def split(value):
    high = value.astype(BF16)
    low = (value - high.astype(F32)).astype(BF16)
    return high, low


def tripled(value, axis):
    high, low = split(value)
    return jnp.concatenate([high, low, high], axis=axis)


def dot(a, b, dims=((1,), (0,))):
    return lax.dot_general(a, b, (dims, ((), ())), preferred_element_type=F32)


SMEM = pl.BlockSpec(memory_space=pltpu.SMEM)
VMEM = pl.BlockSpec(memory_space=pltpu.VMEM)
HBM = pl.BlockSpec(memory_space=pltpu.HBM)


def call(kernel, out_shape, scalars, arrays, scratch=(), limit=24, far=False):
    space = pltpu.HBM if far else pltpu.VMEM
    arrays = [pltpu.with_memory_space_constraint(value, space) if keep else value for value, keep in arrays]
    return pl.pallas_call(
        kernel,
        out_shape=out_shape,
        in_specs=[SMEM] * len(scalars) + [HBM if far else VMEM] * len(arrays),
        out_specs=[VMEM] * len(out_shape),
        scratch_shapes=list(scratch),
        compiler_params=pltpu.CompilerParams(vmem_limit_bytes=limit * MIB),
    )(*scalars, *arrays)


def position(col_row, size):
    place = col_row.astype(F32)
    kx = jnp.floor((place + 0.5) * (1.0 / size))
    ky = place - kx * size
    half = float(size // 2)
    return jnp.where(kx < half, kx, kx - size), jnp.where(ky < half, ky, ky - size)


def sphere(col_row, size):
    cols = col_row.shape[1]
    radius = size // 4
    gx, gy = position(col_row, size)
    first, last = kept(size)
    index = lax.broadcasted_iota(jnp.int32, (first + last, cols), 0)
    freq = jnp.where(index < first, index, index - (first + last)).astype(F32)
    radius2 = (gx * gx + gy * gy) + freq * freq
    return radius2 <= float(radius * radius), radius2 * (2.0 / (radius * radius))


def kept_rows(ref, p, size):
    first, last = kept(size)
    return jnp.concatenate([ref[p, :first], ref[p, size - last :]], axis=0)


def to_planes(me, parts, table_ref, outs, step):
    value = tripled(jnp.concatenate(parts, axis=0), 0)
    table = jnp.concatenate([table_ref[step(me, k)] for k in range(len(outs))], axis=0)
    total = dot(table, value)
    rows = table_ref.shape[1]
    for k in range(len(outs)):
        outs[k][:rows] = total[k * rows : (k + 1) * rows]


def from_planes(me, planes, table_ref, held, step, size):
    rows = planes[0].shape[0]
    third = rows * len(planes)
    for k in range(len(planes)):
        high, low = split(planes[k][...])
        at = step(me, k) * rows
        for j, value in enumerate((high, low, high)):
            held[pl.ds(pl.multiple_of(j * third + at, 16), rows), :] = value
    total = dot(table_ref[...], held[...])
    return total[: sum(kept(size))], total[sum(kept(size)) :]


def first_kernel(devices, step, size, me_ref, *refs):
    far, refs = refs[:3], refs[3:]
    outs, (psi_ref, col_ref, ahead_ref, sems) = refs[:devices], refs[devices:]
    first, last = kept(size)
    pairs = [(far[1], col_ref), (far[2], ahead_ref)]
    for p in range(2):
        pairs.append((far[0].at[p, :first], psi_ref.at[p, :first]))
        pairs.append((far[0].at[p, size - last :], psi_ref.at[p, first:]))
    copies = [pltpu.make_async_copy(source, target, sems.at[i]) for i, (source, target) in enumerate(pairs)]
    for copy in copies:
        copy.start()
    copies[0].wait()
    radius = size // 4
    gx, gy = position(col_ref[...], size)
    used = gx * gx + gy * gy <= float(radius * radius)
    rows = ahead_ref.shape[1]
    row = lax.broadcasted_iota(jnp.int32, (8, gx.shape[1]), 0)
    slot, lane = jnp.zeros(row.shape, F32), jnp.zeros(row.shape, F32)
    for i, (_, s, middle) in enumerate(packing(size)[0]):
        here = gx == float(i - radius)
        slot, lane = jnp.where(here, float(s), slot), jnp.where(here, float(middle), lane)
    place = jnp.where(used, jnp.where(row == 0, slot, lane + gy), -9.0)
    for k in range(devices):
        outs[k][rows:] = place
    inside, _ = sphere(col_ref[...], size)
    for copy in copies[1:]:
        copy.wait()
    parts = [jnp.where(inside, psi_ref[p], 0.0) for p in range(2)]
    to_planes(me_ref[0], parts, ahead_ref, outs, step)


def middle_kernel(devices, step, size, me_ref, low_ref, up_ref, *refs):
    planes, refs = refs[:devices], refs[devices:]
    psi_ref, col_ref, ahead_ref, back_ref, first_ref = refs[:5]
    outs, held = refs[5 : 5 + devices], refs[5 + devices]
    center = (up_ref[0] + low_ref[0]) / 2.0
    half = (up_ref[0] - low_ref[0]) / 2.0
    inside, kinetic = sphere(col_ref[...], size)
    back = from_planes(me_ref[0], planes, back_ref, held, step, size)
    parts = []
    for p in range(2):
        value = jnp.where(inside, ((kinetic - center) * kept_rows(psi_ref, p, size) + back[p]) / half, 0.0)
        first_ref[p] = value
        parts.append(value)
    to_planes(me_ref[0], parts, ahead_ref, outs, step)


def last_kernel(devices, bands, step, size, me_ref, low_ref, up_ref, *refs):
    planes, refs = refs[:devices], refs[devices:]
    psi_ref, first_ref, col_ref, back_ref, pick_ref, filtered_ref, packed_ref, held = refs
    center = (up_ref[0] + low_ref[0]) / 2.0
    half = (up_ref[0] - low_ref[0]) / 2.0
    inside, kinetic = sphere(col_ref[...], size)
    back = from_planes(me_ref[0], planes, back_ref, held, step, size)
    first, last = kept(size)
    total = None
    for p in range(2):
        value = 2.0 * ((kinetic - center) * first_ref[p] + back[p]) / half - kept_rows(psi_ref, p, size)
        value = jnp.where(inside, value, 0.0)
        filtered_ref[p, :first] = value[:first]
        filtered_ref[p, first : size - last] = jnp.zeros((size - last - first, value.shape[1]), F32)
        filtered_ref[p, size - last :] = value[first:]
        piece = dot(pick_ref[p], value.astype(BF16))
        total = piece if total is None else total + piece
    rows = packed_ref.shape[1]
    for k in range(bands):
        packed_ref[k] = total[k * rows : (k + 1) * rows].astype(BF16)


def rest(value, unit):
    return value & (unit - 1) if unit & (unit - 1) == 0 else value % unit


def gram_kernel(bands, parts_ref, sum_ref, spare_ref):
    rows, cols = parts_ref.shape[1:]
    count = bands * rows
    stacked = parts_ref[...].reshape(count, cols)
    product = dot(stacked, stacked, ((1,), (1,)))
    down = lax.broadcasted_iota(jnp.int32, (count, count), 0)
    along = lax.broadcasted_iota(jnp.int32, (count, count), 1)
    down, along = rest(down, rows), rest(along, rows)
    real = jnp.where(down == along, product, 0.0)
    imag = jnp.where(along == down + rows // 2, product, jnp.where(down == along + rows // 2, -product, 0.0))
    place = lax.broadcasted_iota(jnp.int32, (count, 128), 0)
    spot = lax.broadcasted_iota(jnp.int32, (count, 128), 1) * rows
    pieces, places = [], []
    for p, value in enumerate((real, imag)):
        value = jnp.sum(value.reshape(bands, rows, count), axis=1)
        gap = place + p * GY * rows - spot
        hot = jnp.where((gap >= 0) & (gap < rows), 1.0, 0.0).astype(BF16)
        for _ in range(3):
            pieces.append(value.astype(BF16))
            value = value - pieces[-1].astype(F32)
            places.append(hot)
    value = dot(jnp.concatenate(pieces, axis=1), jnp.concatenate(places, axis=0))
    for g in range(sum_ref.shape[0] // bands):
        sum_ref[g * bands : (g + 1) * bands, 0, :] = value
    spare_ref[...] = value


def total_kernel(own, scale, me_ref, parts_ref, out_ref):
    value = jnp.sum(parts_ref[...], axis=0) * scale
    value = pltpu.roll(value, lax.rem(128 - me_ref[0] * own, 128), 1)
    out_ref[0] = value[:, :own]
    out_ref[1] = value[:, GY : GY + own]


def scatter(plane_ref, mark_ref, slots):
    rows, cols = mark_ref.shape[0] - 8, mark_ref.shape[1]
    row = lax.broadcasted_iota(jnp.int32, (8, 256), 0)
    side = lax.broadcasted_iota(jnp.int32, (8, 256), 1) // 128
    spread = jnp.where(row == side, 1.0, 0.0).astype(BF16)
    both = dot(mark_ref[rows:].astype(BF16), spread, ((0,), (0,)))
    slot = both[:, :128].astype(BF16)
    along = lax.broadcasted_iota(jnp.int32, (cols, 128), 1).astype(F32)
    spot = jnp.where(both[:, 128:] == along, 1.0, 0.0).astype(BF16)
    lhs = jnp.concatenate(split(plane_ref[:rows]), axis=0)
    zero = jnp.zeros((), BF16)
    for t in range(0, slots, 2):
        hot = [jnp.where(slot == float(v), spot, zero) for v in (t, t + 1)]
        got = dot(lhs, jnp.concatenate(hot, axis=1))
        yield t, got[:rows] + got[rows:]


def gather(box, mark_ref, out_ref, slots):
    rows, cols = mark_ref.shape[0] - 8, mark_ref.shape[1]
    zero = jnp.zeros((), BF16)
    wide = min(512, cols)
    for at in range(0, cols, wide):
        slot = jnp.broadcast_to(mark_ref[rows : rows + 1, at : at + wide], (16, wide)).astype(BF16)
        spot = jnp.broadcast_to(mark_ref[rows + 1 : rows + 2, at : at + wide], (128, wide))
        down = lax.broadcasted_iota(jnp.int32, (128, wide), 0).astype(F32)
        hot = jnp.where(spot == down, 1.0, 0.0).astype(BF16)
        tall = []
        for v in range(slots):
            here = slot == float(v)
            tall += [jnp.where(here, hot[16 * i : 16 * i + 16], zero) for i in range(8)]
        got = dot(box, jnp.concatenate(tall, axis=0))
        out_ref[:, at : at + wide] = got[:rows] + got[rows:]


def scatter_kernel(slots, plane_ref, mark_ref, *refs):
    before, after = refs[:-1], refs[-1]
    for t, tile in scatter(plane_ref, mark_ref, slots):
        here = slice(128 * t, 128 * t + 256)
        after[:, here] = tile + before[0][:, here] if before else tile


def gather_kernel(slots, box_ref, mark_ref, out_ref):
    gather(box_ref[...], mark_ref, out_ref, slots)


def slab_kernel(devices, size, depth, plane_ref, before_ref, *refs):
    marks, refs = refs[: devices - 1], refs[devices - 1 :]
    pot_ref, ty_ref, tx_ref, txb_ref, tyb_ref = refs[:5]
    outs, box_ref = refs[5 : 4 + devices], refs[4 + devices]
    in_ref, y0_ref, y1_ref, back_ref, q_ref = refs[5 + devices :]
    pad = round_up(depth, 8)
    radius = size // 4
    places, slots = packing(size)
    lane = lax.broadcasted_iota(jnp.int32, (pad, 128), 1)

    def between(first, last):
        return (lane >= first) & (lane <= last)

    in_ref[...] = jnp.zeros(in_ref.shape, F32)
    for t, tile in scatter(plane_ref, marks[-1], slots):
        got = tile + before_ref[:, 128 * t : 128 * t + 256]
        for i, (width, slot, middle) in enumerate(places):
            if slot // 2 * 2 != t:
                continue
            at = 128 * (slot - t)
            re = pltpu.roll(got[:pad, at : at + 128], (radius - middle) % 128, 1)
            im = pltpu.roll(got[pad:, at : at + 128], (radius + GY - middle) % 128, 1)
            im = jnp.where(between(GY + radius - width, GY + radius + width), im, 0.0)
            in_ref[pl.ds(i, pad, stride=GX), :] = jnp.where(between(radius - width, radius + width), re, im)
    moved = dot(tripled(in_ref[...], 1), ty_ref[...])
    y0_ref[...] = moved[:, :128]
    y1_ref[...] = moved[:, 128:]
    if depth < pad:
        q_ref[depth * GX :] = jnp.zeros(((pad - depth) * GX, 128), F32)

    chunk, group = 8, 4
    for first in range(0, depth, chunk):
        last = min(depth, first + chunk)
        for z in range(first, last, group):
            near = range(z, min(z + group, last))
            sides = []
            for w in near:
                line = slice(w * GX, (w + 1) * GX)
                sides.append(jnp.concatenate([y0_ref[line, :], y1_ref[line, :]], axis=0))
            field = dot(tx_ref[...], jnp.concatenate(split(jnp.concatenate(sides, axis=1)), axis=0))
            pot = jnp.concatenate([pot_ref[w] for w in near], axis=1)
            field = (field[: 2 * size] + field[2 * size :]) * jnp.concatenate([pot, pot], axis=0)
            high, low = split(field)
            back = dot(txb_ref[...], high)
            back = back[: 2 * GX] + back[2 * GX :] + dot(txb_ref[: 2 * GX], low)
            for w in near:
                for p in range(2):
                    at = 128 * (w - z)
                    back_ref[w * GX : (w + 1) * GX, 128 * p : 128 * p + 128] = back[
                        p * GX : (p + 1) * GX, at : at + 128
                    ]
        part = slice(first * GX, last * GX)
        high, low = split(back_ref[part])
        moved = dot(high, tyb_ref[...])
        q_ref[part] = moved[:, :128] + moved[:, 128:] + dot(low, tyb_ref[:, :128])

    for s in range(slots):
        re, im = jnp.zeros((pad, 128), F32), jnp.zeros((pad, 128), F32)
        for i, (width, slot, middle) in enumerate(places):
            if slot != s:
                continue
            value = q_ref[pl.ds(i, pad, stride=GX), :]
            here = between(middle - width, middle + width)
            re = jnp.where(here, pltpu.roll(value, (middle - radius) % 128, 1), re)
            im = jnp.where(here, pltpu.roll(value, (middle - radius - GY) % 128, 1), im)
        box_ref[:, 128 * s : 128 * s + 128] = jnp.concatenate(split(jnp.concatenate([re, im], axis=0)), axis=0)

    box = box_ref[...]
    for k in range(devices - 1):
        gather(box, marks[k], outs[k], slots)


def body(devices, bands, psi, col_map, potential, lower, upper):
    cols, size = psi.shape[2], psi.shape[3]
    radius = size // 4
    depth = size // devices
    pad = round_up(depth, 8)
    rows = 2 * pad
    me = lax.axis_index("grid")
    me_arg = me.astype(jnp.int32).reshape(1)
    if devices & (devices - 1):
        raise ValueError("mesh size")

    def step(at, k):
        return at ^ k

    def exchange(values):
        return [values[0]] + [
            lax.ppermute(values[k], "grid", [(d, step(d, k)) for d in range(devices)]) for k in range(1, devices)
        ]

    ahead, back = z_tables(size, devices, pad)
    tables = plane_tables(size)
    count = 2 * radius + 1
    slots = round_up(-(-count // bands), 8)
    pick = np.zeros((2, bands * 2 * slots, sum(kept(size))), ml_dtypes.bfloat16)
    for j in range(count):
        at = (j % bands) * 2 * slots + j // bands
        pick[0, at, (j - radius) % sum(kept(size))] = 1
        pick[1, at + slots, (j - radius) % sum(kept(size))] = 1

    pot = (potential * (1.0 / float(size**3))).reshape(depth, size, size)
    pot = jnp.pad(pot, ((0, 0), (0, 0), (0, 128 - size)))
    psi_t = jnp.transpose(psi.reshape(2, cols, size), (0, 2, 1))
    col_row = col_map.reshape(1, cols)

    def vmem(shape, dtype=F32):
        return pltpu.VMEM(shape, dtype)

    marks = exchange(
        call(
            functools.partial(first_kernel, devices, step, size),
            [vmem((rows + 8, cols))] * devices,
            [me_arg],
            [(psi_t, True), (col_row, True), (ahead, True)],
            [
                pltpu.VMEM((2, sum(kept(size)), cols), F32),
                pltpu.VMEM(col_row.shape, jnp.int32),
                pltpu.VMEM(ahead.shape, BF16),
                pltpu.SemaphoreType.DMA((6,)),
            ],
            far=True,
        )
    )

    slots_all = packing(size)[1]
    box_shape = (rows, 128 * slots_all)

    def slab(values):
        order = [0] + list(range(devices - 1, 0, -1))
        sums = []
        for k in order[:-1]:
            sums = call(
                functools.partial(scatter_kernel, slots_all),
                [vmem(box_shape)],
                [],
                [(value, True) for value in [values[k], marks[k]] + list(sums)],
            )
        given = [values[order[-1]], sums[0]] + [marks[k] for k in order[1:]]
        *sent, box = call(
            functools.partial(slab_kernel, devices, size, depth),
            [vmem((rows, cols))] * (devices - 1) + [vmem((2 * rows, 128 * slots_all), BF16)],
            [],
            [(value, True) for value in given] + [(pot, False)] + [(table, False) for table in tables],
            [
                pltpu.VMEM((GX * pad, 128), F32),
                pltpu.VMEM((GX * pad, 128), F32),
                pltpu.VMEM((GX * pad, 128), F32),
                pltpu.VMEM((pad * GX, 256), F32),
                pltpu.VMEM((pad * GX, 128), F32),
            ],
        )
        own = call(
            functools.partial(gather_kernel, slots_all),
            [vmem((rows, cols))],
            [],
            [(box, True), (marks[0], True)],
        )
        return list(own) + [sent[order.index(k) - 1] for k in range(1, devices)]

    held = pltpu.VMEM((3 * devices * rows, cols), BF16)
    planes = exchange(slab(marks))
    first, *sent = call(
        functools.partial(middle_kernel, devices, step, size),
        [vmem((2, sum(kept(size)), cols))] + [vmem((rows, cols))] * devices,
        [me_arg, lower, upper],
        [(value, True) for value in planes] + [(psi_t, False), (col_row, False), (ahead, False), (back, False)],
        [held],
    )
    planes = exchange(slab(exchange(sent)))
    filtered, packed = call(
        functools.partial(last_kernel, devices, bands, step, size),
        [vmem((2, size, cols)), vmem((bands, 2 * slots, cols), BF16)],
        [me_arg, lower, upper],
        [(value, True) for value in planes]
        + [(psi_t, False), (first, True), (col_row, False), (back, False), (pick, False)],
        [held],
    )
    partial_sum, _ = call(
        functools.partial(gram_kernel, bands),
        [vmem((devices * bands, 1, 128)), vmem((bands, 128))],
        [],
        [(lax.all_to_all(packed, "band", 0, 0, tiled=True), True)],
    )
    own = bands // devices
    (gram,) = call(
        functools.partial(total_kernel, own, 1.0 / (4.0 * radius**3)),
        [jax.ShapeDtypeStruct((2, 1, own), F32)],
        [me_arg],
        [(lax.all_to_all(partial_sum, ("grid", "band"), 0, 0, tiled=True), True)],
    )
    return jnp.transpose(filtered, (0, 2, 1)).reshape(psi.shape), gram


def solution(mesh):
    return jax.shard_map(
        functools.partial(body, mesh.shape["grid"], mesh.shape["band"]),
        mesh=mesh,
        in_specs=(P(None, "band", "grid", None), P("grid"), P("grid", None), P(), P()),
        out_specs=(P(None, "band", "grid", None), P(None, "band", "grid")),
        check_vma=False,
    )
```

```python
import functools

import jax
import jax.numpy as jnp
import ml_dtypes
import numpy as np
from jax import lax
from jax.experimental import pallas as pl
from jax.experimental.pallas import tpu as pltpu
from jax.sharding import PartitionSpec as P

GY = 64
GX = 56
F32 = jnp.float32
BF16 = jnp.bfloat16
MIB = 1024 * 1024


def round_up(value, unit):
    return -(-value // unit) * unit


def halves(table):
    table = np.asarray(table, np.float32)
    high = table.astype(ml_dtypes.bfloat16)
    low = (table - high.astype(np.float32)).astype(ml_dtypes.bfloat16)
    return high, low


def stacked_table(table, axis):
    high, low = halves(table)
    return np.concatenate([high, high, low], axis=axis)


def folded(index, size):
    return np.where(index < size // 2, index, index - size)


def kept(size):
    radius = size // 4
    return round_up(radius + 1, 8), radius


def z_tables(size, devices, pad):
    depth = size // devices
    rows = 2 * pad
    first, last = kept(size)
    count = first + last
    freq = np.concatenate([np.arange(first), np.arange(size - last, size)])
    ahead = np.zeros((devices, rows, 2 * count))
    back = np.zeros((2 * count, devices * rows))
    for d in range(devices):
        plane = d * depth + np.arange(depth)
        angle = 2 * np.pi * ((plane[:, None] * freq[None, :]) % size) / size
        c, s = np.cos(angle), np.sin(angle)
        ahead[d, :depth, :count], ahead[d, :depth, count:] = c, -s
        ahead[d, pad : pad + depth, :count], ahead[d, pad : pad + depth, count:] = s, c
        at = d * rows
        back[:count, at : at + depth], back[:count, at + pad : at + pad + depth] = c.T, s.T
        back[count:, at : at + depth], back[count:, at + pad : at + pad + depth] = -s.T, c.T
    return stacked_table(ahead, 2), stacked_table(back, 1)


def plane_tables(size):
    radius = size // 4
    count = 2 * radius + 1
    freq = np.arange(count) - radius
    angle = 2 * np.pi * ((freq[:, None] * np.arange(size)[None, :]) % size) / size
    c, s = np.cos(angle), np.sin(angle)
    ty = np.zeros((2 * GY, 256))
    ty[:count, :size], ty[:count, 128 : 128 + size] = c, s
    ty[GY : GY + count, :size], ty[GY : GY + count, 128 : 128 + size] = -s, c
    tyb = np.zeros((256, 2 * GY))
    tyb[:size, :count], tyb[:size, GY : GY + count] = c.T, -s.T
    tyb[128 : 128 + size, :count], tyb[128 : 128 + size, GY : GY + count] = s.T, c.T
    tx = np.zeros((2 * size, 2 * GX))
    tx[:size, :count], tx[:size, GX : GX + count] = c.T, -s.T
    tx[size:, :count], tx[size:, GX : GX + count] = s.T, c.T
    txb = np.zeros((2 * GX, 2 * size))
    txb[:count, :size], txb[:count, size:] = c, s
    txb[GX : GX + count, :size], txb[GX : GX + count, size:] = -s, c
    high, low = halves(tx)
    tx = np.concatenate([np.concatenate([high, high], 1), np.concatenate([low, 0 * low], 1)], 0)
    return stacked_table(ty, 0), tx, np.concatenate(halves(txb), 0), np.concatenate(halves(tyb), 1)


def packing(size):
    radius = size // 4
    widths = [int(np.sqrt(radius * radius - g * g)) for g in range(-radius, radius + 1)]
    slots, free = [None] * len(widths), []
    for i in sorted(range(len(widths)), key=lambda j: (-widths[j], j)):
        span = 2 * widths[i] + 1
        for s in range(len(free) + 1):
            if s == len(free):
                free.append(128)
            if free[s] >= span:
                slots[i] = (widths[i], s, 128 - free[s] + widths[i])
                free[s] -= span
                break
    return slots, round_up(len(free), 2)


def split(value):
    high = value.astype(BF16)
    low = (value - high.astype(F32)).astype(BF16)
    return high, low


def tripled(value, axis):
    high, low = split(value)
    return jnp.concatenate([high, low, high], axis=axis)


def dot(a, b, dims=((1,), (0,))):
    return lax.dot_general(a, b, (dims, ((), ())), preferred_element_type=F32)


SMEM = pl.BlockSpec(memory_space=pltpu.SMEM)
VMEM = pl.BlockSpec(memory_space=pltpu.VMEM)
HBM = pl.BlockSpec(memory_space=pltpu.HBM)


def call(kernel, out_shape, scalars, arrays, scratch=(), limit=24, far=False):
    space = pltpu.HBM if far else pltpu.VMEM
    arrays = [pltpu.with_memory_space_constraint(value, space) if keep else value for value, keep in arrays]
    return pl.pallas_call(
        kernel,
        out_shape=out_shape,
        in_specs=[SMEM] * len(scalars) + [HBM if far else VMEM] * len(arrays),
        out_specs=[VMEM] * len(out_shape),
        scratch_shapes=list(scratch),
        compiler_params=pltpu.CompilerParams(vmem_limit_bytes=limit * MIB),
    )(*scalars, *arrays)


def position(col_row, size):
    place = col_row.astype(F32)
    kx = jnp.floor((place + 0.5) * (1.0 / size))
    ky = place - kx * size
    half = float(size // 2)
    return jnp.where(kx < half, kx, kx - size), jnp.where(ky < half, ky, ky - size)


def sphere(col_row, size):
    cols = col_row.shape[1]
    radius = size // 4
    gx, gy = position(col_row, size)
    first, last = kept(size)
    index = lax.broadcasted_iota(jnp.int32, (first + last, cols), 0)
    freq = jnp.where(index < first, index, index - (first + last)).astype(F32)
    radius2 = (gx * gx + gy * gy) + freq * freq
    return radius2 <= float(radius * radius), radius2 * (2.0 / (radius * radius))


def kept_rows(ref, p, size):
    first, last = kept(size)
    return jnp.concatenate([ref[p, :first], ref[p, size - last :]], axis=0)


def to_planes(me, parts, table_ref, outs, step):
    value = tripled(jnp.concatenate(parts, axis=0), 0)
    table = jnp.concatenate([table_ref[step(me, k)] for k in range(len(outs))], axis=0)
    total = dot(table, value)
    rows = table_ref.shape[1]
    for k in range(len(outs)):
        outs[k][:rows] = total[k * rows : (k + 1) * rows]


def from_planes(me, planes, table_ref, held, step, size):
    rows = planes[0].shape[0]
    third = rows * len(planes)
    for k in range(len(planes)):
        high, low = split(planes[k][...])
        at = step(me, k) * rows
        for j, value in enumerate((high, low, high)):
            held[pl.ds(pl.multiple_of(j * third + at, 16), rows), :] = value
    total = dot(table_ref[...], held[...])
    return total[: sum(kept(size))], total[sum(kept(size)) :]


def first_kernel(devices, step, size, me_ref, *refs):
    far, refs = refs[:3], refs[3:]
    outs, (psi_ref, col_ref, ahead_ref, sems) = refs[:devices], refs[devices:]
    first, last = kept(size)
    pairs = [(far[1], col_ref), (far[2], ahead_ref)]
    for p in range(2):
        pairs.append((far[0].at[p, :first], psi_ref.at[p, :first]))
        pairs.append((far[0].at[p, size - last :], psi_ref.at[p, first:]))
    copies = [pltpu.make_async_copy(source, target, sems.at[i]) for i, (source, target) in enumerate(pairs)]
    for copy in copies:
        copy.start()
    copies[0].wait()
    radius = size // 4
    gx, gy = position(col_ref[...], size)
    used = gx * gx + gy * gy <= float(radius * radius)
    rows = ahead_ref.shape[1]
    row = lax.broadcasted_iota(jnp.int32, (8, gx.shape[1]), 0)
    slot, lane = jnp.zeros(row.shape, F32), jnp.zeros(row.shape, F32)
    for i, (_, s, middle) in enumerate(packing(size)[0]):
        here = gx == float(i - radius)
        slot, lane = jnp.where(here, float(s), slot), jnp.where(here, float(middle), lane)
    place = jnp.where(used, jnp.where(row == 0, slot, lane + gy), -9.0)
    for k in range(devices):
        outs[k][rows:] = place
    inside, _ = sphere(col_ref[...], size)
    for copy in copies[1:]:
        copy.wait()
    parts = [jnp.where(inside, psi_ref[p], 0.0) for p in range(2)]
    to_planes(me_ref[0], parts, ahead_ref, outs, step)


def middle_kernel(devices, step, size, me_ref, low_ref, up_ref, *refs):
    planes, refs = refs[:devices], refs[devices:]
    psi_ref, col_ref, ahead_ref, back_ref, first_ref = refs[:5]
    outs, held = refs[5 : 5 + devices], refs[5 + devices]
    center = (up_ref[0] + low_ref[0]) / 2.0
    half = (up_ref[0] - low_ref[0]) / 2.0
    inside, kinetic = sphere(col_ref[...], size)
    back = from_planes(me_ref[0], planes, back_ref, held, step, size)
    parts = []
    for p in range(2):
        value = jnp.where(inside, ((kinetic - center) * kept_rows(psi_ref, p, size) + back[p]) / half, 0.0)
        first_ref[p] = value
        parts.append(value)
    to_planes(me_ref[0], parts, ahead_ref, outs, step)


def last_kernel(devices, bands, step, size, me_ref, low_ref, up_ref, *refs):
    planes, refs = refs[:devices], refs[devices:]
    psi_ref, first_ref, col_ref, back_ref, pick_ref, filtered_ref, packed_ref, held = refs
    center = (up_ref[0] + low_ref[0]) / 2.0
    half = (up_ref[0] - low_ref[0]) / 2.0
    inside, kinetic = sphere(col_ref[...], size)
    back = from_planes(me_ref[0], planes, back_ref, held, step, size)
    first, last = kept(size)
    total = None
    for p in range(2):
        value = 2.0 * ((kinetic - center) * first_ref[p] + back[p]) / half - kept_rows(psi_ref, p, size)
        value = jnp.where(inside, value, 0.0)
        filtered_ref[p, :first] = value[:first]
        filtered_ref[p, first : size - last] = jnp.zeros((size - last - first, value.shape[1]), F32)
        filtered_ref[p, size - last :] = value[first:]
        piece = dot(pick_ref[p], value.astype(BF16))
        total = piece if total is None else total + piece
    rows = packed_ref.shape[1]
    for k in range(bands):
        packed_ref[k] = total[k * rows : (k + 1) * rows].astype(BF16)


def rest(value, unit):
    return value & (unit - 1) if unit & (unit - 1) == 0 else value % unit


def gram_kernel(bands, parts_ref, sum_ref, spare_ref):
    rows, cols = parts_ref.shape[1:]
    count = bands * rows
    stacked = parts_ref[...].reshape(count, cols)
    product = dot(stacked, stacked, ((1,), (1,)))
    down = lax.broadcasted_iota(jnp.int32, (count, count), 0)
    along = lax.broadcasted_iota(jnp.int32, (count, count), 1)
    down, along = rest(down, rows), rest(along, rows)
    real = jnp.where(down == along, product, 0.0)
    imag = jnp.where(along == down + rows // 2, product, jnp.where(down == along + rows // 2, -product, 0.0))
    place = lax.broadcasted_iota(jnp.int32, (count, 128), 0)
    spot = lax.broadcasted_iota(jnp.int32, (count, 128), 1) * rows
    pieces, places = [], []
    for p, value in enumerate((real, imag)):
        value = jnp.sum(value.reshape(bands, rows, count), axis=1)
        gap = place + p * GY * rows - spot
        hot = jnp.where((gap >= 0) & (gap < rows), 1.0, 0.0).astype(BF16)
        for _ in range(3):
            pieces.append(value.astype(BF16))
            value = value - pieces[-1].astype(F32)
            places.append(hot)
    value = dot(jnp.concatenate(pieces, axis=1), jnp.concatenate(places, axis=0))
    for g in range(sum_ref.shape[0] // bands):
        sum_ref[g * bands : (g + 1) * bands, 0, :] = value
    spare_ref[...] = value


def total_kernel(own, scale, me_ref, parts_ref, out_ref):
    value = jnp.sum(parts_ref[...], axis=0) * scale
    value = pltpu.roll(value, lax.rem(128 - me_ref[0] * own, 128), 1)
    out_ref[0] = value[:, :own]
    out_ref[1] = value[:, GY : GY + own]


def scatter(plane_ref, mark_ref, slots):
    rows, cols = mark_ref.shape[0] - 8, mark_ref.shape[1]
    row = lax.broadcasted_iota(jnp.int32, (8, 256), 0)
    side = lax.broadcasted_iota(jnp.int32, (8, 256), 1) // 128
    spread = jnp.where(row == side, 1.0, 0.0).astype(BF16)
    both = dot(mark_ref[rows:].astype(BF16), spread, ((0,), (0,)))
    slot = both[:, :128].astype(BF16)
    along = lax.broadcasted_iota(jnp.int32, (cols, 128), 1).astype(F32)
    spot = jnp.where(both[:, 128:] == along, 1.0, 0.0).astype(BF16)
    lhs = jnp.concatenate(split(plane_ref[:rows]), axis=0)
    zero = jnp.zeros((), BF16)
    for t in range(0, slots, 2):
        hot = [jnp.where(slot == float(v), spot, zero) for v in (t, t + 1)]
        got = dot(lhs, jnp.concatenate(hot, axis=1))
        yield t, got[:rows] + got[rows:]


def gather(box, mark_ref, out_ref, slots):
    rows, cols = mark_ref.shape[0] - 8, mark_ref.shape[1]
    zero = jnp.zeros((), BF16)
    wide = min(512, cols)
    for at in range(0, cols, wide):
        slot = jnp.broadcast_to(mark_ref[rows : rows + 1, at : at + wide], (16, wide)).astype(BF16)
        spot = jnp.broadcast_to(mark_ref[rows + 1 : rows + 2, at : at + wide], (128, wide))
        down = lax.broadcasted_iota(jnp.int32, (128, wide), 0).astype(F32)
        hot = jnp.where(spot == down, 1.0, 0.0).astype(BF16)
        tall = []
        for v in range(slots):
            here = slot == float(v)
            tall += [jnp.where(here, hot[16 * i : 16 * i + 16], zero) for i in range(8)]
        got = dot(box, jnp.concatenate(tall, axis=0))
        out_ref[:, at : at + wide] = got[:rows] + got[rows:]


def scatter_kernel(slots, plane_ref, mark_ref, *refs):
    before, after = refs[:-1], refs[-1]
    for t, tile in scatter(plane_ref, mark_ref, slots):
        here = slice(128 * t, 128 * t + 256)
        after[:, here] = tile + before[0][:, here] if before else tile


def gather_kernel(slots, box_ref, mark_ref, out_ref):
    gather(box_ref[...], mark_ref, out_ref, slots)


def slab_kernel(devices, size, depth, plane_ref, before_ref, *refs):
    marks, refs = refs[: devices - 1], refs[devices - 1 :]
    pot_ref, ty_ref, tx_ref, txb_ref, tyb_ref = refs[:5]
    outs, box_ref = refs[5 : 4 + devices], refs[4 + devices]
    in_ref, y0_ref, y1_ref, back_ref, q_ref = refs[5 + devices :]
    pad = round_up(depth, 8)
    radius = size // 4
    places, slots = packing(size)
    lane = lax.broadcasted_iota(jnp.int32, (pad, 128), 1)

    def between(first, last):
        return (lane >= first) & (lane <= last)

    in_ref[...] = jnp.zeros(in_ref.shape, F32)
    for t, tile in scatter(plane_ref, marks[0], slots):
        got = tile + before_ref[:, 128 * t : 128 * t + 256]
        for i, (width, slot, middle) in enumerate(places):
            if slot // 2 * 2 != t:
                continue
            at = 128 * (slot - t)
            re = pltpu.roll(got[:pad, at : at + 128], (radius - middle) % 128, 1)
            im = pltpu.roll(got[pad:, at : at + 128], (radius + GY - middle) % 128, 1)
            im = jnp.where(between(GY + radius - width, GY + radius + width), im, 0.0)
            in_ref[pl.ds(i, pad, stride=GX), :] = jnp.where(between(radius - width, radius + width), re, im)
    moved = dot(tripled(in_ref[...], 1), ty_ref[...])
    y0_ref[...] = moved[:, :128]
    y1_ref[...] = moved[:, 128:]
    if depth < pad:
        q_ref[depth * GX :] = jnp.zeros(((pad - depth) * GX, 128), F32)

    chunk, group = 8, 4
    for first in range(0, depth, chunk):
        last = min(depth, first + chunk)
        for z in range(first, last, group):
            near = range(z, min(z + group, last))
            sides = []
            for w in near:
                line = slice(w * GX, (w + 1) * GX)
                sides.append(jnp.concatenate([y0_ref[line, :], y1_ref[line, :]], axis=0))
            field = dot(tx_ref[...], jnp.concatenate(split(jnp.concatenate(sides, axis=1)), axis=0))
            pot = jnp.concatenate([pot_ref[w] for w in near], axis=1)
            field = (field[: 2 * size] + field[2 * size :]) * jnp.concatenate([pot, pot], axis=0)
            high, low = split(field)
            back = dot(txb_ref[...], high)
            back = back[: 2 * GX] + back[2 * GX :] + dot(txb_ref[: 2 * GX], low)
            for w in near:
                for p in range(2):
                    at = 128 * (w - z)
                    back_ref[w * GX : (w + 1) * GX, 128 * p : 128 * p + 128] = back[
                        p * GX : (p + 1) * GX, at : at + 128
                    ]
        part = slice(first * GX, last * GX)
        high, low = split(back_ref[part])
        moved = dot(high, tyb_ref[...])
        q_ref[part] = moved[:, :128] + moved[:, 128:] + dot(low, tyb_ref[:, :128])

    for s in range(slots):
        re, im = jnp.zeros((pad, 128), F32), jnp.zeros((pad, 128), F32)
        for i, (width, slot, middle) in enumerate(places):
            if slot != s:
                continue
            value = q_ref[pl.ds(i, pad, stride=GX), :]
            here = between(middle - width, middle + width)
            re = jnp.where(here, pltpu.roll(value, (middle - radius) % 128, 1), re)
            im = jnp.where(here, pltpu.roll(value, (middle - radius - GY) % 128, 1), im)
        box_ref[:, 128 * s : 128 * s + 128] = jnp.concatenate(split(jnp.concatenate([re, im], axis=0)), axis=0)

    box = box_ref[...]
    for k in range(devices - 1):
        gather(box, marks[k], outs[k], slots)


def body(devices, bands, psi, col_map, potential, lower, upper):
    cols, size = psi.shape[2], psi.shape[3]
    radius = size // 4
    depth = size // devices
    pad = round_up(depth, 8)
    rows = 2 * pad
    me = lax.axis_index("grid")
    me_arg = me.astype(jnp.int32).reshape(1)
    if devices & (devices - 1):
        raise ValueError("mesh size")

    def step(at, k):
        return at ^ k

    def exchange(values):
        return [values[0]] + [
            lax.ppermute(values[k], "grid", [(d, step(d, k)) for d in range(devices)]) for k in range(1, devices)
        ]

    ahead, back = z_tables(size, devices, pad)
    tables = plane_tables(size)
    count = 2 * radius + 1
    slots = round_up(-(-count // bands), 8)
    pick = np.zeros((2, bands * 2 * slots, sum(kept(size))), ml_dtypes.bfloat16)
    for j in range(count):
        at = (j % bands) * 2 * slots + j // bands
        pick[0, at, (j - radius) % sum(kept(size))] = 1
        pick[1, at + slots, (j - radius) % sum(kept(size))] = 1

    pot = (potential * (1.0 / float(size**3))).reshape(depth, size, size)
    pot = jnp.pad(pot, ((0, 0), (0, 0), (0, 128 - size)))
    psi_t = jnp.transpose(psi.reshape(2, cols, size), (0, 2, 1))
    col_row = col_map.reshape(1, cols)

    def vmem(shape, dtype=F32):
        return pltpu.VMEM(shape, dtype)

    marks = exchange(
        call(
            functools.partial(first_kernel, devices, step, size),
            [vmem((rows + 8, cols))] * devices,
            [me_arg],
            [(psi_t, True), (col_row, True), (ahead, True)],
            [
                pltpu.VMEM((2, sum(kept(size)), cols), F32),
                pltpu.VMEM(col_row.shape, jnp.int32),
                pltpu.VMEM(ahead.shape, BF16),
                pltpu.SemaphoreType.DMA((6,)),
            ],
            far=True,
        )
    )

    slots_all = packing(size)[1]
    box_shape = (rows, 128 * slots_all)

    def slab(values):
        order = [0] + list(range(devices - 1, 0, -1))
        sums = []
        for k in order[:-1]:
            sums = call(
                functools.partial(scatter_kernel, slots_all),
                [vmem(box_shape)],
                [],
                [(value, True) for value in [values[k], marks[k]] + list(sums)],
            )
        given = [values[1], sums[0]] + marks[1:]
        *sent, box = call(
            functools.partial(slab_kernel, devices, size, depth),
            [vmem((rows, cols))] * (devices - 1) + [vmem((2 * rows, 128 * slots_all), BF16)],
            [],
            [(value, True) for value in given] + [(pot, False)] + [(table, False) for table in tables],
            [
                pltpu.VMEM((GX * pad, 128), F32),
                pltpu.VMEM((GX * pad, 128), F32),
                pltpu.VMEM((GX * pad, 128), F32),
                pltpu.VMEM((pad * GX, 256), F32),
                pltpu.VMEM((pad * GX, 128), F32),
            ],
        )
        own = call(
            functools.partial(gather_kernel, slots_all),
            [vmem((rows, cols))],
            [],
            [(box, True), (marks[0], True)],
        )
        return list(own) + list(sent)

    held = pltpu.VMEM((3 * devices * rows, cols), BF16)
    planes = exchange(slab(marks))
    first, *sent = call(
        functools.partial(middle_kernel, devices, step, size),
        [vmem((2, sum(kept(size)), cols))] + [vmem((rows, cols))] * devices,
        [me_arg, lower, upper],
        [(value, True) for value in planes] + [(psi_t, False), (col_row, False), (ahead, False), (back, False)],
        [held],
    )
    planes = exchange(slab(exchange(sent)))
    filtered, packed = call(
        functools.partial(last_kernel, devices, bands, step, size),
        [vmem((2, size, cols)), vmem((bands, 2 * slots, cols), BF16)],
        [me_arg, lower, upper],
        [(value, True) for value in planes]
        + [(psi_t, False), (first, True), (col_row, False), (back, False), (pick, False)],
        [held],
    )
    partial_sum, _ = call(
        functools.partial(gram_kernel, bands),
        [vmem((devices * bands, 1, 128)), vmem((bands, 128))],
        [],
        [(lax.all_to_all(packed, "band", 0, 0, tiled=True), True)],
    )
    own = bands // devices
    (gram,) = call(
        functools.partial(total_kernel, own, 1.0 / (4.0 * radius**3)),
        [jax.ShapeDtypeStruct((2, 1, own), F32)],
        [me_arg],
        [(lax.all_to_all(partial_sum, ("grid", "band"), 0, 0, tiled=True), True)],
    )
    return jnp.transpose(filtered, (0, 2, 1)).reshape(psi.shape), gram


def solution(mesh):
    return jax.shard_map(
        functools.partial(body, mesh.shape["grid"], mesh.shape["band"]),
        mesh=mesh,
        in_specs=(P(None, "band", "grid", None), P("grid"), P("grid", None), P(), P()),
        out_specs=(P(None, "band", "grid", None), P(None, "band", "grid")),
        check_vma=False,
    )
```

```python
import functools

import jax
import jax.numpy as jnp
import ml_dtypes
import numpy as np
from jax import lax
from jax.experimental import pallas as pl
from jax.experimental.pallas import tpu as pltpu
from jax.sharding import PartitionSpec as P

GY = 64
GX = 56
F32 = jnp.float32
BF16 = jnp.bfloat16
MIB = 1024 * 1024


def round_up(value, unit):
    return -(-value // unit) * unit


def halves(table):
    table = np.asarray(table, np.float32)
    high = table.astype(ml_dtypes.bfloat16)
    low = (table - high.astype(np.float32)).astype(ml_dtypes.bfloat16)
    return high, low


def stacked_table(table, axis):
    high, low = halves(table)
    return np.concatenate([high, high, low], axis=axis)


def folded(index, size):
    return np.where(index < size // 2, index, index - size)


def kept(size):
    radius = size // 4
    return round_up(radius + 1, 8), radius


def z_tables(size, devices, pad):
    depth = size // devices
    rows = 2 * pad
    first, last = kept(size)
    count = first + last
    freq = np.concatenate([np.arange(first), np.arange(size - last, size)])
    ahead = np.zeros((devices, rows, 2 * count))
    back = np.zeros((2 * count, devices * rows))
    for d in range(devices):
        plane = d * depth + np.arange(depth)
        angle = 2 * np.pi * ((plane[:, None] * freq[None, :]) % size) / size
        c, s = np.cos(angle), np.sin(angle)
        ahead[d, :depth, :count], ahead[d, :depth, count:] = c, -s
        ahead[d, pad : pad + depth, :count], ahead[d, pad : pad + depth, count:] = s, c
        at = d * rows
        back[:count, at : at + depth], back[:count, at + pad : at + pad + depth] = c.T, s.T
        back[count:, at : at + depth], back[count:, at + pad : at + pad + depth] = -s.T, c.T
    return stacked_table(ahead, 2), stacked_table(back, 1)


def plane_tables(size):
    radius = size // 4
    count = 2 * radius + 1
    freq = np.arange(count) - radius
    angle = 2 * np.pi * ((freq[:, None] * np.arange(size)[None, :]) % size) / size
    c, s = np.cos(angle), np.sin(angle)
    ty = np.zeros((2 * GY, 256))
    ty[:count, :size], ty[:count, 128 : 128 + size] = c, s
    ty[GY : GY + count, :size], ty[GY : GY + count, 128 : 128 + size] = -s, c
    tyb = np.zeros((256, 2 * GY))
    tyb[:size, :count], tyb[:size, GY : GY + count] = c.T, -s.T
    tyb[128 : 128 + size, :count], tyb[128 : 128 + size, GY : GY + count] = s.T, c.T
    tx = np.zeros((2 * size, 2 * GX))
    tx[:size, :count], tx[:size, GX : GX + count] = c.T, -s.T
    tx[size:, :count], tx[size:, GX : GX + count] = s.T, c.T
    txb = np.zeros((2 * GX, 2 * size))
    txb[:count, :size], txb[:count, size:] = c, s
    txb[GX : GX + count, :size], txb[GX : GX + count, size:] = -s, c
    high, low = halves(tx)
    tx = np.concatenate([np.concatenate([high, high], 1), np.concatenate([low, 0 * low], 1)], 0)
    return stacked_table(ty, 0), tx, np.concatenate(halves(txb), 0), np.concatenate(halves(tyb), 1)


def packing(size):
    radius = size // 4
    widths = [int(np.sqrt(radius * radius - g * g)) for g in range(-radius, radius + 1)]
    slots, free = [None] * len(widths), []
    for i in sorted(range(len(widths)), key=lambda j: (-widths[j], j)):
        span = 2 * widths[i] + 1
        for s in range(len(free) + 1):
            if s == len(free):
                free.append(128)
            if free[s] >= span:
                slots[i] = (widths[i], s, 128 - free[s] + widths[i])
                free[s] -= span
                break
    return slots, round_up(len(free), 2)


def split(value):
    high = value.astype(BF16)
    low = (value - high.astype(F32)).astype(BF16)
    return high, low


def tripled(value, axis):
    high, low = split(value)
    return jnp.concatenate([high, low, high], axis=axis)


def dot(a, b, dims=((1,), (0,))):
    return lax.dot_general(a, b, (dims, ((), ())), preferred_element_type=F32)


SMEM = pl.BlockSpec(memory_space=pltpu.SMEM)
VMEM = pl.BlockSpec(memory_space=pltpu.VMEM)
HBM = pl.BlockSpec(memory_space=pltpu.HBM)


def call(kernel, out_shape, scalars, arrays, scratch=(), limit=24, far=False):
    space = pltpu.HBM if far else pltpu.VMEM
    arrays = [pltpu.with_memory_space_constraint(value, space) if keep else value for value, keep in arrays]
    return pl.pallas_call(
        kernel,
        out_shape=out_shape,
        in_specs=[SMEM] * len(scalars) + [HBM if far else VMEM] * len(arrays),
        out_specs=[VMEM] * len(out_shape),
        scratch_shapes=list(scratch),
        compiler_params=pltpu.CompilerParams(vmem_limit_bytes=limit * MIB),
    )(*scalars, *arrays)


def position(col_row, size):
    place = col_row.astype(F32)
    kx = jnp.floor((place + 0.5) * (1.0 / size))
    ky = place - kx * size
    half = float(size // 2)
    return jnp.where(kx < half, kx, kx - size), jnp.where(ky < half, ky, ky - size)


def sphere(col_row, size):
    cols = col_row.shape[1]
    radius = size // 4
    gx, gy = position(col_row, size)
    first, last = kept(size)
    index = lax.broadcasted_iota(jnp.int32, (first + last, cols), 0)
    freq = jnp.where(index < first, index, index - (first + last)).astype(F32)
    radius2 = (gx * gx + gy * gy) + freq * freq
    return radius2 <= float(radius * radius), radius2 * (2.0 / (radius * radius))


def kept_rows(ref, p, size):
    first, last = kept(size)
    return jnp.concatenate([ref[p, :first], ref[p, size - last :]], axis=0)


def to_planes(me, parts, table_ref, outs, step):
    value = tripled(jnp.concatenate(parts, axis=0), 0)
    table = jnp.concatenate([table_ref[step(me, k)] for k in range(len(outs))], axis=0)
    total = dot(table, value)
    rows = table_ref.shape[1]
    for k in range(len(outs)):
        outs[k][:rows] = total[k * rows : (k + 1) * rows]


def from_planes(me, planes, table_ref, held, step, size):
    rows = planes[0].shape[0]
    third = rows * len(planes)
    for k in range(len(planes)):
        high, low = split(planes[k][...])
        at = step(me, k) * rows
        for j, value in enumerate((high, low, high)):
            held[pl.ds(pl.multiple_of(j * third + at, 16), rows), :] = value
    total = dot(table_ref[...], held[...])
    return total[: sum(kept(size))], total[sum(kept(size)) :]


def first_kernel(devices, step, size, me_ref, *refs):
    far, refs = refs[:3], refs[3:]
    outs, (psi_ref, col_ref, ahead_ref, sems) = refs[:devices], refs[devices:]
    first, last = kept(size)
    pairs = [(far[1], col_ref), (far[2], ahead_ref)]
    for p in range(2):
        pairs.append((far[0].at[p, :first], psi_ref.at[p, :first]))
        pairs.append((far[0].at[p, size - last :], psi_ref.at[p, first:]))
    copies = [pltpu.make_async_copy(source, target, sems.at[i]) for i, (source, target) in enumerate(pairs)]
    for copy in copies:
        copy.start()
    copies[0].wait()
    radius = size // 4
    gx, gy = position(col_ref[...], size)
    used = gx * gx + gy * gy <= float(radius * radius)
    rows = ahead_ref.shape[1]
    row = lax.broadcasted_iota(jnp.int32, (8, gx.shape[1]), 0)
    slot, lane = jnp.zeros(row.shape, F32), jnp.zeros(row.shape, F32)
    for i, (_, s, middle) in enumerate(packing(size)[0]):
        here = gx == float(i - radius)
        slot, lane = jnp.where(here, float(s), slot), jnp.where(here, float(middle), lane)
    place = jnp.where(used, jnp.where(row == 0, slot, lane + gy), -9.0)
    for k in range(devices):
        outs[k][rows:] = place
    inside, _ = sphere(col_ref[...], size)
    for copy in copies[1:]:
        copy.wait()
    parts = [jnp.where(inside, psi_ref[p], 0.0) for p in range(2)]
    to_planes(me_ref[0], parts, ahead_ref, outs, step)


def middle_kernel(devices, step, size, me_ref, low_ref, up_ref, *refs):
    planes, refs = refs[:devices], refs[devices:]
    psi_ref, col_ref, ahead_ref, back_ref, first_ref = refs[:5]
    outs, held = refs[5 : 5 + devices], refs[5 + devices]
    center = (up_ref[0] + low_ref[0]) / 2.0
    half = (up_ref[0] - low_ref[0]) / 2.0
    inside, kinetic = sphere(col_ref[...], size)
    back = from_planes(me_ref[0], planes, back_ref, held, step, size)
    parts = []
    for p in range(2):
        value = jnp.where(inside, ((kinetic - center) * kept_rows(psi_ref, p, size) + back[p]) / half, 0.0)
        first_ref[p] = value
        parts.append(value)
    to_planes(me_ref[0], parts, ahead_ref, outs, step)


def last_kernel(devices, bands, step, size, me_ref, low_ref, up_ref, *refs):
    planes, refs = refs[:devices], refs[devices:]
    psi_ref, first_ref, col_ref, back_ref, pick_ref, filtered_ref, packed_ref, held = refs
    center = (up_ref[0] + low_ref[0]) / 2.0
    half = (up_ref[0] - low_ref[0]) / 2.0
    inside, kinetic = sphere(col_ref[...], size)
    back = from_planes(me_ref[0], planes, back_ref, held, step, size)
    first, last = kept(size)
    total = None
    for p in range(2):
        value = 2.0 * ((kinetic - center) * first_ref[p] + back[p]) / half - kept_rows(psi_ref, p, size)
        value = jnp.where(inside, value, 0.0)
        filtered_ref[p, :first] = value[:first]
        filtered_ref[p, first : size - last] = jnp.zeros((size - last - first, value.shape[1]), F32)
        filtered_ref[p, size - last :] = value[first:]
        piece = dot(pick_ref[p], value.astype(BF16))
        total = piece if total is None else total + piece
    rows = packed_ref.shape[1]
    for k in range(bands):
        packed_ref[k] = total[k * rows : (k + 1) * rows].astype(BF16)


def rest(value, unit):
    return value & (unit - 1) if unit & (unit - 1) == 0 else value % unit


def gram_kernel(bands, parts_ref, sum_ref, spare_ref):
    rows, cols = parts_ref.shape[1:]
    count = bands * rows
    stacked = parts_ref[...].reshape(count, cols)
    product = dot(stacked, stacked, ((1,), (1,)))
    down = lax.broadcasted_iota(jnp.int32, (count, count), 0)
    along = lax.broadcasted_iota(jnp.int32, (count, count), 1)
    down, along = rest(down, rows), rest(along, rows)
    real = jnp.where(down == along, product, 0.0)
    imag = jnp.where(along == down + rows // 2, product, jnp.where(down == along + rows // 2, -product, 0.0))
    place = lax.broadcasted_iota(jnp.int32, (count, 128), 0)
    spot = lax.broadcasted_iota(jnp.int32, (count, 128), 1) * rows
    pieces, places = [], []
    for p, value in enumerate((real, imag)):
        value = jnp.sum(value.reshape(bands, rows, count), axis=1)
        gap = place + p * GY * rows - spot
        hot = jnp.where((gap >= 0) & (gap < rows), 1.0, 0.0).astype(BF16)
        for _ in range(3):
            pieces.append(value.astype(BF16))
            value = value - pieces[-1].astype(F32)
            places.append(hot)
    value = dot(jnp.concatenate(pieces, axis=1), jnp.concatenate(places, axis=0))
    for g in range(sum_ref.shape[0] // bands):
        sum_ref[g * bands : (g + 1) * bands, 0, :] = value
    spare_ref[...] = value


def total_kernel(own, scale, me_ref, parts_ref, out_ref):
    value = jnp.sum(parts_ref[...], axis=0) * scale
    value = pltpu.roll(value, lax.rem(128 - me_ref[0] * own, 128), 1)
    out_ref[0] = value[:, :own]
    out_ref[1] = value[:, GY : GY + own]


def scatter(plane_ref, mark_ref, slots):
    rows, cols = mark_ref.shape[0] - 8, mark_ref.shape[1]
    row = lax.broadcasted_iota(jnp.int32, (8, 256), 0)
    side = lax.broadcasted_iota(jnp.int32, (8, 256), 1) // 128
    spread = jnp.where(row == side, 1.0, 0.0).astype(BF16)
    both = dot(mark_ref[rows:].astype(BF16), spread, ((0,), (0,)))
    slot = both[:, :128].astype(BF16)
    along = lax.broadcasted_iota(jnp.int32, (cols, 128), 1).astype(F32)
    spot = jnp.where(both[:, 128:] == along, 1.0, 0.0).astype(BF16)
    lhs = jnp.concatenate(split(plane_ref[:rows]), axis=0)
    zero = jnp.zeros((), BF16)
    for t in range(0, slots, 2):
        hot = [jnp.where(slot == float(v), spot, zero) for v in (t, t + 1)]
        got = dot(lhs, jnp.concatenate(hot, axis=1))
        yield t, got[:rows] + got[rows:]


def gather(box, mark_ref, out_ref, slots):
    rows, cols = mark_ref.shape[0] - 8, mark_ref.shape[1]
    zero = jnp.zeros((), BF16)
    wide = min(512, cols)
    for at in range(0, cols, wide):
        slot = jnp.broadcast_to(mark_ref[rows : rows + 1, at : at + wide], (16, wide)).astype(BF16)
        spot = jnp.broadcast_to(mark_ref[rows + 1 : rows + 2, at : at + wide], (128, wide))
        down = lax.broadcasted_iota(jnp.int32, (128, wide), 0).astype(F32)
        hot = jnp.where(spot == down, 1.0, 0.0).astype(BF16)
        tall = []
        for v in range(slots):
            here = slot == float(v)
            tall += [jnp.where(here, hot[16 * i : 16 * i + 16], zero) for i in range(8)]
        got = dot(box, jnp.concatenate(tall, axis=0))
        out_ref[:, at : at + wide] = got[:rows] + got[rows:]


def scatter_kernel(slots, plane_ref, mark_ref, *refs):
    before, after = refs[:-1], refs[-1]
    for t, tile in scatter(plane_ref, mark_ref, slots):
        here = slice(128 * t, 128 * t + 256)
        after[:, here] = tile + before[0][:, here] if before else tile


def gather_kernel(slots, box_ref, mark_ref, out_ref):
    gather(box_ref[...], mark_ref, out_ref, slots)


def slab_kernel(devices, size, depth, plane_ref, before_ref, *refs):
    marks, refs = refs[: devices - 1], refs[devices - 1 :]
    pot_ref, ty_ref, tx_ref, txb_ref, tyb_ref = refs[:5]
    outs, box_ref = refs[5 : 4 + devices], refs[4 + devices]
    in_ref, y0_ref, y1_ref, back_ref, q_ref = refs[5 + devices :]
    pad = round_up(depth, 8)
    radius = size // 4
    places, slots = packing(size)
    lane = lax.broadcasted_iota(jnp.int32, (pad, 128), 1)

    def between(first, last):
        return (lane >= first) & (lane <= last)

    in_ref[...] = jnp.zeros(in_ref.shape, F32)
    for t, tile in scatter(plane_ref, marks[-1], slots):
        got = tile + before_ref[:, 128 * t : 128 * t + 256]
        for i, (width, slot, middle) in enumerate(places):
            if slot // 2 * 2 != t:
                continue
            at = 128 * (slot - t)
            re = pltpu.roll(got[:pad, at : at + 128], (radius - middle) % 128, 1)
            im = pltpu.roll(got[pad:, at : at + 128], (radius + GY - middle) % 128, 1)
            im = jnp.where(between(GY + radius - width, GY + radius + width), im, 0.0)
            in_ref[pl.ds(i, pad, stride=GX), :] = jnp.where(between(radius - width, radius + width), re, im)
    moved = dot(tripled(in_ref[...], 1), ty_ref[...])
    y0_ref[...] = moved[:, :128]
    y1_ref[...] = moved[:, 128:]
    if depth < pad:
        q_ref[depth * GX :] = jnp.zeros(((pad - depth) * GX, 128), F32)

    chunk, group = 8, 4
    for first in range(0, depth, chunk):
        last = min(depth, first + chunk)
        for z in range(first, last, group):
            near = range(z, min(z + group, last))
            sides = []
            for w in near:
                line = slice(w * GX, (w + 1) * GX)
                sides.append(jnp.concatenate([y0_ref[line, :], y1_ref[line, :]], axis=0))
            field = dot(tx_ref[...], jnp.concatenate(split(jnp.concatenate(sides, axis=1)), axis=0))
            pot = jnp.concatenate([pot_ref[w] for w in near], axis=1)
            field = (field[: 2 * size] + field[2 * size :]) * jnp.concatenate([pot, pot], axis=0)
            high, low = split(field)
            back = dot(txb_ref[...], high)
            back = back[: 2 * GX] + back[2 * GX :] + dot(txb_ref[: 2 * GX], low)
            for w in near:
                for p in range(2):
                    at = 128 * (w - z)
                    back_ref[w * GX : (w + 1) * GX, 128 * p : 128 * p + 128] = back[
                        p * GX : (p + 1) * GX, at : at + 128
                    ]
        part = slice(first * GX, last * GX)
        high, low = split(back_ref[part])
        moved = dot(high, tyb_ref[...])
        q_ref[part] = moved[:, :128] + moved[:, 128:] + dot(low, tyb_ref[:, :128])

    for s in range(slots):
        re, im = jnp.zeros((pad, 128), F32), jnp.zeros((pad, 128), F32)
        for i, (width, slot, middle) in enumerate(places):
            if slot != s:
                continue
            value = q_ref[pl.ds(i, pad, stride=GX), :]
            here = between(middle - width, middle + width)
            re = jnp.where(here, pltpu.roll(value, (middle - radius) % 128, 1), re)
            im = jnp.where(here, pltpu.roll(value, (middle - radius - GY) % 128, 1), im)
        box_ref[:, 128 * s : 128 * s + 128] = jnp.concatenate(split(jnp.concatenate([re, im], axis=0)), axis=0)

    box = box_ref[...]
    for k in range(devices - 1):
        gather(box, marks[k], outs[k], slots)


def body(devices, bands, psi, col_map, potential, lower, upper):
    cols, size = psi.shape[2], psi.shape[3]
    radius = size // 4
    depth = size // devices
    pad = round_up(depth, 8)
    rows = 2 * pad
    me = lax.axis_index("grid")
    me_arg = me.astype(jnp.int32).reshape(1)
    if devices & (devices - 1):
        raise ValueError("mesh size")

    def step(at, k):
        return at ^ k

    def exchange(values):
        moved = [
            lax.ppermute(values[k], "grid", [(d, step(d, k)) for d in range(devices)])
            for k in range(devices - 1, 0, -1)
        ]
        return [values[0]] + moved[::-1]

    ahead, back = z_tables(size, devices, pad)
    tables = plane_tables(size)
    count = 2 * radius + 1
    slots = round_up(-(-count // bands), 8)
    pick = np.zeros((2, bands * 2 * slots, sum(kept(size))), ml_dtypes.bfloat16)
    for j in range(count):
        at = (j % bands) * 2 * slots + j // bands
        pick[0, at, (j - radius) % sum(kept(size))] = 1
        pick[1, at + slots, (j - radius) % sum(kept(size))] = 1

    pot = (potential * (1.0 / float(size**3))).reshape(depth, size, size)
    pot = jnp.pad(pot, ((0, 0), (0, 0), (0, 128 - size)))
    psi_t = jnp.transpose(psi.reshape(2, cols, size), (0, 2, 1))
    col_row = col_map.reshape(1, cols)

    def vmem(shape, dtype=F32):
        return pltpu.VMEM(shape, dtype)

    marks = exchange(
        call(
            functools.partial(first_kernel, devices, step, size),
            [vmem((rows + 8, cols))] * devices,
            [me_arg],
            [(psi_t, True), (col_row, True), (ahead, True)],
            [
                pltpu.VMEM((2, sum(kept(size)), cols), F32),
                pltpu.VMEM(col_row.shape, jnp.int32),
                pltpu.VMEM(ahead.shape, BF16),
                pltpu.SemaphoreType.DMA((6,)),
            ],
            far=True,
        )
    )

    slots_all = packing(size)[1]
    box_shape = (rows, 128 * slots_all)

    def slab(values):
        order = [0] + list(range(devices - 1, 0, -1))
        sums = []
        for k in order[:-1]:
            sums = call(
                functools.partial(scatter_kernel, slots_all),
                [vmem(box_shape)],
                [],
                [(value, True) for value in [values[k], marks[k]] + list(sums)],
            )
        given = [values[order[-1]], sums[0]] + [marks[k] for k in order[1:]]
        *sent, box = call(
            functools.partial(slab_kernel, devices, size, depth),
            [vmem((rows, cols))] * (devices - 1) + [vmem((2 * rows, 128 * slots_all), BF16)],
            [],
            [(value, True) for value in given] + [(pot, False)] + [(table, False) for table in tables],
            [
                pltpu.VMEM((GX * pad, 128), F32),
                pltpu.VMEM((GX * pad, 128), F32),
                pltpu.VMEM((GX * pad, 128), F32),
                pltpu.VMEM((pad * GX, 256), F32),
                pltpu.VMEM((pad * GX, 128), F32),
            ],
        )
        own = call(
            functools.partial(gather_kernel, slots_all),
            [vmem((rows, cols))],
            [],
            [(box, True), (marks[0], True)],
        )
        return list(own) + [sent[order.index(k) - 1] for k in range(1, devices)]

    held = pltpu.VMEM((3 * devices * rows, cols), BF16)
    planes = exchange(slab(marks))
    first, *sent = call(
        functools.partial(middle_kernel, devices, step, size),
        [vmem((2, sum(kept(size)), cols))] + [vmem((rows, cols))] * devices,
        [me_arg, lower, upper],
        [(value, True) for value in planes] + [(psi_t, False), (col_row, False), (ahead, False), (back, False)],
        [held],
    )
    planes = exchange(slab(exchange(sent)))
    filtered, packed = call(
        functools.partial(last_kernel, devices, bands, step, size),
        [vmem((2, size, cols)), vmem((bands, 2 * slots, cols), BF16)],
        [me_arg, lower, upper],
        [(value, True) for value in planes]
        + [(psi_t, False), (first, True), (col_row, False), (back, False), (pick, False)],
        [held],
    )
    partial_sum, _ = call(
        functools.partial(gram_kernel, bands),
        [vmem((devices * bands, 1, 128)), vmem((bands, 128))],
        [],
        [(lax.all_to_all(packed, "band", 0, 0, tiled=True), True)],
    )
    own = bands // devices
    (gram,) = call(
        functools.partial(total_kernel, own, 1.0 / (4.0 * radius**3)),
        [jax.ShapeDtypeStruct((2, 1, own), F32)],
        [me_arg],
        [(lax.all_to_all(partial_sum, ("grid", "band"), 0, 0, tiled=True), True)],
    )
    return jnp.transpose(filtered, (0, 2, 1)).reshape(psi.shape), gram


def solution(mesh):
    return jax.shard_map(
        functools.partial(body, mesh.shape["grid"], mesh.shape["band"]),
        mesh=mesh,
        in_specs=(P(None, "band", "grid", None), P("grid"), P("grid", None), P(), P()),
        out_specs=(P(None, "band", "grid", None), P(None, "band", "grid")),
        check_vma=False,
    )
```

```python
import functools

import jax
import jax.numpy as jnp
import ml_dtypes
import numpy as np
from jax import lax
from jax.experimental import pallas as pl
from jax.experimental.pallas import tpu as pltpu
from jax.sharding import PartitionSpec as P

GY = 64
GX = 56
F32 = jnp.float32
BF16 = jnp.bfloat16
MIB = 1024 * 1024


def round_up(value, unit):
    return -(-value // unit) * unit


def halves(table):
    table = np.asarray(table, np.float32)
    high = table.astype(ml_dtypes.bfloat16)
    low = (table - high.astype(np.float32)).astype(ml_dtypes.bfloat16)
    return high, low


def stacked_table(table, axis):
    high, low = halves(table)
    return np.concatenate([high, high, low], axis=axis)


def folded(index, size):
    return np.where(index < size // 2, index, index - size)


def kept(size):
    radius = size // 4
    return round_up(radius + 1, 8), radius


def z_tables(size, devices, pad):
    depth = size // devices
    rows = 2 * pad
    first, last = kept(size)
    count = first + last
    freq = np.concatenate([np.arange(first), np.arange(size - last, size)])
    ahead = np.zeros((devices, rows, 2 * count))
    back = np.zeros((2 * count, devices * rows))
    for d in range(devices):
        plane = d * depth + np.arange(depth)
        angle = 2 * np.pi * ((plane[:, None] * freq[None, :]) % size) / size
        c, s = np.cos(angle), np.sin(angle)
        ahead[d, :depth, :count], ahead[d, :depth, count:] = c, -s
        ahead[d, pad : pad + depth, :count], ahead[d, pad : pad + depth, count:] = s, c
        at = d * rows
        back[:count, at : at + depth], back[:count, at + pad : at + pad + depth] = c.T, s.T
        back[count:, at : at + depth], back[count:, at + pad : at + pad + depth] = -s.T, c.T
    return stacked_table(ahead, 2), stacked_table(back, 1)


def plane_tables(size):
    radius = size // 4
    count = 2 * radius + 1
    freq = np.arange(count) - radius
    angle = 2 * np.pi * ((freq[:, None] * np.arange(size)[None, :]) % size) / size
    c, s = np.cos(angle), np.sin(angle)
    ty = np.zeros((2 * GY, 256))
    ty[:count, :size], ty[:count, 128 : 128 + size] = c, s
    ty[GY : GY + count, :size], ty[GY : GY + count, 128 : 128 + size] = -s, c
    tyb = np.zeros((256, 2 * GY))
    tyb[:size, :count], tyb[:size, GY : GY + count] = c.T, -s.T
    tyb[128 : 128 + size, :count], tyb[128 : 128 + size, GY : GY + count] = s.T, c.T
    tx = np.zeros((2 * size, 2 * GX))
    tx[:size, :count], tx[:size, GX : GX + count] = c.T, -s.T
    tx[size:, :count], tx[size:, GX : GX + count] = s.T, c.T
    txb = np.zeros((2 * GX, 2 * size))
    txb[:count, :size], txb[:count, size:] = c, s
    txb[GX : GX + count, :size], txb[GX : GX + count, size:] = -s, c
    high, low = halves(tx)
    tx = np.concatenate([np.concatenate([high, high], 1), np.concatenate([low, 0 * low], 1)], 0)
    return stacked_table(ty, 0), tx, np.concatenate(halves(txb), 0), np.concatenate(halves(tyb), 1)


def packing(size):
    radius = size // 4
    widths = [int(np.sqrt(radius * radius - g * g)) for g in range(-radius, radius + 1)]
    slots, free = [None] * len(widths), []
    for i in sorted(range(len(widths)), key=lambda j: (-widths[j], j)):
        span = 2 * widths[i] + 1
        for s in range(len(free) + 1):
            if s == len(free):
                free.append(128)
            if free[s] >= span:
                slots[i] = (widths[i], s, 128 - free[s] + widths[i])
                free[s] -= span
                break
    return slots, round_up(len(free), 2)


def split(value):
    high = value.astype(BF16)
    low = (value - high.astype(F32)).astype(BF16)
    return high, low


def tripled(value, axis):
    high, low = split(value)
    return jnp.concatenate([high, low, high], axis=axis)


def dot(a, b, dims=((1,), (0,))):
    return lax.dot_general(a, b, (dims, ((), ())), preferred_element_type=F32)


SMEM = pl.BlockSpec(memory_space=pltpu.SMEM)
VMEM = pl.BlockSpec(memory_space=pltpu.VMEM)
HBM = pl.BlockSpec(memory_space=pltpu.HBM)


def call(kernel, out_shape, scalars, arrays, scratch=(), limit=24, far=False):
    space = pltpu.HBM if far else pltpu.VMEM
    arrays = [pltpu.with_memory_space_constraint(value, space) if keep else value for value, keep in arrays]
    return pl.pallas_call(
        kernel,
        out_shape=out_shape,
        in_specs=[SMEM] * len(scalars) + [HBM if far else VMEM] * len(arrays),
        out_specs=[VMEM] * len(out_shape),
        scratch_shapes=list(scratch),
        compiler_params=pltpu.CompilerParams(vmem_limit_bytes=limit * MIB),
    )(*scalars, *arrays)


def position(col_row, size):
    place = col_row.astype(F32)
    kx = jnp.floor((place + 0.5) * (1.0 / size))
    ky = place - kx * size
    half = float(size // 2)
    return jnp.where(kx < half, kx, kx - size), jnp.where(ky < half, ky, ky - size)


def sphere(col_row, size):
    cols = col_row.shape[1]
    radius = size // 4
    gx, gy = position(col_row, size)
    first, last = kept(size)
    index = lax.broadcasted_iota(jnp.int32, (first + last, cols), 0)
    freq = jnp.where(index < first, index, index - (first + last)).astype(F32)
    radius2 = (gx * gx + gy * gy) + freq * freq
    return radius2 <= float(radius * radius), radius2 * (2.0 / (radius * radius))


def kept_rows(ref, p, size):
    first, last = kept(size)
    return jnp.concatenate([ref[p, :first], ref[p, size - last :]], axis=0)


def to_planes(me, parts, table_ref, outs, step):
    value = tripled(jnp.concatenate(parts, axis=0), 0)
    table = jnp.concatenate([table_ref[step(me, k)] for k in range(len(outs))], axis=0)
    total = dot(table, value)
    rows = table_ref.shape[1]
    for k in range(len(outs)):
        outs[k][:rows] = total[k * rows : (k + 1) * rows]


def from_planes(me, planes, table_ref, held, step, size):
    rows = planes[0].shape[0]
    third = rows * len(planes)
    for k in range(len(planes)):
        high, low = split(planes[k][...])
        at = step(me, k) * rows
        for j, value in enumerate((high, low, high)):
            held[pl.ds(pl.multiple_of(j * third + at, 16), rows), :] = value
    total = dot(table_ref[...], held[...])
    return total[: sum(kept(size))], total[sum(kept(size)) :]


def first_kernel(devices, step, size, me_ref, *refs):
    far, refs = refs[:3], refs[3:]
    outs, (psi_ref, col_ref, ahead_ref, sems) = refs[:devices], refs[devices:]
    first, last = kept(size)
    pairs = [(far[1], col_ref), (far[2], ahead_ref)]
    for p in range(2):
        pairs.append((far[0].at[p, :first], psi_ref.at[p, :first]))
        pairs.append((far[0].at[p, size - last :], psi_ref.at[p, first:]))
    copies = [pltpu.make_async_copy(source, target, sems.at[i]) for i, (source, target) in enumerate(pairs)]
    for copy in copies:
        copy.start()
    copies[0].wait()
    radius = size // 4
    gx, gy = position(col_ref[...], size)
    used = gx * gx + gy * gy <= float(radius * radius)
    rows = ahead_ref.shape[1]
    row = lax.broadcasted_iota(jnp.int32, (8, gx.shape[1]), 0)
    slot, lane = jnp.zeros(row.shape, F32), jnp.zeros(row.shape, F32)
    for i, (_, s, middle) in enumerate(packing(size)[0]):
        here = gx == float(i - radius)
        slot, lane = jnp.where(here, float(s), slot), jnp.where(here, float(middle), lane)
    place = jnp.where(used, jnp.where(row == 0, slot, lane + gy), -9.0)
    for k in range(devices):
        outs[k][rows:] = place
    inside, _ = sphere(col_ref[...], size)
    for copy in copies[1:]:
        copy.wait()
    parts = [jnp.where(inside, psi_ref[p], 0.0) for p in range(2)]
    to_planes(me_ref[0], parts, ahead_ref, outs, step)


def middle_kernel(devices, step, size, me_ref, low_ref, up_ref, *refs):
    planes, refs = refs[:devices], refs[devices:]
    psi_ref, col_ref, ahead_ref, back_ref, first_ref = refs[:5]
    outs, held = refs[5 : 5 + devices], refs[5 + devices]
    center = (up_ref[0] + low_ref[0]) / 2.0
    half = (up_ref[0] - low_ref[0]) / 2.0
    inside, kinetic = sphere(col_ref[...], size)
    back = from_planes(me_ref[0], planes, back_ref, held, step, size)
    parts = []
    for p in range(2):
        value = jnp.where(inside, ((kinetic - center) * kept_rows(psi_ref, p, size) + back[p]) / half, 0.0)
        first_ref[p] = value
        parts.append(value)
    to_planes(me_ref[0], parts, ahead_ref, outs, step)


def last_kernel(devices, bands, step, size, me_ref, low_ref, up_ref, *refs):
    planes, refs = refs[:devices], refs[devices:]
    psi_ref, first_ref, col_ref, back_ref, pick_ref, filtered_ref, packed_ref, held = refs
    center = (up_ref[0] + low_ref[0]) / 2.0
    half = (up_ref[0] - low_ref[0]) / 2.0
    inside, kinetic = sphere(col_ref[...], size)
    back = from_planes(me_ref[0], planes, back_ref, held, step, size)
    first, last = kept(size)
    total = None
    for p in range(2):
        value = 2.0 * ((kinetic - center) * first_ref[p] + back[p]) / half - kept_rows(psi_ref, p, size)
        value = jnp.where(inside, value, 0.0)
        filtered_ref[p, :first] = value[:first]
        filtered_ref[p, first : size - last] = jnp.zeros((size - last - first, value.shape[1]), F32)
        filtered_ref[p, size - last :] = value[first:]
        piece = dot(pick_ref[p], value.astype(BF16))
        total = piece if total is None else total + piece
    rows = packed_ref.shape[1]
    for k in range(bands):
        packed_ref[k] = total[k * rows : (k + 1) * rows].astype(BF16)


def rest(value, unit):
    return value & (unit - 1) if unit & (unit - 1) == 0 else value % unit


def gram_kernel(bands, parts_ref, sum_ref, spare_ref):
    rows, cols = parts_ref.shape[1:]
    count = bands * rows
    stacked = parts_ref[...].reshape(count, cols)
    product = dot(stacked, stacked, ((1,), (1,)))
    down = lax.broadcasted_iota(jnp.int32, (count, count), 0)
    along = lax.broadcasted_iota(jnp.int32, (count, count), 1)
    down, along = rest(down, rows), rest(along, rows)
    real = jnp.where(down == along, product, 0.0)
    imag = jnp.where(along == down + rows // 2, product, jnp.where(down == along + rows // 2, -product, 0.0))
    place = lax.broadcasted_iota(jnp.int32, (count, 128), 0)
    spot = lax.broadcasted_iota(jnp.int32, (count, 128), 1) * rows
    pieces, places = [], []
    for p, value in enumerate((real, imag)):
        value = jnp.sum(value.reshape(bands, rows, count), axis=1)
        gap = place + p * GY * rows - spot
        hot = jnp.where((gap >= 0) & (gap < rows), 1.0, 0.0).astype(BF16)
        for _ in range(3):
            pieces.append(value.astype(BF16))
            value = value - pieces[-1].astype(F32)
            places.append(hot)
    value = dot(jnp.concatenate(pieces, axis=1), jnp.concatenate(places, axis=0))
    for g in range(sum_ref.shape[0] // bands):
        sum_ref[g * bands : (g + 1) * bands, 0, :] = value
    spare_ref[...] = value


def total_kernel(own, scale, me_ref, parts_ref, out_ref):
    value = jnp.sum(parts_ref[...], axis=0) * scale
    value = pltpu.roll(value, lax.rem(128 - me_ref[0] * own, 128), 1)
    out_ref[0] = value[:, :own]
    out_ref[1] = value[:, GY : GY + own]


def scatter(plane_ref, mark_ref, slots):
    rows, cols = mark_ref.shape[0] - 8, mark_ref.shape[1]
    row = lax.broadcasted_iota(jnp.int32, (8, 256), 0)
    side = lax.broadcasted_iota(jnp.int32, (8, 256), 1) // 128
    spread = jnp.where(row == side, 1.0, 0.0).astype(BF16)
    both = dot(mark_ref[rows:].astype(BF16), spread, ((0,), (0,)))
    slot = both[:, :128].astype(BF16)
    along = lax.broadcasted_iota(jnp.int32, (cols, 128), 1).astype(F32)
    spot = jnp.where(both[:, 128:] == along, 1.0, 0.0).astype(BF16)
    lhs = jnp.concatenate(split(plane_ref[:rows]), axis=0)
    zero = jnp.zeros((), BF16)
    for t in range(0, slots, 2):
        hot = [jnp.where(slot == float(v), spot, zero) for v in (t, t + 1)]
        got = dot(lhs, jnp.concatenate(hot, axis=1))
        yield t, got[:rows] + got[rows:]


def gather(box, mark_ref, out_ref, slots):
    rows, cols = mark_ref.shape[0] - 8, mark_ref.shape[1]
    zero = jnp.zeros((), BF16)
    wide = min(512, cols)
    for at in range(0, cols, wide):
        slot = jnp.broadcast_to(mark_ref[rows : rows + 1, at : at + wide], (16, wide)).astype(BF16)
        spot = jnp.broadcast_to(mark_ref[rows + 1 : rows + 2, at : at + wide], (128, wide))
        down = lax.broadcasted_iota(jnp.int32, (128, wide), 0).astype(F32)
        hot = jnp.where(spot == down, 1.0, 0.0).astype(BF16)
        tall = []
        for v in range(slots):
            here = slot == float(v)
            tall += [jnp.where(here, hot[16 * i : 16 * i + 16], zero) for i in range(8)]
        got = dot(box, jnp.concatenate(tall, axis=0))
        out_ref[:, at : at + wide] = got[:rows] + got[rows:]


def scatter_kernel(slots, plane_ref, mark_ref, *refs):
    before, after = refs[:-1], refs[-1]
    for t, tile in scatter(plane_ref, mark_ref, slots):
        here = slice(128 * t, 128 * t + 256)
        after[:, here] = tile + before[0][:, here] if before else tile


def gather_kernel(slots, box_ref, mark_ref, out_ref):
    gather(box_ref[...], mark_ref, out_ref, slots)


def slab_kernel(devices, size, depth, plane_ref, before_ref, *refs):
    marks, refs = refs[: devices - 1], refs[devices - 1 :]
    pot_ref, ty_ref, tx_ref, txb_ref, tyb_ref = refs[:5]
    outs, box_ref = refs[5 : 4 + devices], refs[4 + devices]
    in_ref, y0_ref, y1_ref, back_ref, q_ref = refs[5 + devices :]
    pad = round_up(depth, 8)
    radius = size // 4
    places, slots = packing(size)
    lane = lax.broadcasted_iota(jnp.int32, (pad, 128), 1)

    def between(first, last):
        return (lane >= first) & (lane <= last)

    in_ref[...] = jnp.zeros(in_ref.shape, F32)
    for t, tile in scatter(plane_ref, marks[-1], slots):
        got = tile + before_ref[:, 128 * t : 128 * t + 256]
        for i, (width, slot, middle) in enumerate(places):
            if slot // 2 * 2 != t:
                continue
            at = 128 * (slot - t)
            re = pltpu.roll(got[:pad, at : at + 128], (radius - middle) % 128, 1)
            im = pltpu.roll(got[pad:, at : at + 128], (radius + GY - middle) % 128, 1)
            im = jnp.where(between(GY + radius - width, GY + radius + width), im, 0.0)
            in_ref[pl.ds(i, pad, stride=GX), :] = jnp.where(between(radius - width, radius + width), re, im)
    moved = dot(tripled(in_ref[...], 1), ty_ref[...])
    y0_ref[...] = moved[:, :128]
    y1_ref[...] = moved[:, 128:]
    if depth < pad:
        q_ref[depth * GX :] = jnp.zeros(((pad - depth) * GX, 128), F32)

    chunk, group = 8, 4
    for first in range(0, depth, chunk):
        last = min(depth, first + chunk)
        for z in range(first, last, group):
            near = range(z, min(z + group, last))
            sides = []
            for w in near:
                line = slice(w * GX, (w + 1) * GX)
                sides.append(jnp.concatenate([y0_ref[line, :], y1_ref[line, :]], axis=0))
            field = dot(tx_ref[...], jnp.concatenate(split(jnp.concatenate(sides, axis=1)), axis=0))
            pot = jnp.concatenate([pot_ref[w] for w in near], axis=1)
            field = (field[: 2 * size] + field[2 * size :]) * jnp.concatenate([pot, pot], axis=0)
            high, low = split(field)
            back = dot(txb_ref[...], high)
            back = back[: 2 * GX] + back[2 * GX :] + dot(txb_ref[: 2 * GX], low)
            for w in near:
                for p in range(2):
                    at = 128 * (w - z)
                    back_ref[w * GX : (w + 1) * GX, 128 * p : 128 * p + 128] = back[
                        p * GX : (p + 1) * GX, at : at + 128
                    ]
        part = slice(first * GX, last * GX)
        high, low = split(back_ref[part])
        moved = dot(high, tyb_ref[...])
        q_ref[part] = moved[:, :128] + moved[:, 128:] + dot(low, tyb_ref[:, :128])

    for s in range(slots):
        re, im = jnp.zeros((pad, 128), F32), jnp.zeros((pad, 128), F32)
        for i, (width, slot, middle) in enumerate(places):
            if slot != s:
                continue
            value = q_ref[pl.ds(i, pad, stride=GX), :]
            here = between(middle - width, middle + width)
            re = jnp.where(here, pltpu.roll(value, (middle - radius) % 128, 1), re)
            im = jnp.where(here, pltpu.roll(value, (middle - radius - GY) % 128, 1), im)
        box_ref[:, 128 * s : 128 * s + 128] = jnp.concatenate(split(jnp.concatenate([re, im], axis=0)), axis=0)

    box = box_ref[...]
    for k in range(devices - 1):
        gather(box, marks[k], outs[k], slots)


def body(devices, bands, psi, col_map, potential, lower, upper):
    cols, size = psi.shape[2], psi.shape[3]
    radius = size // 4
    depth = size // devices
    pad = round_up(depth, 8)
    rows = 2 * pad
    me = lax.axis_index("grid")
    me_arg = me.astype(jnp.int32).reshape(1)
    if devices & (devices - 1):
        raise ValueError("mesh size")

    def step(at, k):
        return at ^ k

    def exchange(values, late=0):
        order = list(range(1, late + 1)) + list(range(devices - 1, late, -1))
        moved = {k: lax.ppermute(values[k], "grid", [(d, step(d, k)) for d in range(devices)]) for k in order}
        return [values[0]] + [moved[k] for k in range(1, devices)]

    ahead, back = z_tables(size, devices, pad)
    tables = plane_tables(size)
    count = 2 * radius + 1
    slots = round_up(-(-count // bands), 8)
    pick = np.zeros((2, bands * 2 * slots, sum(kept(size))), ml_dtypes.bfloat16)
    for j in range(count):
        at = (j % bands) * 2 * slots + j // bands
        pick[0, at, (j - radius) % sum(kept(size))] = 1
        pick[1, at + slots, (j - radius) % sum(kept(size))] = 1

    pot = (potential * (1.0 / float(size**3))).reshape(depth, size, size)
    pot = jnp.pad(pot, ((0, 0), (0, 0), (0, 128 - size)))
    psi_t = jnp.transpose(psi.reshape(2, cols, size), (0, 2, 1))
    col_row = col_map.reshape(1, cols)

    def vmem(shape, dtype=F32):
        return pltpu.VMEM(shape, dtype)

    marks = exchange(
        call(
            functools.partial(first_kernel, devices, step, size),
            [vmem((rows + 8, cols))] * devices,
            [me_arg],
            [(psi_t, True), (col_row, True), (ahead, True)],
            [
                pltpu.VMEM((2, sum(kept(size)), cols), F32),
                pltpu.VMEM(col_row.shape, jnp.int32),
                pltpu.VMEM(ahead.shape, BF16),
                pltpu.SemaphoreType.DMA((6,)),
            ],
            far=True,
        )
    )

    slots_all = packing(size)[1]
    box_shape = (rows, 128 * slots_all)

    def slab(values):
        order = [0] + list(range(devices - 1, 0, -1))
        sums = []
        for k in order[:-1]:
            sums = call(
                functools.partial(scatter_kernel, slots_all),
                [vmem(box_shape)],
                [],
                [(value, True) for value in [values[k], marks[k]] + list(sums)],
            )
        given = [values[order[-1]], sums[0]] + [marks[k] for k in order[1:]]
        *sent, box = call(
            functools.partial(slab_kernel, devices, size, depth),
            [vmem((rows, cols))] * (devices - 1) + [vmem((2 * rows, 128 * slots_all), BF16)],
            [],
            [(value, True) for value in given] + [(pot, False)] + [(table, False) for table in tables],
            [
                pltpu.VMEM((GX * pad, 128), F32),
                pltpu.VMEM((GX * pad, 128), F32),
                pltpu.VMEM((GX * pad, 128), F32),
                pltpu.VMEM((pad * GX, 256), F32),
                pltpu.VMEM((pad * GX, 128), F32),
            ],
        )
        own = call(
            functools.partial(gather_kernel, slots_all),
            [vmem((rows, cols))],
            [],
            [(box, True), (marks[0], True)],
        )
        return list(own) + [sent[order.index(k) - 1] for k in range(1, devices)]

    held = pltpu.VMEM((3 * devices * rows, cols), BF16)
    planes = exchange(slab(marks))
    first, *sent = call(
        functools.partial(middle_kernel, devices, step, size),
        [vmem((2, sum(kept(size)), cols))] + [vmem((rows, cols))] * devices,
        [me_arg, lower, upper],
        [(value, True) for value in planes] + [(psi_t, False), (col_row, False), (ahead, False), (back, False)],
        [held],
    )
    planes = exchange(slab(exchange(sent)), late=1)
    filtered, packed = call(
        functools.partial(last_kernel, devices, bands, step, size),
        [vmem((2, size, cols)), vmem((bands, 2 * slots, cols), BF16)],
        [me_arg, lower, upper],
        [(value, True) for value in planes]
        + [(psi_t, False), (first, True), (col_row, False), (back, False), (pick, False)],
        [held],
    )
    partial_sum, _ = call(
        functools.partial(gram_kernel, bands),
        [vmem((devices * bands, 1, 128)), vmem((bands, 128))],
        [],
        [(lax.all_to_all(packed, "band", 0, 0, tiled=True), True)],
    )
    own = bands // devices
    (gram,) = call(
        functools.partial(total_kernel, own, 1.0 / (4.0 * radius**3)),
        [jax.ShapeDtypeStruct((2, 1, own), F32)],
        [me_arg],
        [(lax.all_to_all(partial_sum, ("grid", "band"), 0, 0, tiled=True), True)],
    )
    return jnp.transpose(filtered, (0, 2, 1)).reshape(psi.shape), gram


def solution(mesh):
    return jax.shard_map(
        functools.partial(body, mesh.shape["grid"], mesh.shape["band"]),
        mesh=mesh,
        in_specs=(P(None, "band", "grid", None), P("grid"), P("grid", None), P(), P()),
        out_specs=(P(None, "band", "grid", None), P(None, "band", "grid")),
        check_vma=False,
    )
```

```python
import functools

import jax
import jax.numpy as jnp
import ml_dtypes
import numpy as np
from jax import lax
from jax.experimental import pallas as pl
from jax.experimental.pallas import tpu as pltpu
from jax.sharding import PartitionSpec as P

GY = 64
GX = 56
F32 = jnp.float32
BF16 = jnp.bfloat16
MIB = 1024 * 1024


def round_up(value, unit):
    return -(-value // unit) * unit


def halves(table):
    table = np.asarray(table, np.float32)
    high = table.astype(ml_dtypes.bfloat16)
    low = (table - high.astype(np.float32)).astype(ml_dtypes.bfloat16)
    return high, low


def stacked_table(table, axis):
    high, low = halves(table)
    return np.concatenate([high, high, low], axis=axis)


def folded(index, size):
    return np.where(index < size // 2, index, index - size)


def kept(size):
    radius = size // 4
    return round_up(radius + 1, 8), radius


def z_tables(size, devices, pad):
    depth = size // devices
    rows = 2 * pad
    first, last = kept(size)
    count = first + last
    freq = np.concatenate([np.arange(first), np.arange(size - last, size)])
    ahead = np.zeros((devices, rows, 2 * count))
    back = np.zeros((2 * count, devices * rows))
    for d in range(devices):
        plane = d * depth + np.arange(depth)
        angle = 2 * np.pi * ((plane[:, None] * freq[None, :]) % size) / size
        c, s = np.cos(angle), np.sin(angle)
        ahead[d, :depth, :count], ahead[d, :depth, count:] = c, -s
        ahead[d, pad : pad + depth, :count], ahead[d, pad : pad + depth, count:] = s, c
        at = d * rows
        back[:count, at : at + depth], back[:count, at + pad : at + pad + depth] = c.T, s.T
        back[count:, at : at + depth], back[count:, at + pad : at + pad + depth] = -s.T, c.T
    return stacked_table(ahead, 2), stacked_table(back, 1)


def plane_tables(size):
    radius = size // 4
    count = 2 * radius + 1
    freq = np.arange(count) - radius
    angle = 2 * np.pi * ((freq[:, None] * np.arange(size)[None, :]) % size) / size
    c, s = np.cos(angle), np.sin(angle)
    ty = np.zeros((2 * GY, 256))
    ty[:count, :size], ty[:count, 128 : 128 + size] = c, s
    ty[GY : GY + count, :size], ty[GY : GY + count, 128 : 128 + size] = -s, c
    tyb = np.zeros((256, 2 * GY))
    tyb[:size, :count], tyb[:size, GY : GY + count] = c.T, -s.T
    tyb[128 : 128 + size, :count], tyb[128 : 128 + size, GY : GY + count] = s.T, c.T
    tx = np.zeros((2 * size, 2 * GX))
    tx[:size, :count], tx[:size, GX : GX + count] = c.T, -s.T
    tx[size:, :count], tx[size:, GX : GX + count] = s.T, c.T
    txb = np.zeros((2 * GX, 2 * size))
    txb[:count, :size], txb[:count, size:] = c, s
    txb[GX : GX + count, :size], txb[GX : GX + count, size:] = -s, c
    high, low = halves(tx)
    tx = np.concatenate([np.concatenate([high, high], 1), np.concatenate([low, 0 * low], 1)], 0)
    return stacked_table(ty, 0), tx, np.concatenate(halves(txb), 0), np.concatenate(halves(tyb), 1)


def packing(size):
    radius = size // 4
    widths = [int(np.sqrt(radius * radius - g * g)) for g in range(-radius, radius + 1)]
    slots, free = [None] * len(widths), []
    for i in sorted(range(len(widths)), key=lambda j: (-widths[j], j)):
        span = 2 * widths[i] + 1
        for s in range(len(free) + 1):
            if s == len(free):
                free.append(128)
            if free[s] >= span:
                slots[i] = (widths[i], s, 128 - free[s] + widths[i])
                free[s] -= span
                break
    return slots, round_up(len(free), 2)


def split(value):
    high = value.astype(BF16)
    low = (value - high.astype(F32)).astype(BF16)
    return high, low


def tripled(value, axis):
    high, low = split(value)
    return jnp.concatenate([high, low, high], axis=axis)


def dot(a, b, dims=((1,), (0,))):
    return lax.dot_general(a, b, (dims, ((), ())), preferred_element_type=F32)


SMEM = pl.BlockSpec(memory_space=pltpu.SMEM)
VMEM = pl.BlockSpec(memory_space=pltpu.VMEM)
HBM = pl.BlockSpec(memory_space=pltpu.HBM)


def call(kernel, out_shape, scalars, arrays, scratch=(), limit=24, far=False):
    space = pltpu.HBM if far else pltpu.VMEM
    arrays = [pltpu.with_memory_space_constraint(value, space) if keep else value for value, keep in arrays]
    return pl.pallas_call(
        kernel,
        out_shape=out_shape,
        in_specs=[SMEM] * len(scalars) + [HBM if far else VMEM] * len(arrays),
        out_specs=[VMEM] * len(out_shape),
        scratch_shapes=list(scratch),
        compiler_params=pltpu.CompilerParams(vmem_limit_bytes=limit * MIB),
    )(*scalars, *arrays)


def position(col_row, size):
    place = col_row.astype(F32)
    kx = jnp.floor((place + 0.5) * (1.0 / size))
    ky = place - kx * size
    half = float(size // 2)
    return jnp.where(kx < half, kx, kx - size), jnp.where(ky < half, ky, ky - size)


def sphere(col_row, size):
    cols = col_row.shape[1]
    radius = size // 4
    gx, gy = position(col_row, size)
    first, last = kept(size)
    index = lax.broadcasted_iota(jnp.int32, (first + last, cols), 0)
    freq = jnp.where(index < first, index, index - (first + last)).astype(F32)
    radius2 = (gx * gx + gy * gy) + freq * freq
    return radius2 <= float(radius * radius), radius2 * (2.0 / (radius * radius))


def kept_rows(ref, p, size):
    first, last = kept(size)
    return jnp.concatenate([ref[p, :first], ref[p, size - last :]], axis=0)


def to_planes(me, parts, table_ref, outs, step):
    value = tripled(jnp.concatenate(parts, axis=0), 0)
    table = jnp.concatenate([table_ref[step(me, k)] for k in range(len(outs))], axis=0)
    total = dot(table, value)
    rows = table_ref.shape[1]
    for k in range(len(outs)):
        outs[k][:rows] = total[k * rows : (k + 1) * rows]


def from_planes(me, planes, table_ref, held, step, size):
    rows = planes[0].shape[0]
    third = rows * len(planes)
    for k in range(len(planes)):
        high, low = split(planes[k][...])
        at = step(me, k) * rows
        for j, value in enumerate((high, low, high)):
            held[pl.ds(pl.multiple_of(j * third + at, 16), rows), :] = value
    total = dot(table_ref[...], held[...])
    return total[: sum(kept(size))], total[sum(kept(size)) :]


def first_kernel(devices, step, size, me_ref, *refs):
    far, refs = refs[:3], refs[3:]
    outs, (psi_ref, col_ref, ahead_ref, sems) = refs[:devices], refs[devices:]
    first, last = kept(size)
    pairs = [(far[1], col_ref), (far[2], ahead_ref)]
    for p in range(2):
        pairs.append((far[0].at[p, :first], psi_ref.at[p, :first]))
        pairs.append((far[0].at[p, size - last :], psi_ref.at[p, first:]))
    copies = [pltpu.make_async_copy(source, target, sems.at[i]) for i, (source, target) in enumerate(pairs)]
    for copy in copies:
        copy.start()
    copies[0].wait()
    radius = size // 4
    gx, gy = position(col_ref[...], size)
    used = gx * gx + gy * gy <= float(radius * radius)
    rows = ahead_ref.shape[1]
    row = lax.broadcasted_iota(jnp.int32, (8, gx.shape[1]), 0)
    slot, lane = jnp.zeros(row.shape, F32), jnp.zeros(row.shape, F32)
    for i, (_, s, middle) in enumerate(packing(size)[0]):
        here = gx == float(i - radius)
        slot, lane = jnp.where(here, float(s), slot), jnp.where(here, float(middle), lane)
    place = jnp.where(used, jnp.where(row == 0, slot, lane + gy), -9.0)
    for k in range(devices):
        outs[k][rows:] = place
    inside, _ = sphere(col_ref[...], size)
    for copy in copies[1:]:
        copy.wait()
    parts = [jnp.where(inside, psi_ref[p], 0.0) for p in range(2)]
    to_planes(me_ref[0], parts, ahead_ref, outs, step)


def middle_kernel(devices, step, size, me_ref, low_ref, up_ref, *refs):
    planes, refs = refs[:devices], refs[devices:]
    psi_ref, col_ref, ahead_ref, back_ref, first_ref = refs[:5]
    outs, held = refs[5 : 5 + devices], refs[5 + devices]
    center = (up_ref[0] + low_ref[0]) / 2.0
    half = (up_ref[0] - low_ref[0]) / 2.0
    inside, kinetic = sphere(col_ref[...], size)
    back = from_planes(me_ref[0], planes, back_ref, held, step, size)
    parts = []
    for p in range(2):
        value = jnp.where(inside, ((kinetic - center) * kept_rows(psi_ref, p, size) + back[p]) / half, 0.0)
        first_ref[p] = value
        parts.append(value)
    to_planes(me_ref[0], parts, ahead_ref, outs, step)


def last_kernel(devices, bands, step, size, me_ref, low_ref, up_ref, *refs):
    planes, refs = refs[:devices], refs[devices:]
    psi_ref, first_ref, col_ref, back_ref, pick_ref, filtered_ref, packed_ref, held = refs
    center = (up_ref[0] + low_ref[0]) / 2.0
    half = (up_ref[0] - low_ref[0]) / 2.0
    inside, kinetic = sphere(col_ref[...], size)
    back = from_planes(me_ref[0], planes, back_ref, held, step, size)
    first, last = kept(size)
    total = None
    for p in range(2):
        value = 2.0 * ((kinetic - center) * first_ref[p] + back[p]) / half - kept_rows(psi_ref, p, size)
        value = jnp.where(inside, value, 0.0)
        filtered_ref[p, :first] = value[:first]
        filtered_ref[p, first : size - last] = jnp.zeros((size - last - first, value.shape[1]), F32)
        filtered_ref[p, size - last :] = value[first:]
        piece = dot(pick_ref[p], value.astype(BF16))
        total = piece if total is None else total + piece
    rows = packed_ref.shape[1]
    for k in range(bands):
        packed_ref[k] = total[k * rows : (k + 1) * rows].astype(BF16)


def rest(value, unit):
    return value & (unit - 1) if unit & (unit - 1) == 0 else value % unit


def gram_kernel(bands, parts_ref, sum_ref, spare_ref):
    rows, cols = parts_ref.shape[1:]
    count = bands * rows
    stacked = parts_ref[...].reshape(count, cols)
    product = dot(stacked, stacked, ((1,), (1,)))
    down = lax.broadcasted_iota(jnp.int32, (count, count), 0)
    along = lax.broadcasted_iota(jnp.int32, (count, count), 1)
    down, along = rest(down, rows), rest(along, rows)
    real = jnp.where(down == along, product, 0.0)
    imag = jnp.where(along == down + rows // 2, product, jnp.where(down == along + rows // 2, -product, 0.0))
    place = lax.broadcasted_iota(jnp.int32, (count, 128), 0)
    spot = lax.broadcasted_iota(jnp.int32, (count, 128), 1) * rows
    pieces, places = [], []
    for p, value in enumerate((real, imag)):
        value = jnp.sum(value.reshape(bands, rows, count), axis=1)
        gap = place + p * GY * rows - spot
        hot = jnp.where((gap >= 0) & (gap < rows), 1.0, 0.0).astype(BF16)
        for _ in range(3):
            pieces.append(value.astype(BF16))
            value = value - pieces[-1].astype(F32)
            places.append(hot)
    value = dot(jnp.concatenate(pieces, axis=1), jnp.concatenate(places, axis=0))
    for g in range(sum_ref.shape[0] // bands):
        sum_ref[g * bands : (g + 1) * bands, 0, :] = value
    spare_ref[...] = value


def total_kernel(own, scale, me_ref, parts_ref, out_ref):
    value = jnp.sum(parts_ref[...], axis=0) * scale
    value = pltpu.roll(value, lax.rem(128 - me_ref[0] * own, 128), 1)
    out_ref[0] = value[:, :own]
    out_ref[1] = value[:, GY : GY + own]


def scatter(plane_ref, mark_ref, slots):
    rows, cols = mark_ref.shape[0] - 8, mark_ref.shape[1]
    row = lax.broadcasted_iota(jnp.int32, (8, 256), 0)
    side = lax.broadcasted_iota(jnp.int32, (8, 256), 1) // 128
    spread = jnp.where(row == side, 1.0, 0.0).astype(BF16)
    both = dot(mark_ref[rows:].astype(BF16), spread, ((0,), (0,)))
    slot = both[:, :128].astype(BF16)
    along = lax.broadcasted_iota(jnp.int32, (cols, 128), 1).astype(F32)
    spot = jnp.where(both[:, 128:] == along, 1.0, 0.0).astype(BF16)
    lhs = jnp.concatenate(split(plane_ref[:rows]), axis=0)
    zero = jnp.zeros((), BF16)
    for t in range(0, slots, 2):
        hot = [jnp.where(slot == float(v), spot, zero) for v in (t, t + 1)]
        got = dot(lhs, jnp.concatenate(hot, axis=1))
        yield t, got[:rows] + got[rows:]


def gather(box, mark_ref, out_ref, slots):
    rows, cols = mark_ref.shape[0] - 8, mark_ref.shape[1]
    zero = jnp.zeros((), BF16)
    wide = min(512, cols)
    for at in range(0, cols, wide):
        slot = jnp.broadcast_to(mark_ref[rows : rows + 1, at : at + wide], (16, wide)).astype(BF16)
        spot = jnp.broadcast_to(mark_ref[rows + 1 : rows + 2, at : at + wide], (128, wide))
        down = lax.broadcasted_iota(jnp.int32, (128, wide), 0).astype(F32)
        hot = jnp.where(spot == down, 1.0, 0.0).astype(BF16)
        tall = []
        for v in range(slots):
            here = slot == float(v)
            tall += [jnp.where(here, hot[16 * i : 16 * i + 16], zero) for i in range(8)]
        got = dot(box, jnp.concatenate(tall, axis=0))
        out_ref[:, at : at + wide] = got[:rows] + got[rows:]


def scatter_kernel(slots, plane_ref, mark_ref, *refs):
    before, after = refs[:-1], refs[-1]
    for t, tile in scatter(plane_ref, mark_ref, slots):
        here = slice(128 * t, 128 * t + 256)
        after[:, here] = tile + before[0][:, here] if before else tile


def gather_kernel(slots, box_ref, mark_ref, out_ref):
    gather(box_ref[...], mark_ref, out_ref, slots)


def slab_kernel(devices, size, depth, plane_ref, before_ref, *refs):
    marks, refs = refs[: devices - 1], refs[devices - 1 :]
    pot_ref, ty_ref, tx_ref, txb_ref, tyb_ref = refs[:5]
    outs, box_ref = refs[5 : 4 + devices], refs[4 + devices]
    in_ref, y0_ref, y1_ref, back_ref, q_ref = refs[5 + devices :]
    pad = round_up(depth, 8)
    radius = size // 4
    places, slots = packing(size)
    lane = lax.broadcasted_iota(jnp.int32, (pad, 128), 1)

    def between(first, last):
        return (lane >= first) & (lane <= last)

    in_ref[...] = jnp.zeros(in_ref.shape, F32)
    for t, tile in scatter(plane_ref, marks[-1], slots):
        got = tile + before_ref[:, 128 * t : 128 * t + 256]
        for i, (width, slot, middle) in enumerate(places):
            if slot // 2 * 2 != t:
                continue
            at = 128 * (slot - t)
            re = pltpu.roll(got[:pad, at : at + 128], (radius - middle) % 128, 1)
            im = pltpu.roll(got[pad:, at : at + 128], (radius + GY - middle) % 128, 1)
            im = jnp.where(between(GY + radius - width, GY + radius + width), im, 0.0)
            in_ref[pl.ds(i, pad, stride=GX), :] = jnp.where(between(radius - width, radius + width), re, im)
    moved = dot(tripled(in_ref[...], 1), ty_ref[...])
    y0_ref[...] = moved[:, :128]
    y1_ref[...] = moved[:, 128:]
    if depth < pad:
        q_ref[depth * GX :] = jnp.zeros(((pad - depth) * GX, 128), F32)

    chunk, group = 8, 8
    for first in range(0, depth, chunk):
        last = min(depth, first + chunk)
        for z in range(first, last, group):
            near = range(z, min(z + group, last))
            sides = []
            for w in near:
                line = slice(w * GX, (w + 1) * GX)
                sides.append(jnp.concatenate([y0_ref[line, :], y1_ref[line, :]], axis=0))
            field = dot(tx_ref[...], jnp.concatenate(split(jnp.concatenate(sides, axis=1)), axis=0))
            pot = jnp.concatenate([pot_ref[w] for w in near], axis=1)
            field = (field[: 2 * size] + field[2 * size :]) * jnp.concatenate([pot, pot], axis=0)
            high, low = split(field)
            back = dot(txb_ref[...], high)
            back = back[: 2 * GX] + back[2 * GX :] + dot(txb_ref[: 2 * GX], low)
            for w in near:
                for p in range(2):
                    at = 128 * (w - z)
                    back_ref[w * GX : (w + 1) * GX, 128 * p : 128 * p + 128] = back[
                        p * GX : (p + 1) * GX, at : at + 128
                    ]
        part = slice(first * GX, last * GX)
        high, low = split(back_ref[part])
        moved = dot(high, tyb_ref[...])
        q_ref[part] = moved[:, :128] + moved[:, 128:] + dot(low, tyb_ref[:, :128])

    for s in range(slots):
        re, im = jnp.zeros((pad, 128), F32), jnp.zeros((pad, 128), F32)
        for i, (width, slot, middle) in enumerate(places):
            if slot != s:
                continue
            value = q_ref[pl.ds(i, pad, stride=GX), :]
            here = between(middle - width, middle + width)
            re = jnp.where(here, pltpu.roll(value, (middle - radius) % 128, 1), re)
            im = jnp.where(here, pltpu.roll(value, (middle - radius - GY) % 128, 1), im)
        box_ref[:, 128 * s : 128 * s + 128] = jnp.concatenate(split(jnp.concatenate([re, im], axis=0)), axis=0)

    box = box_ref[...]
    for k in range(devices - 1):
        gather(box, marks[k], outs[k], slots)


def body(devices, bands, psi, col_map, potential, lower, upper):
    cols, size = psi.shape[2], psi.shape[3]
    radius = size // 4
    depth = size // devices
    pad = round_up(depth, 8)
    rows = 2 * pad
    me = lax.axis_index("grid")
    me_arg = me.astype(jnp.int32).reshape(1)
    if devices & (devices - 1):
        raise ValueError("mesh size")

    def step(at, k):
        return at ^ k

    def exchange(values):
        moved = [
            lax.ppermute(values[k], "grid", [(d, step(d, k)) for d in range(devices)])
            for k in range(devices - 1, 0, -1)
        ]
        return [values[0]] + moved[::-1]

    ahead, back = z_tables(size, devices, pad)
    tables = plane_tables(size)
    count = 2 * radius + 1
    slots = round_up(-(-count // bands), 8)
    pick = np.zeros((2, bands * 2 * slots, sum(kept(size))), ml_dtypes.bfloat16)
    for j in range(count):
        at = (j % bands) * 2 * slots + j // bands
        pick[0, at, (j - radius) % sum(kept(size))] = 1
        pick[1, at + slots, (j - radius) % sum(kept(size))] = 1

    pot = (potential * (1.0 / float(size**3))).reshape(depth, size, size)
    pot = jnp.pad(pot, ((0, 0), (0, 0), (0, 128 - size)))
    psi_t = jnp.transpose(psi.reshape(2, cols, size), (0, 2, 1))
    col_row = col_map.reshape(1, cols)

    def vmem(shape, dtype=F32):
        return pltpu.VMEM(shape, dtype)

    marks = exchange(
        call(
            functools.partial(first_kernel, devices, step, size),
            [vmem((rows + 8, cols))] * devices,
            [me_arg],
            [(psi_t, True), (col_row, True), (ahead, True)],
            [
                pltpu.VMEM((2, sum(kept(size)), cols), F32),
                pltpu.VMEM(col_row.shape, jnp.int32),
                pltpu.VMEM(ahead.shape, BF16),
                pltpu.SemaphoreType.DMA((6,)),
            ],
            far=True,
        )
    )

    slots_all = packing(size)[1]
    box_shape = (rows, 128 * slots_all)

    def slab(values):
        order = [0] + list(range(devices - 1, 0, -1))
        sums = []
        for k in order[:-1]:
            sums = call(
                functools.partial(scatter_kernel, slots_all),
                [vmem(box_shape)],
                [],
                [(value, True) for value in [values[k], marks[k]] + list(sums)],
            )
        given = [values[order[-1]], sums[0]] + [marks[k] for k in order[1:]]
        *sent, box = call(
            functools.partial(slab_kernel, devices, size, depth),
            [vmem((rows, cols))] * (devices - 1) + [vmem((2 * rows, 128 * slots_all), BF16)],
            [],
            [(value, True) for value in given] + [(pot, False)] + [(table, False) for table in tables],
            [
                pltpu.VMEM((GX * pad, 128), F32),
                pltpu.VMEM((GX * pad, 128), F32),
                pltpu.VMEM((GX * pad, 128), F32),
                pltpu.VMEM((pad * GX, 256), F32),
                pltpu.VMEM((pad * GX, 128), F32),
            ],
        )
        own = call(
            functools.partial(gather_kernel, slots_all),
            [vmem((rows, cols))],
            [],
            [(box, True), (marks[0], True)],
        )
        return list(own) + [sent[order.index(k) - 1] for k in range(1, devices)]

    held = pltpu.VMEM((3 * devices * rows, cols), BF16)
    planes = exchange(slab(marks))
    first, *sent = call(
        functools.partial(middle_kernel, devices, step, size),
        [vmem((2, sum(kept(size)), cols))] + [vmem((rows, cols))] * devices,
        [me_arg, lower, upper],
        [(value, True) for value in planes] + [(psi_t, False), (col_row, False), (ahead, False), (back, False)],
        [held],
    )
    planes = exchange(slab(exchange(sent)))
    filtered, packed = call(
        functools.partial(last_kernel, devices, bands, step, size),
        [vmem((2, size, cols)), vmem((bands, 2 * slots, cols), BF16)],
        [me_arg, lower, upper],
        [(value, True) for value in planes]
        + [(psi_t, False), (first, True), (col_row, False), (back, False), (pick, False)],
        [held],
    )
    partial_sum, _ = call(
        functools.partial(gram_kernel, bands),
        [vmem((devices * bands, 1, 128)), vmem((bands, 128))],
        [],
        [(lax.all_to_all(packed, "band", 0, 0, tiled=True), True)],
    )
    own = bands // devices
    (gram,) = call(
        functools.partial(total_kernel, own, 1.0 / (4.0 * radius**3)),
        [jax.ShapeDtypeStruct((2, 1, own), F32)],
        [me_arg],
        [(lax.all_to_all(partial_sum, ("grid", "band"), 0, 0, tiled=True), True)],
    )
    return jnp.transpose(filtered, (0, 2, 1)).reshape(psi.shape), gram


def solution(mesh):
    return jax.shard_map(
        functools.partial(body, mesh.shape["grid"], mesh.shape["band"]),
        mesh=mesh,
        in_specs=(P(None, "band", "grid", None), P("grid"), P("grid", None), P(), P()),
        out_specs=(P(None, "band", "grid", None), P(None, "band", "grid")),
        check_vma=False,
    )
```

```python
import functools

import jax
import jax.numpy as jnp
import ml_dtypes
import numpy as np
from jax import lax
from jax.experimental import pallas as pl
from jax.experimental.pallas import tpu as pltpu
from jax.sharding import PartitionSpec as P

GY = 64
GX = 56
F32 = jnp.float32
BF16 = jnp.bfloat16
MIB = 1024 * 1024


def round_up(value, unit):
    return -(-value // unit) * unit


def halves(table):
    table = np.asarray(table, np.float32)
    high = table.astype(ml_dtypes.bfloat16)
    low = (table - high.astype(np.float32)).astype(ml_dtypes.bfloat16)
    return high, low


def stacked_table(table, axis):
    high, low = halves(table)
    return np.concatenate([high, high, low], axis=axis)


def folded(index, size):
    return np.where(index < size // 2, index, index - size)


def kept(size):
    radius = size // 4
    return round_up(radius + 1, 8), radius


def z_tables(size, devices, pad):
    depth = size // devices
    rows = 2 * pad
    first, last = kept(size)
    count = first + last
    freq = np.concatenate([np.arange(first), np.arange(size - last, size)])
    ahead = np.zeros((devices, rows, 2 * count))
    back = np.zeros((2 * count, devices * rows))
    for d in range(devices):
        plane = d * depth + np.arange(depth)
        angle = 2 * np.pi * ((plane[:, None] * freq[None, :]) % size) / size
        c, s = np.cos(angle), np.sin(angle)
        ahead[d, :depth, :count], ahead[d, :depth, count:] = c, -s
        ahead[d, pad : pad + depth, :count], ahead[d, pad : pad + depth, count:] = s, c
        at = d * rows
        back[:count, at : at + depth], back[:count, at + pad : at + pad + depth] = c.T, s.T
        back[count:, at : at + depth], back[count:, at + pad : at + pad + depth] = -s.T, c.T
    return stacked_table(ahead, 2), stacked_table(back, 1)


def plane_tables(size):
    radius = size // 4
    count = 2 * radius + 1
    freq = np.arange(count) - radius
    angle = 2 * np.pi * ((freq[:, None] * np.arange(size)[None, :]) % size) / size
    c, s = np.cos(angle), np.sin(angle)
    ty = np.zeros((2 * GY, 256))
    ty[:count, :size], ty[:count, 128 : 128 + size] = c, s
    ty[GY : GY + count, :size], ty[GY : GY + count, 128 : 128 + size] = -s, c
    tyb = np.zeros((256, 2 * GY))
    tyb[:size, :count], tyb[:size, GY : GY + count] = c.T, -s.T
    tyb[128 : 128 + size, :count], tyb[128 : 128 + size, GY : GY + count] = s.T, c.T
    tx = np.zeros((2 * size, 2 * GX))
    tx[:size, :count], tx[:size, GX : GX + count] = c.T, -s.T
    tx[size:, :count], tx[size:, GX : GX + count] = s.T, c.T
    txb = np.zeros((2 * GX, 2 * size))
    txb[:count, :size], txb[:count, size:] = c, s
    txb[GX : GX + count, :size], txb[GX : GX + count, size:] = -s, c
    high, low = halves(tx)
    tx = np.concatenate([np.concatenate([high, high], 1), np.concatenate([low, 0 * low], 1)], 0)
    return stacked_table(ty, 0), tx, np.concatenate(halves(txb), 0), np.concatenate(halves(tyb), 1)


def packing(size):
    radius = size // 4
    widths = [int(np.sqrt(radius * radius - g * g)) for g in range(-radius, radius + 1)]
    slots, free = [None] * len(widths), []
    for i in sorted(range(len(widths)), key=lambda j: (-widths[j], j)):
        span = 2 * widths[i] + 1
        for s in range(len(free) + 1):
            if s == len(free):
                free.append(128)
            if free[s] >= span:
                slots[i] = (widths[i], s, 128 - free[s] + widths[i])
                free[s] -= span
                break
    return slots, round_up(len(free), 2)


def split(value):
    high = value.astype(BF16)
    low = (value - high.astype(F32)).astype(BF16)
    return high, low


def tripled(value, axis):
    high, low = split(value)
    return jnp.concatenate([high, low, high], axis=axis)


def dot(a, b, dims=((1,), (0,))):
    return lax.dot_general(a, b, (dims, ((), ())), preferred_element_type=F32)


SMEM = pl.BlockSpec(memory_space=pltpu.SMEM)
VMEM = pl.BlockSpec(memory_space=pltpu.VMEM)
HBM = pl.BlockSpec(memory_space=pltpu.HBM)


def call(kernel, out_shape, scalars, arrays, scratch=(), limit=24, far=False):
    space = pltpu.HBM if far else pltpu.VMEM
    arrays = [pltpu.with_memory_space_constraint(value, space) if keep else value for value, keep in arrays]
    return pl.pallas_call(
        kernel,
        out_shape=out_shape,
        in_specs=[SMEM] * len(scalars) + [HBM if far else VMEM] * len(arrays),
        out_specs=[VMEM] * len(out_shape),
        scratch_shapes=list(scratch),
        compiler_params=pltpu.CompilerParams(vmem_limit_bytes=limit * MIB),
    )(*scalars, *arrays)


def position(col_row, size):
    place = col_row.astype(F32)
    kx = jnp.floor((place + 0.5) * (1.0 / size))
    ky = place - kx * size
    half = float(size // 2)
    return jnp.where(kx < half, kx, kx - size), jnp.where(ky < half, ky, ky - size)


def sphere(col_row, size):
    cols = col_row.shape[1]
    radius = size // 4
    gx, gy = position(col_row, size)
    first, last = kept(size)
    index = lax.broadcasted_iota(jnp.int32, (first + last, cols), 0)
    freq = jnp.where(index < first, index, index - (first + last)).astype(F32)
    radius2 = (gx * gx + gy * gy) + freq * freq
    return radius2 <= float(radius * radius), radius2 * (2.0 / (radius * radius))


def kept_rows(ref, p, size):
    first, last = kept(size)
    return jnp.concatenate([ref[p, :first], ref[p, size - last :]], axis=0)


def to_planes(me, parts, table_ref, outs, step):
    value = tripled(jnp.concatenate(parts, axis=0), 0)
    table = jnp.concatenate([table_ref[step(me, k)] for k in range(len(outs))], axis=0)
    total = dot(table, value)
    rows = table_ref.shape[1]
    for k in range(len(outs)):
        outs[k][:rows] = total[k * rows : (k + 1) * rows]


def from_planes(me, planes, table_ref, held, step, size):
    rows = planes[0].shape[0]
    third = rows * len(planes)
    for k in range(len(planes)):
        high, low = split(planes[k][...])
        at = step(me, k) * rows
        for j, value in enumerate((high, low, high)):
            held[pl.ds(pl.multiple_of(j * third + at, 16), rows), :] = value
    total = dot(table_ref[...], held[...])
    return total[: sum(kept(size))], total[sum(kept(size)) :]


def first_kernel(devices, step, size, me_ref, *refs):
    far, refs = refs[:3], refs[3:]
    outs, (psi_ref, col_ref, ahead_ref, sems) = refs[:devices], refs[devices:]
    first, last = kept(size)
    pairs = [(far[1], col_ref), (far[2], ahead_ref)]
    for p in range(2):
        pairs.append((far[0].at[p, :first], psi_ref.at[p, :first]))
        pairs.append((far[0].at[p, size - last :], psi_ref.at[p, first:]))
    copies = [pltpu.make_async_copy(source, target, sems.at[i]) for i, (source, target) in enumerate(pairs)]
    for copy in copies:
        copy.start()
    copies[0].wait()
    radius = size // 4
    gx, gy = position(col_ref[...], size)
    used = gx * gx + gy * gy <= float(radius * radius)
    rows = ahead_ref.shape[1]
    row = lax.broadcasted_iota(jnp.int32, (8, gx.shape[1]), 0)
    slot, lane = jnp.zeros(row.shape, F32), jnp.zeros(row.shape, F32)
    for i, (_, s, middle) in enumerate(packing(size)[0]):
        here = gx == float(i - radius)
        slot, lane = jnp.where(here, float(s), slot), jnp.where(here, float(middle), lane)
    place = jnp.where(used, jnp.where(row == 0, slot, lane + gy), -9.0)
    for k in range(devices):
        outs[k][rows:] = place
    inside, _ = sphere(col_ref[...], size)
    for copy in copies[1:]:
        copy.wait()
    parts = [jnp.where(inside, psi_ref[p], 0.0) for p in range(2)]
    to_planes(me_ref[0], parts, ahead_ref, outs, step)


def middle_kernel(devices, step, size, me_ref, low_ref, up_ref, *refs):
    planes, refs = refs[:devices], refs[devices:]
    psi_ref, col_ref, ahead_ref, back_ref, first_ref = refs[:5]
    outs, held = refs[5 : 5 + devices], refs[5 + devices]
    center = (up_ref[0] + low_ref[0]) / 2.0
    half = (up_ref[0] - low_ref[0]) / 2.0
    inside, kinetic = sphere(col_ref[...], size)
    back = from_planes(me_ref[0], planes, back_ref, held, step, size)
    parts = []
    for p in range(2):
        value = jnp.where(inside, ((kinetic - center) * kept_rows(psi_ref, p, size) + back[p]) / half, 0.0)
        first_ref[p] = value
        parts.append(value)
    to_planes(me_ref[0], parts, ahead_ref, outs, step)


def last_kernel(devices, bands, step, size, me_ref, low_ref, up_ref, *refs):
    planes, refs = refs[:devices], refs[devices:]
    psi_ref, first_ref, col_ref, back_ref, pick_ref, filtered_ref, packed_ref, held = refs
    center = (up_ref[0] + low_ref[0]) / 2.0
    half = (up_ref[0] - low_ref[0]) / 2.0
    inside, kinetic = sphere(col_ref[...], size)
    back = from_planes(me_ref[0], planes, back_ref, held, step, size)
    first, last = kept(size)
    total = None
    for p in range(2):
        value = 2.0 * ((kinetic - center) * first_ref[p] + back[p]) / half - kept_rows(psi_ref, p, size)
        value = jnp.where(inside, value, 0.0)
        filtered_ref[p, :first] = value[:first]
        filtered_ref[p, first : size - last] = jnp.zeros((size - last - first, value.shape[1]), F32)
        filtered_ref[p, size - last :] = value[first:]
        piece = dot(pick_ref[p], value.astype(BF16))
        total = piece if total is None else total + piece
    rows = packed_ref.shape[1]
    for k in range(bands):
        packed_ref[k] = total[k * rows : (k + 1) * rows].astype(BF16)


def rest(value, unit):
    return value & (unit - 1) if unit & (unit - 1) == 0 else value % unit


def gram_kernel(bands, parts_ref, sum_ref, spare_ref):
    rows, cols = parts_ref.shape[1:]
    count = bands * rows
    stacked = parts_ref[...].reshape(count, cols)
    product = dot(stacked, stacked, ((1,), (1,)))
    down = lax.broadcasted_iota(jnp.int32, (count, count), 0)
    along = lax.broadcasted_iota(jnp.int32, (count, count), 1)
    down, along = rest(down, rows), rest(along, rows)
    real = jnp.where(down == along, product, 0.0)
    imag = jnp.where(along == down + rows // 2, product, jnp.where(down == along + rows // 2, -product, 0.0))
    place = lax.broadcasted_iota(jnp.int32, (count, 128), 0)
    spot = lax.broadcasted_iota(jnp.int32, (count, 128), 1) * rows
    pieces, places = [], []
    for p, value in enumerate((real, imag)):
        value = jnp.sum(value.reshape(bands, rows, count), axis=1)
        gap = place + p * GY * rows - spot
        hot = jnp.where((gap >= 0) & (gap < rows), 1.0, 0.0).astype(BF16)
        for _ in range(3):
            pieces.append(value.astype(BF16))
            value = value - pieces[-1].astype(F32)
            places.append(hot)
    value = dot(jnp.concatenate(pieces, axis=1), jnp.concatenate(places, axis=0))
    for g in range(sum_ref.shape[0] // bands):
        sum_ref[g * bands : (g + 1) * bands, 0, :] = value
    spare_ref[...] = value


def total_kernel(own, scale, me_ref, parts_ref, out_ref):
    value = jnp.sum(parts_ref[...], axis=0) * scale
    value = pltpu.roll(value, lax.rem(128 - me_ref[0] * own, 128), 1)
    out_ref[0] = value[:, :own]
    out_ref[1] = value[:, GY : GY + own]


def scatter(plane_ref, mark_ref, slots):
    rows, cols = mark_ref.shape[0] - 8, mark_ref.shape[1]
    row = lax.broadcasted_iota(jnp.int32, (8, 256), 0)
    side = lax.broadcasted_iota(jnp.int32, (8, 256), 1) // 128
    spread = jnp.where(row == side, 1.0, 0.0).astype(BF16)
    both = dot(mark_ref[rows:].astype(BF16), spread, ((0,), (0,)))
    slot = both[:, :128].astype(BF16)
    along = lax.broadcasted_iota(jnp.int32, (cols, 128), 1).astype(F32)
    spot = jnp.where(both[:, 128:] == along, 1.0, 0.0).astype(BF16)
    lhs = jnp.concatenate(split(plane_ref[:rows]), axis=0)
    zero = jnp.zeros((), BF16)
    for t in range(0, slots, 2):
        hot = [jnp.where(slot == float(v), spot, zero) for v in (t, t + 1)]
        got = dot(lhs, jnp.concatenate(hot, axis=1))
        yield t, got[:rows] + got[rows:]


def gather(box, mark_ref, out_ref, slots):
    rows, cols = mark_ref.shape[0] - 8, mark_ref.shape[1]
    zero = jnp.zeros((), BF16)
    wide = min(512, cols)
    for at in range(0, cols, wide):
        slot = jnp.broadcast_to(mark_ref[rows : rows + 1, at : at + wide], (16, wide)).astype(BF16)
        spot = jnp.broadcast_to(mark_ref[rows + 1 : rows + 2, at : at + wide], (128, wide))
        down = lax.broadcasted_iota(jnp.int32, (128, wide), 0).astype(F32)
        hot = jnp.where(spot == down, 1.0, 0.0).astype(BF16)
        tall = []
        for v in range(slots):
            here = slot == float(v)
            tall += [jnp.where(here, hot[16 * i : 16 * i + 16], zero) for i in range(8)]
        got = dot(box, jnp.concatenate(tall, axis=0))
        out_ref[:, at : at + wide] = got[:rows] + got[rows:]


def scatter_kernel(slots, plane_ref, mark_ref, *refs):
    before, after = refs[:-1], refs[-1]
    for t, tile in scatter(plane_ref, mark_ref, slots):
        here = slice(128 * t, 128 * t + 256)
        after[:, here] = tile + before[0][:, here] if before else tile


def gather_kernel(slots, box_ref, mark_ref, out_ref):
    gather(box_ref[...], mark_ref, out_ref, slots)


def slab_kernel(devices, size, depth, plane_ref, before_ref, *refs):
    marks, refs = refs[: devices - 1], refs[devices - 1 :]
    pot_ref, ty_ref, tx_ref, txb_ref, tyb_ref = refs[:5]
    outs, box_ref = refs[5 : 4 + devices], refs[4 + devices]
    in_ref, y0_ref, y1_ref, back_ref, q_ref = refs[5 + devices :]
    pad = round_up(depth, 8)
    radius = size // 4
    places, slots = packing(size)
    lane = lax.broadcasted_iota(jnp.int32, (pad, 128), 1)

    def between(first, last):
        return (lane >= first) & (lane <= last)

    in_ref[...] = jnp.zeros(in_ref.shape, F32)
    for t, tile in scatter(plane_ref, marks[-1], slots):
        got = tile + before_ref[:, 128 * t : 128 * t + 256]
        for i, (width, slot, middle) in enumerate(places):
            if slot // 2 * 2 != t:
                continue
            at = 128 * (slot - t)
            re = pltpu.roll(got[:pad, at : at + 128], (radius - middle) % 128, 1)
            im = pltpu.roll(got[pad:, at : at + 128], (radius + GY - middle) % 128, 1)
            im = jnp.where(between(GY + radius - width, GY + radius + width), im, 0.0)
            in_ref[pl.ds(i, pad, stride=GX), :] = jnp.where(between(radius - width, radius + width), re, im)
    moved = dot(tripled(in_ref[...], 1), ty_ref[...])
    y0_ref[...] = moved[:, :128]
    y1_ref[...] = moved[:, 128:]
    if depth < pad:
        q_ref[depth * GX :] = jnp.zeros(((pad - depth) * GX, 128), F32)

    chunk, group = 24, 8
    for first in range(0, depth, chunk):
        last = min(depth, first + chunk)
        for z in range(first, last, group):
            near = range(z, min(z + group, last))
            sides = []
            for w in near:
                line = slice(w * GX, (w + 1) * GX)
                sides.append(jnp.concatenate([y0_ref[line, :], y1_ref[line, :]], axis=0))
            field = dot(tx_ref[...], jnp.concatenate(split(jnp.concatenate(sides, axis=1)), axis=0))
            pot = jnp.concatenate([pot_ref[w] for w in near], axis=1)
            field = (field[: 2 * size] + field[2 * size :]) * jnp.concatenate([pot, pot], axis=0)
            high, low = split(field)
            back = dot(txb_ref[...], high)
            back = back[: 2 * GX] + back[2 * GX :] + dot(txb_ref[: 2 * GX], low)
            for w in near:
                for p in range(2):
                    at = 128 * (w - z)
                    back_ref[w * GX : (w + 1) * GX, 128 * p : 128 * p + 128] = back[
                        p * GX : (p + 1) * GX, at : at + 128
                    ]
        part = slice(first * GX, last * GX)
        high, low = split(back_ref[part])
        moved = dot(high, tyb_ref[...])
        q_ref[part] = moved[:, :128] + moved[:, 128:] + dot(low, tyb_ref[:, :128])

    for s in range(slots):
        re, im = jnp.zeros((pad, 128), F32), jnp.zeros((pad, 128), F32)
        for i, (width, slot, middle) in enumerate(places):
            if slot != s:
                continue
            value = q_ref[pl.ds(i, pad, stride=GX), :]
            here = between(middle - width, middle + width)
            re = jnp.where(here, pltpu.roll(value, (middle - radius) % 128, 1), re)
            im = jnp.where(here, pltpu.roll(value, (middle - radius - GY) % 128, 1), im)
        box_ref[:, 128 * s : 128 * s + 128] = jnp.concatenate(split(jnp.concatenate([re, im], axis=0)), axis=0)

    box = box_ref[...]
    for k in range(devices - 1):
        gather(box, marks[k], outs[k], slots)


def body(devices, bands, psi, col_map, potential, lower, upper):
    cols, size = psi.shape[2], psi.shape[3]
    radius = size // 4
    depth = size // devices
    pad = round_up(depth, 8)
    rows = 2 * pad
    me = lax.axis_index("grid")
    me_arg = me.astype(jnp.int32).reshape(1)
    if devices & (devices - 1):
        raise ValueError("mesh size")

    def step(at, k):
        return at ^ k

    def exchange(values):
        moved = [
            lax.ppermute(values[k], "grid", [(d, step(d, k)) for d in range(devices)])
            for k in range(devices - 1, 0, -1)
        ]
        return [values[0]] + moved[::-1]

    ahead, back = z_tables(size, devices, pad)
    tables = plane_tables(size)
    count = 2 * radius + 1
    slots = round_up(-(-count // bands), 8)
    pick = np.zeros((2, bands * 2 * slots, sum(kept(size))), ml_dtypes.bfloat16)
    for j in range(count):
        at = (j % bands) * 2 * slots + j // bands
        pick[0, at, (j - radius) % sum(kept(size))] = 1
        pick[1, at + slots, (j - radius) % sum(kept(size))] = 1

    pot = (potential * (1.0 / float(size**3))).reshape(depth, size, size)
    pot = jnp.pad(pot, ((0, 0), (0, 0), (0, 128 - size)))
    psi_t = jnp.transpose(psi.reshape(2, cols, size), (0, 2, 1))
    col_row = col_map.reshape(1, cols)

    def vmem(shape, dtype=F32):
        return pltpu.VMEM(shape, dtype)

    marks = exchange(
        call(
            functools.partial(first_kernel, devices, step, size),
            [vmem((rows + 8, cols))] * devices,
            [me_arg],
            [(psi_t, True), (col_row, True), (ahead, True)],
            [
                pltpu.VMEM((2, sum(kept(size)), cols), F32),
                pltpu.VMEM(col_row.shape, jnp.int32),
                pltpu.VMEM(ahead.shape, BF16),
                pltpu.SemaphoreType.DMA((6,)),
            ],
            far=True,
        )
    )

    slots_all = packing(size)[1]
    box_shape = (rows, 128 * slots_all)

    def slab(values):
        order = [0] + list(range(devices - 1, 0, -1))
        sums = []
        for k in order[:-1]:
            sums = call(
                functools.partial(scatter_kernel, slots_all),
                [vmem(box_shape)],
                [],
                [(value, True) for value in [values[k], marks[k]] + list(sums)],
            )
        given = [values[order[-1]], sums[0]] + [marks[k] for k in order[1:]]
        *sent, box = call(
            functools.partial(slab_kernel, devices, size, depth),
            [vmem((rows, cols))] * (devices - 1) + [vmem((2 * rows, 128 * slots_all), BF16)],
            [],
            [(value, True) for value in given] + [(pot, False)] + [(table, False) for table in tables],
            [
                pltpu.VMEM((GX * pad, 128), F32),
                pltpu.VMEM((GX * pad, 128), F32),
                pltpu.VMEM((GX * pad, 128), F32),
                pltpu.VMEM((pad * GX, 256), F32),
                pltpu.VMEM((pad * GX, 128), F32),
            ],
        )
        own = call(
            functools.partial(gather_kernel, slots_all),
            [vmem((rows, cols))],
            [],
            [(box, True), (marks[0], True)],
        )
        return list(own) + [sent[order.index(k) - 1] for k in range(1, devices)]

    held = pltpu.VMEM((3 * devices * rows, cols), BF16)
    planes = exchange(slab(marks))
    first, *sent = call(
        functools.partial(middle_kernel, devices, step, size),
        [vmem((2, sum(kept(size)), cols))] + [vmem((rows, cols))] * devices,
        [me_arg, lower, upper],
        [(value, True) for value in planes] + [(psi_t, False), (col_row, False), (ahead, False), (back, False)],
        [held],
    )
    planes = exchange(slab(exchange(sent)))
    filtered, packed = call(
        functools.partial(last_kernel, devices, bands, step, size),
        [vmem((2, size, cols)), vmem((bands, 2 * slots, cols), BF16)],
        [me_arg, lower, upper],
        [(value, True) for value in planes]
        + [(psi_t, False), (first, True), (col_row, False), (back, False), (pick, False)],
        [held],
    )
    partial_sum, _ = call(
        functools.partial(gram_kernel, bands),
        [vmem((devices * bands, 1, 128)), vmem((bands, 128))],
        [],
        [(lax.all_to_all(packed, "band", 0, 0, tiled=True), True)],
    )
    own = bands // devices
    (gram,) = call(
        functools.partial(total_kernel, own, 1.0 / (4.0 * radius**3)),
        [jax.ShapeDtypeStruct((2, 1, own), F32)],
        [me_arg],
        [(lax.all_to_all(partial_sum, ("grid", "band"), 0, 0, tiled=True), True)],
    )
    return jnp.transpose(filtered, (0, 2, 1)).reshape(psi.shape), gram


def solution(mesh):
    return jax.shard_map(
        functools.partial(body, mesh.shape["grid"], mesh.shape["band"]),
        mesh=mesh,
        in_specs=(P(None, "band", "grid", None), P("grid"), P("grid", None), P(), P()),
        out_specs=(P(None, "band", "grid", None), P(None, "band", "grid")),
        check_vma=False,
    )
```
